32 devices in a mesh: ens: 2 (over x), tile: 16 (over z, y, core).
Axes of the slice: x: 2, y: 2, z: 4, core: 2. Of those that a mesh axis runs over, the one named last changes fastest.
Arguments:
- thermal_snapshot: float32 [32, 30, 8100], P(('ens', 'tile')), parts along dimension 0, may hold values from -4 to 4
- layer_boundary_stirring_factor: float32 [16, 30, 8100], P('tile'), may hold values from 0.05 to 20
- flooded_layer_number: int32 [16, 8100], P('tile'), may hold values from 0 to 30
- adjacent_patch: int32 [16, 4], P('tile'), may hold values from -1 to 15, as said below
- joint_facing_flag: int32 [16, 4], P('tile'), may hold values from 0 to 7, as said below
- elevation_operator_main_entry: float32 [16, 8100], P('tile'), may hold values from 0.05 to 0.2
- scalar_adjoint_sensitivity: float32 [32, 30, 8100], P(('ens', 'tile')), parts along dimension 0, may hold values from -4 to 4
- elevation_adjoint_sensitivity: float32 [32, 8100], P(('ens', 'tile')), parts along dimension 0, may hold values from -4 to 4
Outputs:
- surface_height: float32 [32, 8100], P(('ens', 'tile')), parts along dimension 0
- temp_gradient: float32 [32, 30, 8100], P(('ens', 'tile')), parts along dimension 0
The draws below stay inside these ranges and needn't reach their ends.
There are 2 independent parts, one for each index of `ens`. The reference program is written for one: setup_inputs(seed, part) draws one part's arguments, and reference() takes and returns one part's arrays. A program takes and returns all parts, laid end to end along the dimension named above; an argument that names none is the same for every part. Nothing has to cross between parts.
Inputs may be any that keep to these rules, and one draw needn't show every extreme that they name: adjacent_patch[t, s] is the tile across side s of tile t, or -1 where land or the window's edge closes it; when not -1 it is one of t - 1, t + 1, t - 8, t + 8, t - 8, t + 8. Seams pair up: if side s of tile t meets side s2 of tile u with joint_facing_flag[t, s] = 2 s2 + f, then adjacent_patch[u, s2] = t and joint_facing_flag[u, s2] = 2 s + f. joint_facing_flag[t, s] = 2 s2 + f: s2 is the side of the neighbour that is met, f = 1 reverses the order along the seam.
All inputs are finite; a program needn't handle non-finite values.
Results may differ from the reference program's by a relative error of at most 0.0003.
Values sent between devices are 32-bit elements; how exact they have to be, the bound alone decides.
No kernel may reach another device: no remote copies, remote signals or barrier semaphores. Data moves between devices by JAX's collectives and lax.ppermute only.
A program may use at most 128 MiB of HBM per device.

```python
import math
import jax
import jax.numpy as jnp
import numpy as np
from jax import lax

DEPTH_LAYERS = 30
ITERS = 4
SEA_PATCH_TOTAL = 16
ROW_TILES = 8
PATCH_POINT_SUM = 8100


def tile_layout():
    row_length = ROW_TILES
    row_total = SEA_PATCH_TOTAL // row_length
    half_row = row_length // 2
    middle_row = row_total // 2
    half_total = SEA_PATCH_TOTAL // 2
    pair_list = []
    for row_index in range(row_total):
        for col_index in range(row_length):
            here_tile = row_index * row_length + col_index
            if col_index + 1 < row_length:
                other_tile = here_tile + 1
                if col_index + 1 < half_row:
                    pair_list.append((here_tile, 3, other_tile, 2, 0))
                elif col_index >= half_row:
                    pair_list.append((here_tile, 1, other_tile, 0, 0))
                else:
                    pair_list.append((here_tile, 3, other_tile, 0, 1))
            if row_index + 1 < row_total:
                other_tile = here_tile + row_length
                if col_index < half_row:
                    if row_index + 1 != middle_row:
                        pair_list.append((here_tile, 1, other_tile, 0, 0))
                else:
                    pair_list.append((here_tile, 2, other_tile, 3, 0))
    for col_index in range(half_row):
        pair_list.append((col_index, 0, col_index + half_total, 0, 1))
        upper_last = (middle_row - 1) * row_length + col_index
        pair_list.append((upper_last, 1, upper_last + half_total, 1, 1))
    base_neighbour = np.full((SEA_PATCH_TOTAL, 4), -1, np.int32)
    base_side = np.zeros((SEA_PATCH_TOTAL, 4), np.int32)
    base_flip = np.zeros((SEA_PATCH_TOTAL, 4), np.int32)
    pair_number = np.zeros((SEA_PATCH_TOTAL, 4), np.int32)
    for number, entry in enumerate(pair_list):
        first_tile, first_side, second_tile, second_side, flipped = entry
        base_neighbour[first_tile, first_side] = second_tile
        base_neighbour[second_tile, second_side] = first_tile
        base_side[first_tile, first_side] = second_side
        base_side[second_tile, second_side] = first_side
        base_flip[first_tile, first_side] = flipped
        base_flip[second_tile, second_side] = flipped
        pair_number[first_tile, first_side] = number
        pair_number[second_tile, second_side] = number
    return (base_neighbour, base_side, base_flip, pair_number, len(pair_list))


def seam_pairing(key):
    base_neighbour, base_side, base_flip, pair_number, pair_total = tile_layout()
    closed = jax.random.randint(jax.random.fold_in(key, 1), (pair_total,), 0, 8) == 0
    flips = jax.random.randint(jax.random.fold_in(key, 2), (pair_total,), 0, 2)
    numbers = jnp.asarray(pair_number)
    closed_sides = jnp.take(closed, numbers, axis=0)
    side_flips = jnp.take(flips, numbers, axis=0)
    adjacent_patch = jnp.where(closed_sides, -1, jnp.asarray(base_neighbour)).astype(jnp.int32)
    joint_facing_flag = (2 * jnp.asarray(base_side) + (jnp.asarray(base_flip) + side_flips) % 2).astype(jnp.int32)
    return (adjacent_patch, joint_facing_flag)


def draw_adjacent_patch(key, part):
    shared = seam_pairing(key)
    return shared[0]


def draw_joint_facing_flag(key, part):
    shared = seam_pairing(key)
    return shared[1]


def tile_offsets(key, shape, reach, noise):
    offset_shape = (shape[0],) + (1,) * (len(shape) - 1)
    offsets = jax.random.uniform(jax.random.fold_in(key, 1), offset_shape, jnp.float32, -reach, reach)
    return jnp.clip(offsets + noise, -4.0, 4.0)


def draw_thermal_snapshot(key, part):
    key = jax.random.fold_in(key, 21)
    shape = (SEA_PATCH_TOTAL, DEPTH_LAYERS, PATCH_POINT_SUM)
    noise = 0.3 * jax.random.normal(jax.random.fold_in(key, 2), shape, jnp.float32)
    return tile_offsets(key, shape, 2.0, noise)


def draw_scalar_adjoint_sensitivity(key, part):
    key = jax.random.fold_in(key, 22)
    shape = (SEA_PATCH_TOTAL, DEPTH_LAYERS, PATCH_POINT_SUM)
    noise = 0.3 * jax.random.normal(jax.random.fold_in(key, 2), shape, jnp.float32)
    return tile_offsets(key, shape, 2.0, noise)


def draw_elevation_adjoint_sensitivity(key, part):
    key = jax.random.fold_in(key, 23)
    shape = (SEA_PATCH_TOTAL, PATCH_POINT_SUM)
    noise = 0.3 * jax.random.normal(jax.random.fold_in(key, 2), shape, jnp.float32)
    return tile_offsets(key, shape, 2.0, noise)


def place_ends(result, stream_key, smallest, high):
    spot = [jax.random.randint(jax.random.fold_in(stream_key, axis), (), 0, length) for axis, length in enumerate(result.shape)]
    main_axis = result.shape.index(max(result.shape))
    neighbour = spot[:main_axis] + [(spot[main_axis] + 1) % result.shape[main_axis]] + spot[main_axis + 1:]
    return result.at[tuple(spot)].set(smallest).at[tuple(neighbour)].set(high)


def steps_of(own_key, shape, cuts, low, high):
    def one(dim, shards_of):
        draws = jax.random.uniform(jax.random.fold_in(jax.random.fold_in(own_key, 6), dim), (shards_of,), jnp.float32, low / len(cuts), high / len(cuts))
        return jnp.repeat(jnp.exp(draws), shape[dim] // shards_of).reshape((-1,) + (1,) * (len(shape) - dim - 1))

    loudness = one(*cuts[0])
    for cut in cuts[1:]:
        loudness = loudness * one(*cut)
    return loudness


def setup_inputs(seed: int = 0, part: int = 0) -> dict:
    key_of = jax.random.split(jax.random.key(seed), 9)
    own_keys = jax.random.split(jax.random.fold_in(key_of[8], part), 9)
    thermal_snapshot = draw_thermal_snapshot(jax.random.fold_in(jax.random.fold_in(key_of[8], part), 71), part)
    layer_boundary_stirring_factor = jnp.clip(jnp.exp(math.log(20.0) - 5.9914645 * jax.random.uniform(key_of[1], (SEA_PATCH_TOTAL, DEPTH_LAYERS, PATCH_POINT_SUM), jnp.float32) ** steps_of(key_of[1], (SEA_PATCH_TOTAL, DEPTH_LAYERS, PATCH_POINT_SUM), ((0, 16),), -0.2, 0.2)), 0.05, 20.0)
    flooded_layer_number = place_ends(jax.random.randint(key_of[2], (SEA_PATCH_TOTAL, PATCH_POINT_SUM), 0, DEPTH_LAYERS + 1), jax.random.fold_in(key_of[2], 1), 0, DEPTH_LAYERS).astype(jnp.int32)
    adjacent_patch = draw_adjacent_patch(jax.random.fold_in(key_of[8], 71), part)
    joint_facing_flag = draw_joint_facing_flag(jax.random.fold_in(key_of[8], 71), part)
    elevation_operator_main_entry = jnp.clip(jnp.exp(math.log(0.2) - 1.3862944 * jax.random.uniform(key_of[5], (SEA_PATCH_TOTAL, PATCH_POINT_SUM), jnp.float32) ** steps_of(key_of[5], (SEA_PATCH_TOTAL, PATCH_POINT_SUM), ((0, 16),), -0.2, 0.2)), 0.05, 0.2)
    scalar_adjoint_sensitivity = draw_scalar_adjoint_sensitivity(jax.random.fold_in(jax.random.fold_in(key_of[8], part), 71), part)
    elevation_adjoint_sensitivity = draw_elevation_adjoint_sensitivity(jax.random.fold_in(jax.random.fold_in(key_of[8], part), 71), part)
    return {"thermal_snapshot": thermal_snapshot, "layer_boundary_stirring_factor": layer_boundary_stirring_factor, "flooded_layer_number": flooded_layer_number, "adjacent_patch": adjacent_patch, "joint_facing_flag": joint_facing_flag, "elevation_operator_main_entry": elevation_operator_main_entry, "scalar_adjoint_sensitivity": scalar_adjoint_sensitivity, "elevation_adjoint_sensitivity": elevation_adjoint_sensitivity}


scalar_spreading_increment = 0.2

def edge_strips(field):
    cells = field.shape[-1]
    tile_size = math.isqrt(cells)
    return jnp.stack([field[..., :tile_size], field[..., cells - tile_size:], field[..., ::tile_size], field[..., tile_size - 1::tile_size]], axis=1)

def pick_range(all_strips, adjacent_patch, joint_facing_flag, first_row):
    row_count = all_strips.shape[0]
    present = (adjacent_patch >= first_row) & (adjacent_patch < first_row + row_count)
    source_rows = jnp.clip(adjacent_patch - first_row, 0, row_count - 1).astype(jnp.int32)
    flat_strips = all_strips.reshape((row_count * 4,) + all_strips.shape[2:])
    flat_index = (source_rows * 4 + joint_facing_flag // 2).reshape(-1).astype(jnp.int32)
    fetched = jnp.take(flat_strips, flat_index, axis=0).reshape(adjacent_patch.shape + all_strips.shape[2:])
    reverse_mask = (joint_facing_flag % 2 == 1)[:, :, None, None]
    fetched = jnp.where(reverse_mask, fetched[..., ::-1], fetched)
    return jnp.where(present[:, :, None, None], fetched, jnp.zeros_like(fetched))

def place_side(edge_strip, side_index, tile_size, cells):
    leading = [(0, 0)] * (edge_strip.ndim - 1)
    if side_index == 0:
        return jnp.pad(edge_strip, leading + [(0, cells - tile_size)])
    if side_index == 1:
        return jnp.pad(edge_strip, leading + [(cells - tile_size, 0)])
    before = 0 if side_index == 2 else tile_size - 1
    padded = jnp.pad(edge_strip[..., None], leading + [(0, 0), (before, tile_size - 1 - before)])
    return padded.reshape(edge_strip.shape[:-1] + (cells,))

def spread_scalar_field(field, flooded_point_flags, ghost_cells, halo_flooded_flags):
    cells = field.shape[-1]
    tile_size = ghost_cells.shape[-1]
    leading = [(0, 0)] * (field.ndim - 1)
    column_keep = (jnp.arange(cells - 1) % tile_size != tile_size - 1).astype(jnp.float32)
    flux_along = flooded_point_flags[..., 1:] * flooded_point_flags[..., :-1] * column_keep * (field[..., 1:] - field[..., :-1])
    flux_across = flooded_point_flags[..., tile_size:] * flooded_point_flags[..., :-tile_size] * (field[..., tile_size:] - field[..., :-tile_size])
    tendency = jnp.pad(flux_along, leading + [(0, 1)]) - jnp.pad(flux_along, leading + [(1, 0)])
    tendency = tendency + jnp.pad(flux_across, leading + [(0, tile_size)]) - jnp.pad(flux_across, leading + [(tile_size, 0)])
    seam_flux = edge_strips(flooded_point_flags) * halo_flooded_flags * (ghost_cells - edge_strips(field))
    for side_index in range(4):
        tendency = tendency + place_side(seam_flux[:, side_index], side_index, tile_size, cells)
    return tendency

def column_solve(source, layer_boundary_stirring_factor, flooded_point_flags):
    below_wet = jnp.concatenate([flooded_point_flags[:, 1:], jnp.zeros_like(flooded_point_flags[:, :1])], axis=1)
    coupling = layer_boundary_stirring_factor * flooded_point_flags * below_wet
    upper_link = jnp.concatenate([jnp.zeros_like(coupling[:, :1]), coupling[:, :-1]], axis=1)
    diagonal = 1.0 + upper_link + coupling

    def forward_sweep(carry, inputs):
        ratio_prev, value_prev = carry
        link_above, center, link_below, rhs_level = inputs
        denominator = center + link_above * ratio_prev
        ratio_next = -link_below / denominator
        value_next = (rhs_level + link_above * value_prev) / denominator
        return ((ratio_next, value_next), (ratio_next, value_next))

    def back_sweep(later, inputs):
        ratio_here, value_here = inputs
        current = value_here - ratio_here * later
        return (current, current)
    starting = jnp.zeros((source.shape[0], source.shape[2]), jnp.float32)
    sweep_inputs = (jnp.moveaxis(upper_link, 1, 0), jnp.moveaxis(diagonal, 1, 0), jnp.moveaxis(coupling, 1, 0), jnp.moveaxis(source, 1, 0))
    carried, (ratios, values) = lax.scan(forward_sweep, (starting, starting), sweep_inputs)
    carried, solved = lax.scan(back_sweep, starting, (ratios, values), reverse=True)
    return jnp.moveaxis(solved, 0, 1)

def surface_solve(rhs, apply_operator):
    solution = jnp.zeros_like(rhs)
    residual, direction = (rhs, rhs)
    norm_now = jnp.sum(residual * residual)
    for iteration in range(ITERS):
        product_field = apply_operator(direction)
        step_length = norm_now / jnp.sum(direction * product_field)
        solution = solution + step_length * direction
        residual = residual - step_length * product_field
        norm_next = jnp.sum(residual * residual)
        direction = residual + norm_next / norm_now * direction
        norm_now = norm_next
    return solution

def reference(thermal_snapshot, layer_boundary_stirring_factor, flooded_layer_number, adjacent_patch, joint_facing_flag, elevation_operator_main_entry, scalar_adjoint_sensitivity, elevation_adjoint_sensitivity):
    flooded_layer_total = thermal_snapshot.shape[1]
    flooded_point_flags = (jnp.arange(flooded_layer_total)[None, :, None] < flooded_layer_number[:, None, :]).astype(jnp.float32)
    ghost_depth = pick_range(edge_strips(flooded_layer_number[:, None, :]), adjacent_patch, joint_facing_flag, 0)
    halo_flooded_flags = (jnp.arange(flooded_layer_total)[None, None, :, None] < ghost_depth).astype(jnp.float32)
    surface_wet = flooded_point_flags[:, :1]
    surface_ghost_wet = halo_flooded_flags[:, :, :1]

    def find_halo_points(field):
        return pick_range(edge_strips(field), adjacent_patch, joint_facing_flag, 0)

    def apply_operator(field):
        return elevation_operator_main_entry[:, None, :] * field - spread_scalar_field(field, surface_wet, find_halo_points(field), surface_ghost_wet)
    level_scale = 1.0 / math.sqrt(flooded_layer_total)
    stirred_sea_elevation = thermal_snapshot + scalar_spreading_increment * spread_scalar_field(thermal_snapshot, flooded_point_flags, find_halo_points(thermal_snapshot), halo_flooded_flags)
    mixed = column_solve(stirred_sea_elevation, layer_boundary_stirring_factor, flooded_point_flags)
    forcing = lax.optimization_barrier(jnp.sum(flooded_point_flags * mixed, axis=1, keepdims=True)) * level_scale
    surface_height = surface_solve(forcing, apply_operator)
    forcing_adjoint = surface_solve(elevation_adjoint_sensitivity[:, None, :], apply_operator)
    mixed_adjoint = scalar_adjoint_sensitivity + flooded_point_flags * forcing_adjoint * level_scale
    mixed_h_adjoint = column_solve(mixed_adjoint, layer_boundary_stirring_factor, flooded_point_flags)
    temp_gradient = mixed_h_adjoint + scalar_spreading_increment * spread_scalar_field(mixed_h_adjoint, flooded_point_flags, find_halo_points(mixed_h_adjoint), halo_flooded_flags)
    return (surface_height[:, 0], temp_gradient)
```

```python
import functools
import math

import jax
import jax.numpy as jnp
from jax import lax
from jax.experimental import pallas as pl
from jax.experimental.pallas import tpu as pltpu
from jax.sharding import PartitionSpec as P

SIDE = 90
CELLS = SIDE * SIDE
ROWS = 64
LANES = 128
ITERS = 4
ROW_TILES = 8
SPREAD = 0.2
CENTRE = 4.1
BLOCK = 72
F32 = jnp.float32
I32 = jnp.int32


def grid_iotas():
    row = lax.broadcasted_iota(I32, (ROWS, LANES), 0)
    lane = lax.broadcasted_iota(I32, (ROWS, LANES), 1)
    cell = row * LANES + lane
    i = (cell * 46604) >> 22
    j = cell - SIDE * i
    return row, lane, cell, i, j


def ahead(x, n):
    lane = lax.broadcasted_iota(I32, x.shape, 1)
    y = pltpu.roll(x, LANES - n, 1)
    return jnp.where(lane < LANES - n, y, pltpu.roll(y, ROWS - 1, 0))


def behind(x, n):
    lane = lax.broadcasted_iota(I32, x.shape, 1)
    y = pltpu.roll(x, n, 1)
    return jnp.where(lane >= n, y, pltpu.roll(y, 1, 0))


def take(x, index):
    pieces = []
    for first in range(0, x.shape[0], 8):
        part = index if index.shape[0] == 8 else index[first : first + 8]
        pieces.append(jnp.take_along_axis(x[first : first + 8], part, axis=1, mode="promise_in_bounds"))
    return pieces[0] if len(pieces) == 1 else jnp.concatenate(pieces, axis=0)


def lanes8():
    return lax.broadcasted_iota(I32, (8, LANES), 1)


def column_owner(lane):
    odd = lane & 1
    half = (lane - 89 * odd) >> 1
    return (37 * half) & 63


def lines_23(za, zb, depth_row):
    lane = lanes8()
    near = (SIDE * lane + depth_row) & 127
    far = (SIDE * lane + SIDE - 1 - depth_row) & 127
    wide = lax.broadcasted_iota(I32, za.shape, 1)
    first = wide < 64
    return (
        jnp.where(first, take(za, near), take(zb, near)),
        jnp.where(first, take(za, far), take(zb, far)),
    )


def spread_lines(side2, side3, side1):
    lane = lanes8()
    owner = column_owner(lane)
    later = (owner + 64) & 127
    even = (lax.broadcasted_iota(I32, side2.shape, 1) & 1) == 0
    wa = jnp.where(even, take(side2, owner), take(side3, owner))
    wb = jnp.where(even, take(side2, later), take(side3, later))
    return wa, wb, pltpu.roll(side1, 74, 1)


def scatter_masks():
    row, lane, cell, i, j = grid_iotas()
    column = (j == 0) | (j == SIDE - 1)
    return (
        column & (i < 64),
        column & (i >= 64) & (i < SIDE),
        cell < SIDE,
        i == SIDE - 1,
    )


def scatter_rows(masks, wa, wb, side0, w1):
    zero = jnp.zeros((ROWS, LANES), F32)
    out = jnp.where(masks[0], wa, zero) + jnp.where(masks[1], wb, zero)
    return out + jnp.where(masks[2], side0, zero) + jnp.where(masks[3], w1, zero)


def scatter_lines(masks, lines):
    wa, wb, w1 = spread_lines(
        jnp.broadcast_to(lines[2:3], (8, LANES)),
        jnp.broadcast_to(lines[3:4], (8, LANES)),
        jnp.broadcast_to(lines[1:2], (8, LANES)),
    )
    return scatter_rows(masks, wa[0:1], wb[0:1], lines[0:1], w1[0:1])


def row_line(ref, base, first_cell):
    row, off = divmod(first_cell, LANES)
    top = ref[pl.ds(base + row, 1), :]
    if off == 0:
        return top
    lane = lax.broadcasted_iota(I32, (1, LANES), 1)
    top = pltpu.roll(top, LANES - off, 1)
    if off + SIDE <= LANES:
        return top
    low = pltpu.roll(ref[pl.ds(base + row + 1, 1), :], LANES - off, 1)
    return jnp.where(lane < LANES - off, top, low)


def write_frames(field_ref, base, out_ref, first_row, za_ref, zb_ref):
    field = field_ref[base : base + ROWS, :]
    row, lane, cell, i, j = grid_iotas()
    zero = jnp.zeros_like(field)
    for depth in range(4):
        column = (j == depth) | (j == SIDE - 1 - depth)
        za = jnp.where(column & (i < 64), field, zero)
        zb = jnp.where(column & (i >= 64), field, zero)
        za_ref[depth : depth + 1, :] = jnp.sum(za, axis=0, keepdims=True)
        zb_ref[depth : depth + 1, :] = jnp.sum(zb, axis=0, keepdims=True)
        out_ref[first_row + depth * 4 : first_row + depth * 4 + 1, :] = row_line(
            field_ref, base, depth * SIDE
        )
        out_ref[first_row + depth * 4 + 1 : first_row + depth * 4 + 2, :] = row_line(
            field_ref, base, (SIDE - 1 - depth) * SIDE
        )
    for depth in range(4, 8):
        za_ref[depth : depth + 1, :] = jnp.zeros((1, LANES), F32)
        zb_ref[depth : depth + 1, :] = jnp.zeros((1, LANES), F32)
    depth_row = lax.broadcasted_iota(I32, (8, LANES), 0) & 3
    side2, side3 = lines_23(za_ref[0:8, :], zb_ref[0:8, :], depth_row)
    for depth in range(4):
        at = first_row + depth * 4
        out_ref[at + 2 : at + 3, :] = side2[depth : depth + 1]
        out_ref[at + 3 : at + 4, :] = side3[depth : depth + 1]


def tail_row(ref, rows):
    window = ref[rows, CELLS - LANES : CELLS]
    return pltpu.roll(window, CELLS - (ROWS - 1) * LANES, 1)


def edges_kernel(adj_ref, flag_ref, t_ref, depth_ref, d_ref, b_ref, ts_ref, blk_ref, dense_ref, z_ref):
    row, lane, cell, i, j = grid_iotas()
    inside = cell < CELLS
    for number, ref in enumerate((b_ref, d_ref, depth_ref)):
        base = number * ROWS
        for l in range(ROWS - 1):
            dense_ref[base + l : base + l + 1, :] = ref[:, l * LANES : (l + 1) * LANES].astype(F32)
        dense_ref[base + ROWS - 1 : base + ROWS, :] = tail_row(ref, slice(0, 1)).astype(F32)
        dense_ref[base : base + ROWS, :] = jnp.where(inside, dense_ref[base : base + ROWS, :], 0.0)
        write_frames(dense_ref, base, blk_ref, number * 16, z_ref.at[0], z_ref.at[1])
    at = 48
    for sides in ((0, 1, 2, 3), (2, 2, 0, 0), (3, 3, 1, 1)):
        for ref in (adj_ref, flag_ref):
            for side in sides:
                blk_ref[at : at + 1, :] = jnp.full((1, LANES), ref[0, side], I32).astype(F32)
                at += 1
    levels = t_ref.shape[1]
    for first in range(0, levels, 8):
        size = min(8, levels - first)
        lane8 = lax.broadcasted_iota(I32, (size, LANES), 1)
        odd = lane8 & 1
        owner = column_owner(lane8)
        la = (SIDE * owner + 89 * odd) >> 7
        lb = jnp.where(owner + 64 < SIDE, (SIDE * (owner + 64) + 89 * odd) >> 7, -1)
        za = jnp.zeros((size, LANES), F32)
        zb = za
        for l in range(ROWS):
            if l < ROWS - 1:
                x = t_ref[0, first : first + size, l * LANES : (l + 1) * LANES]
            else:
                x = pltpu.roll(
                    t_ref[0, first : first + size, CELLS - LANES : CELLS], CELLS - (ROWS - 1) * LANES, 1
                )
            if l <= (SIDE * 63 + 89) // LANES:
                za = jnp.where(la == l, x, za)
            if l >= (SIDE * 64) // LANES:
                zb = jnp.where(lb == l, x, zb)
        z_ref[0, first : first + size, :] = za
        z_ref[1, first : first + size, :] = zb
        ts_ref[0, first : first + size, :] = t_ref[0, first : first + size, 0:LANES]
        window = t_ref[0, first : first + size, CELLS - LANES : CELLS]
        ts_ref[1, first : first + size, :] = pltpu.roll(window, SIDE, 1)
    side2, side3 = lines_23(z_ref[0], z_ref[1], 0)
    ts_ref[2] = side2
    ts_ref[3] = side3
    for side in range(4):
        ts_ref[side, levels : levels + 1, :] = blk_ref[32 + side : 33 + side, :]
        ts_ref[side, levels + 1 : levels + 2, :] = jnp.zeros((1, LANES), F32)


def to_dense(src_ref, dst_ref, levels):
    for first in range(0, levels, 8):
        size = min(8, levels - first)
        for l in range(ROWS):
            if l < ROWS - 1:
                x = src_ref[0, first : first + size, l * LANES : (l + 1) * LANES]
            else:
                x = pltpu.roll(
                    src_ref[0, first : first + size, CELLS - LANES : CELLS], CELLS - (ROWS - 1) * LANES, 1
                )
            dst_ref[pl.ds(first * ROWS + l, size, stride=ROWS), :] = x


def interior_reach(depth):
    row, lane, cell, i, j = grid_iotas()
    zero = jnp.zeros_like(depth)
    along = jnp.where(j < SIDE - 1, jnp.minimum(depth, ahead(depth, 1)), zero)
    across = jnp.where(cell < CELLS - SIDE, jnp.minimum(depth, ahead(depth, SIDE)), zero)
    return along, across


def interior_spread(x, along, across, level):
    zero = jnp.zeros_like(x)
    flux1 = jnp.where(along > level, ahead(x, 1) - x, zero)
    flux2 = jnp.where(across > level, ahead(x, SIDE) - x, zero)
    return (flux1 - behind(flux1, 1)) + (flux2 - behind(flux2, SIDE))


def columns_kernel(levels, k_ref, s_ref, t_ref, dense_ref, a_ref, q_ref, f_ref, aq_ref, g_ref, v_ref, td_ref, z_ref):
    to_dense(k_ref, g_ref, levels)
    to_dense(s_ref, v_ref, levels)
    to_dense(t_ref, td_ref, levels)
    depth = dense_ref[2 * ROWS : 3 * ROWS, :]
    along, across = interior_reach(depth)
    zero = jnp.zeros((ROWS, LANES), F32)

    def down(level, carry):
        link, below, va, vq = carry
        at = pl.ds(pl.multiple_of(level * ROWS, ROWS), ROWS)
        here = level.astype(F32)
        r = jnp.where(depth > here + 1.0, g_ref[at, :], zero)
        wet = jnp.where(depth > here, 1.0, zero)
        upper = 1.0 + below
        inverse = 1.0 / (upper + r)
        ratio = r * inverse
        va = (v_ref[at, :] + link * va) * inverse
        vq = (wet + link * vq) * inverse
        g_ref[at, :] = ratio
        v_ref[at, :] = va
        q_ref[at, :] = vq
        return r, upper * ratio, va, vq

    lax.fori_loop(0, levels, down, (zero, zero, zero, zero))
    row, lane, cell, i, j = grid_iotas()
    column = (j == 0) | (j == SIDE - 1)
    first = column & (i < 64)
    second = column & (i >= 64) & (i < SIDE)

    def up(step, carry):
        xa, xq, total = carry
        level = levels - 1 - step
        at = pl.ds(pl.multiple_of(level * ROWS, ROWS), ROWS)
        ratio = g_ref[at, :]
        xa = v_ref[at, :] + ratio * xa
        xq = q_ref[at, :] + ratio * xq
        a_ref[at, :] = xa
        q_ref[at, :] = xq
        here = pl.ds(level, 1)
        for number, x in enumerate((xa, xq)):
            z_ref[number * 4, here, :] = jnp.sum(jnp.where(first, x, zero), axis=0, keepdims=True)
            z_ref[number * 4 + 1, here, :] = jnp.sum(jnp.where(second, x, zero), axis=0, keepdims=True)
            aq_ref[number * 4, here, :] = x[0:1]
            z_ref[number * 4 + 2, here, :] = x[ROWS - 2 : ROWS - 1]
            z_ref[number * 4 + 3, here, :] = x[ROWS - 1 : ROWS]
        t = td_ref[at, :]
        mixed_h = t + SPREAD * interior_spread(t, along, across, level.astype(F32))
        return xa, xq, total + xq * mixed_h

    xa, xq, total = lax.fori_loop(0, levels, up, (zero, zero, zero))
    f_ref[...] = jnp.where(cell < CELLS, total, zero)
    spare = z_ref.shape[1] - levels
    for number in range(2):
        for part in range(4):
            z_ref[number * 4 + part, levels:, :] = jnp.zeros((spare, LANES), F32)
        aq_ref[number * 4, levels:, :] = jnp.zeros((spare, LANES), F32)
        side2, side3 = lines_23(z_ref[number * 4], z_ref[number * 4 + 1], 0)
        aq_ref[number * 4 + 2] = side2
        aq_ref[number * 4 + 3] = side3
        low, high = z_ref[number * 4 + 2], z_ref[number * 4 + 3]
        wide = lax.broadcasted_iota(I32, low.shape, 1)
        aq_ref[number * 4 + 1] = jnp.where(wide < 54, pltpu.roll(low, 54, 1), pltpu.roll(high, 54, 1))


def pick(refs, shifts, tiles, me, neighbour, first, side_met):
    value = refs[0][first + side_met]
    for number in range(1, len(shifts)):
        hit = neighbour == lax.rem(me + tiles - shifts[number], tiles)
        value = jnp.where(hit, refs[number][first + side_met], value)
    return value


def seam_index(flag):
    lane = lanes8()
    return jnp.where((flag & 1) == 1, SIDE - 1 - lane, lane) & 127


def forcing_kernel(shifts, tiles, levels, me_ref, adj_ref, flag_ref, f_ref, ts_ref, aq_ref, *rest):
    refs = rest[: len(shifts)]
    out_ref, frame_ref, reach_ref, za_ref, zb_ref = rest[len(shifts) :]
    me = me_ref[0]
    level = lax.broadcasted_iota(I32, (32, LANES), 0).astype(F32)
    lines = []
    for side in range(4):
        neighbour = adj_ref[0, side]
        flag = flag_ref[0, side]
        other = take(pick(refs, shifts, tiles, me, neighbour, 0, flag >> 1), seam_index(flag))
        own = ts_ref[side]
        reach = jnp.minimum(other[levels : levels + 1], own[levels : levels + 1])
        reach = jnp.where(neighbour >= 0, reach, 0.0)
        reach_ref[side : side + 1, :] = reach
        flux = jnp.where(reach > level, other - own, 0.0)
        lines.append(jnp.sum(aq_ref[4 + side] * flux, axis=0, keepdims=True))
    reach_ref[4:8, :] = jnp.zeros((4, LANES), F32)
    seams = scatter_lines(scatter_masks(), jnp.concatenate(lines + lines, axis=0))
    out_ref[...] = (f_ref[...] + SPREAD * seams) * (1.0 / math.sqrt(levels))
    write_frames(out_ref, 0, frame_ref, 0, za_ref, zb_ref)


def block_rows(refs, counts, block, first, size):
    position = 0
    for ref, count in zip(refs, counts):
        for number in range(count):
            at = number * block + first
            yield position, ref[at : at + size, :]
            position += 1


def gather_lines(p, lines):
    high = lines.astype(jnp.bfloat16)
    rest = lines - high.astype(F32)
    middle = rest.astype(jnp.bfloat16)
    low = (rest - middle.astype(F32)).astype(jnp.bfloat16)
    out = jnp.dot(p, high, preferred_element_type=F32)
    out = out + jnp.dot(p, middle, preferred_element_type=F32)
    return out + jnp.dot(p, low, preferred_element_type=F32)


def ends(x, low, high, low_parity, high_parity, depth):
    lane = lax.broadcasted_iota(I32, x.shape, 1)
    low_end = take(low, jnp.where(low_parity == 1, SIDE - 1 - depth, depth))
    high_end = take(high, jnp.where(high_parity == 1, SIDE - 1 - depth, depth))
    return (
        jnp.where(lane == 0, low_end, pltpu.roll(x, 1, 1)),
        jnp.where(lane == SIDE - 1, high_end, pltpu.roll(x, LANES - 1, 1)),
    )


def prepare_kernel(counts, lines, me_ref, dense_ref, *rest):
    refs = rest[: len(counts)]
    p_ref, index_ref, frame_ref, own_ref, seam_ref, work_ref, depth_ref, d_ref = rest[len(counts) :]
    me = me_ref[0]
    for number in range(6):
        for position, rows in block_rows(refs, counts, BLOCK, 48 + 4 * number, 4):
            work_ref[number, position * 4 : position * 4 + 4, :] = rows
    for depth in range(4):
        for position, rows in block_rows(refs, counts, BLOCK, 16 + 4 * depth, 4):
            d_ref[depth, position * 4 : position * 4 + 4, :] = rows
        for position, rows in block_rows(refs, counts, BLOCK, 32 + 4 * depth, 4):
            depth_ref[depth, position * 4 : position * 4 + 4, :] = rows
    lane = lax.broadcasted_iota(I32, (lines, LANES), 1)
    odd = lax.broadcasted_iota(I32, (lines, LANES), 0) & 1
    column = lax.broadcasted_iota(I32, (lines, lines), 1)
    for number in range(3):
        tile = work_ref[2 * number, :, 0:1].astype(I32)
        flag = work_ref[2 * number + 1, :, 0:1].astype(I32)
        at = jnp.where(tile >= 0, 4 * (tile ^ me) + (flag >> 1), -1)
        p = jnp.where(jnp.broadcast_to(at, (lines, lines)) == column, 1.0, 0.0)
        p_ref[number * lines : (number + 1) * lines, :] = p.astype(jnp.bfloat16)
        parity = work_ref[2 * number + 1].astype(I32) & 1
        if number == 0:
            index_ref[0:lines, :] = jnp.where(parity == 1, SIDE - 1 - lane, lane) & 127
        else:
            index_ref[number * lines : (number + 1) * lines, :] = parity ^ odd
    wet = [jnp.where(depth_ref[depth] > 0.0, 1.0, 0.0) for depth in range(4)]
    met = gather_lines(p_ref[...], wet[0])
    facing = take(met[0:lines], index_ref[0:lines, :])
    for depth in range(3):
        low, high = ends(
            wet[depth],
            met[lines : 2 * lines],
            met[2 * lines : 3 * lines],
            index_ref[lines : 2 * lines, :],
            index_ref[2 * lines : 3 * lines, :],
            depth,
        )
        masks = [
            wet[depth] * (facing if depth == 0 else wet[depth - 1]),
            wet[depth] * wet[depth + 1],
            wet[depth] * low,
            wet[depth] * high,
        ]
        frame_ref[depth, 0] = d_ref[depth] + ((masks[0] + masks[1]) + (masks[2] + masks[3]))
        for number in range(4):
            frame_ref[depth, 1 + number] = masks[number]
        if depth == 0:
            seam_ref[...] = masks[0][0:8]
    surface = jnp.minimum(dense_ref[2 * ROWS : 3 * ROWS, :], 1.0)
    along, across = interior_reach(surface)
    degree = (along + behind(along, 1)) + (across + behind(across, SIDE))
    degree = degree + scatter_lines(scatter_masks(), seam_ref[...])
    own_ref[0] = dense_ref[ROWS : 2 * ROWS, :] + degree
    own_ref[1] = along
    own_ref[2] = across


def krylov_kernel(
    counts, block, lines, b_ref, p_ref, index_ref, frame_ref, own_ref, seam_ref, *rest
):
    refs = rest[: len(counts)]
    v_ref, line_ref, gram_ref, x_ref = rest[len(counts) :]
    for depth in range(4):
        for position, rows in block_rows(refs, counts, block, 4 * depth, 4):
            x_ref[depth, position * 4 : position * 4 + 4, :] = rows
    p = p_ref[...]
    facing_at = index_ref[0:lines, :]
    low_parity = index_ref[lines : 2 * lines, :]
    high_parity = index_ref[2 * lines : 3 * lines, :]
    scale = 2.0 / CENTRE
    masks = scatter_masks()
    row, lane, cell, i, j = grid_iotas()
    inside = cell < CELLS
    diagonal, along, across = own_ref[0], own_ref[1], own_ref[2]
    seam = seam_ref[...]
    frames = [[x_ref[depth] for depth in range(4)]]
    own = [b_ref[0:ROWS, :]]
    for step in range(ITERS):
        x = frames[-1]
        met = gather_lines(p, x[0])
        facing = take(met[0:lines], facing_at)
        line_ref[step] = facing[0:8]
        mine = own[-1]
        flow = (along * ahead(mine, 1) + behind(along * mine, 1)) + (
            across * ahead(mine, SIDE) + behind(across * mine, SIDE)
        )
        image = diagonal * mine - flow - scatter_lines(masks, seam * facing[0:8])
        image = jnp.where(inside, scale * image - 2.0 * mine, 0.0)
        own.append(0.5 * image if step == 0 else image - own[-2])
        following = []
        for depth in range(ITERS - 1 - step):
            low, high = ends(
                x[depth],
                met[lines : 2 * lines],
                met[2 * lines : 3 * lines],
                low_parity,
                high_parity,
                depth,
            )
            before = facing if depth == 0 else x[depth - 1]
            flow = (frame_ref[depth, 1] * before + frame_ref[depth, 2] * x[depth + 1]) + (
                frame_ref[depth, 3] * low + frame_ref[depth, 4] * high
            )
            image = scale * (frame_ref[depth, 0] * x[depth] - flow) - 2.0 * x[depth]
            following.append(0.5 * image if step == 0 else image - frames[-2][depth])
        frames.append(following)
        if step < ITERS - 1:
            v_ref[step] = own[-1]
    at = 0
    for first in range(ITERS + 1):
        for second in range(first + 1):
            gram_ref[at : at + 1, :] = jnp.sum(own[first] * own[second], axis=0, keepdims=True)
            at += 1
    gram_ref[15:16, :] = jnp.zeros((1, LANES), F32)


def image_of(p):
    out = [None] * (len(p) + 1)

    def add(at, value):
        out[at] = value if out[at] is None else out[at] + value

    for at, value in enumerate(p):
        add(at, CENTRE * value)
        if at == 0:
            add(1, CENTRE * value)
        else:
            add(at + 1, 0.5 * CENTRE * value)
            add(at - 1, 0.5 * CENTRE * value)
    return out


def form(left, gram, right):
    total = None
    for first, x in enumerate(left):
        inner = None
        for second, y in enumerate(right):
            term = gram[max(first, second)][min(first, second)] * y
            inner = term if inner is None else inner + term
        total = x * inner if total is None else total + x * inner
    return total


def coefficients(refs, sum_ref):
    total = refs[0][...]
    for ref in refs[1:]:
        total = total + ref[...]
    sum_ref[...] = jnp.broadcast_to(jnp.sum(total, axis=1, keepdims=True), (16, LANES))
    gram = []
    at = 0
    for first in range(ITERS + 1):
        gram.append([sum_ref[at + second : at + second + 1, :] for second in range(first + 1)])
        at += first + 1
    one = jnp.ones((1, LANES), F32)
    x = []
    r = [one]
    p = [one]
    rr = gram[0][0]
    for step in range(ITERS):
        image = image_of(p)
        curve = form(p, gram, image)
        alpha = jnp.where(curve > 0.0, rr / curve, 0.0)
        x = [x[n] + alpha * p[n] if n < len(x) else alpha * p[n] for n in range(len(p))]
        r = [r[n] - alpha * image[n] if n < len(r) else -alpha * image[n] for n in range(len(image))]
        if step < ITERS - 1:
            new = jnp.maximum(form(r, gram, r), 0.0)
            beta = jnp.where(rr > 0.0, new / rr, 0.0)
            p = [r[n] + beta * p[n] if n < len(p) else r[n] for n in range(len(r))]
            rr = new
    return x


def combine(x, b_ref, v_ref):
    out = x[0] * b_ref[0:ROWS, :]
    for number in range(1, ITERS):
        out = out + x[number] * v_ref[number - 1]
    return out


def gradient_kernel(shifts, tiles, levels, grams, me_ref, adj_ref, flag_ref, *rest):
    gram_refs = rest[:grams]
    rest = rest[grams:]
    dense_ref, v_ref, line_ref, blk_ref, reach_ref, a_ref, q_ref, aq_ref = rest[:8]
    refs = rest[8 : 8 + len(shifts)]
    out_ref, sum_ref, w_ref, h_ref = rest[8 + len(shifts) :]
    me = me_ref[0]
    x = coefficients(gram_refs, sum_ref)
    level_scale = 1.0 / math.sqrt(levels)
    adjoint = combine(x, dense_ref, v_ref) * level_scale
    own_line = x[0] * blk_ref[0:8, :]
    met_line = x[0] * line_ref[0]
    w_ref[4, 0:ROWS // 2, :] = jnp.zeros((ROWS // 2, LANES), F32)
    own_sides = []
    depth = dense_ref[2 * ROWS : 3 * ROWS, :]
    along, across = interior_reach(depth)
    sum_ref[0:8, :] = met_line + x[1] * line_ref[1] + x[2] * line_ref[2] + x[3] * line_ref[3]
    h_ref[0:ROWS, :] = adjoint
    w_ref[4, 8:9, :] = h_ref[0:1, :]
    w_ref[4, 9:10, :] = row_line(h_ref, 0, (SIDE - 1) * SIDE)
    row, lane, cell, i, j = grid_iotas()
    column = (j == 0) | (j == SIDE - 1)
    zero = jnp.zeros((ROWS, LANES), F32)
    za = jnp.sum(jnp.where(column & (i < 64), adjoint, zero), axis=0, keepdims=True)
    zb = jnp.sum(jnp.where(column & (i >= 64), adjoint, zero), axis=0, keepdims=True)
    side2, side3 = lines_23(jnp.broadcast_to(za, (8, LANES)), jnp.broadcast_to(zb, (8, LANES)), 0)
    w_ref[4, 10:11, :] = side2[0:1]
    w_ref[4, 11:12, :] = side3[0:1]
    level = lax.broadcasted_iota(I32, (32, LANES), 0).astype(F32)
    fluxes = []
    for side in range(4):
        neighbour = adj_ref[0, side]
        flag = flag_ref[0, side]
        index = seam_index(flag)
        a_other = take(pick(refs, shifts, tiles, me, neighbour, 0, flag >> 1), index)
        q_other = take(pick(refs, shifts, tiles, me, neighbour, 4, flag >> 1), index)
        other = a_other + (sum_ref[side : side + 1, :] * level_scale) * q_other
        own = aq_ref[side] + w_ref[4, 8 + side : 9 + side, :] * aq_ref[4 + side]
        fluxes.append(jnp.where(reach_ref[side : side + 1, :] > level, other - own, 0.0))
    wa, wb, w1 = spread_lines(fluxes[2], fluxes[3], fluxes[1])
    w_ref[0] = wa
    w_ref[1] = wb
    w_ref[2] = fluxes[0]
    w_ref[3] = w1
    masks = scatter_masks()

    def per_level(number, carry):
        at = pl.ds(pl.multiple_of(number * ROWS, ROWS), ROWS)
        here = pl.ds(number, 1)
        h = a_ref[at, :] + adjoint * q_ref[at, :]
        spread = interior_spread(h, along, across, number.astype(F32))
        spread = spread + scatter_rows(
            masks, w_ref[0, here, :], w_ref[1, here, :], w_ref[2, here, :], w_ref[3, here, :]
        )
        h_ref[at, :] = h + SPREAD * spread
        return carry

    lax.fori_loop(0, levels, per_level, 0)
    for first in range(0, levels, 8):
        size = min(8, levels - first)
        for l in range(ROWS):
            width = min(LANES, CELLS - l * LANES)
            x_tile = h_ref[pl.ds(first * ROWS + l, size, stride=ROWS), :]
            out_ref[0, first : first + size, l * LANES : l * LANES + width] = x_tile[:, 0:width]


def height_kernel(grams, *rest):
    gram_refs = rest[:grams]
    b_ref, v_ref, out_ref, sum_ref, x_ref = rest[grams:]
    x_ref[...] = combine(coefficients(gram_refs, sum_ref), b_ref, v_ref)
    for l in range(ROWS):
        width = min(LANES, CELLS - l * LANES)
        out_ref[:, l * LANES : l * LANES + width] = x_ref[l : l + 1, 0:width]


def rounds(tiles):
    out = []
    stride = 1
    while stride < tiles:
        radix = 4 if (tiles // stride) % 4 == 0 else 2
        out.append((stride, radix))
        stride *= radix
    return out


def swap(x, tiles, offset):
    return lax.ppermute(x, "tile", [(t, t ^ offset) for t in range(tiles)])


def gather_tiles(block, tiles):
    held = [block]
    counts = [1]
    for stride, radix in rounds(tiles):
        whole = held[0] if len(held) == 1 else jnp.concatenate(held, axis=0)
        for number in range(1, radix):
            held.append(swap(whole, tiles, number * stride))
            counts.append(stride)
    return held, tuple(counts)


def sum_tiles(block, tiles):
    held = [block]
    for stride, radix in rounds(tiles):
        whole = functools.reduce(jnp.add, held)
        held = [whole] + [swap(whole, tiles, number * stride) for number in range(1, radix)]
    return held


def shards(thermal, stirring, depth, adjacent, flags, main_entry, sensitivity, elevation, tiles):
    levels = thermal.shape[1]
    me = lax.axis_index("tile").astype(I32).reshape(1)
    smem = pl.BlockSpec(memory_space=pltpu.SMEM)
    vmem = pl.BlockSpec(memory_space=pltpu.VMEM)
    params = pltpu.CompilerParams(vmem_limit_bytes=48 * 1024 * 1024)

    def shape(*dims):
        return jax.ShapeDtypeStruct(dims, F32)

    def call(kernel, outs, scratch, scalars, arrays, name, flops=1e6, traffic=1e6):
        return pl.pallas_call(
            kernel,
            out_shape=outs,
            in_specs=[smem] * len(scalars) + [vmem] * len(arrays),
            out_specs=jax.tree.map(lambda _: vmem, outs),
            scratch_shapes=scratch,
            compiler_params=params,
            cost_estimate=pl.CostEstimate(flops=int(flops), bytes_accessed=int(traffic), transcendentals=0),
            name=name,
        )(*scalars, *arrays)

    offsets = []
    for offset in (1, -1, ROW_TILES, -ROW_TILES, tiles // 2):
        if offset % tiles not in [o % tiles for o in offsets] and offset % tiles:
            offsets.append(offset)
    shifts = tuple(offset % tiles for offset in offsets)

    def to_neighbours(x):
        out = []
        for offset in offsets:
            pairs = [(t, t + offset) for t in range(tiles) if 0 <= t + offset < tiles]
            if 2 * offset == tiles or 2 * offset == -tiles:
                pairs = [(t, (t + offset) % tiles) for t in range(tiles)]
            out.append(lax.ppermute(x, "tile", pairs))
        return out

    strips, block, dense = call(
        edges_kernel,
        (shape(4, 32, LANES), shape(BLOCK, LANES), shape(3 * ROWS, LANES)),
        [pltpu.VMEM((2, 32, LANES), F32)],
        (adjacent, flags),
        (thermal, depth, main_entry, elevation),
        "edges",
    )
    strips_met = to_neighbours(strips)
    blocks, counts = gather_tiles(block, tiles)
    big = pltpu.VMEM((levels * ROWS, LANES), F32)
    solved, weight, forcing_inside, edge_lines = call(
        functools.partial(columns_kernel, levels),
        (shape(levels * ROWS, LANES), shape(levels * ROWS, LANES), shape(ROWS, LANES), shape(8, 32, LANES)),
        [big, big, big, pltpu.VMEM((8, 32, LANES), F32)],
        (),
        (stirring, sensitivity, thermal, dense),
        "columns",
        2e7,
        8e6,
    )
    edge_lines_met = to_neighbours(edge_lines)
    forcing, forcing_frames, reach = call(
        functools.partial(forcing_kernel, shifts, tiles, levels),
        (shape(ROWS, LANES), shape(16, LANES), shape(8, LANES)),
        [pltpu.VMEM((8, LANES), F32), pltpu.VMEM((8, LANES), F32)],
        (me, adjacent, flags),
        (forcing_inside, strips, edge_lines, *strips_met),
        "forcing",
    )
    forcing_blocks, _ = gather_tiles(forcing_frames, tiles)
    lines = 4 * tiles
    frame = pltpu.VMEM((4, lines, LANES), F32)
    prepared = call(
        functools.partial(prepare_kernel, counts, lines),
        (
            jax.ShapeDtypeStruct((3 * lines, lines), jnp.bfloat16),
            jax.ShapeDtypeStruct((3 * lines, LANES), I32),
            shape(3, 5, lines, LANES),
            shape(3, ROWS, LANES),
            shape(8, LANES),
        ),
        [pltpu.VMEM((6, lines, LANES), F32), frame, frame],
        (me,),
        (dense, *blocks),
        "prepare",
    )

    def krylov(rhs, rhs_blocks, rows, name):
        return call(
            functools.partial(krylov_kernel, counts, rows, lines),
            (shape(ITERS - 1, ROWS, LANES), shape(ITERS, 8, LANES), shape(16, LANES)),
            [frame],
            (),
            (rhs, *prepared, *rhs_blocks),
            name,
        )

    basis_b, lines_b, gram_b = krylov(dense, blocks, BLOCK, "krylov_adjoint")
    grams_b = sum_tiles(gram_b, tiles)
    basis_a, _, gram_a = krylov(forcing, forcing_blocks, 16, "krylov_forward")
    grams_a = sum_tiles(gram_a, tiles)
    gradient = call(
        functools.partial(gradient_kernel, shifts, tiles, levels, len(grams_b)),
        jax.ShapeDtypeStruct(thermal.shape, F32),
        [pltpu.VMEM((16, LANES), F32), pltpu.VMEM((5, 32, LANES), F32), big],
        (me, adjacent, flags),
        (*grams_b, dense, basis_b, lines_b, block, reach, solved, weight, edge_lines, *edge_lines_met),
        "gradient",
        1e7,
        4e6,
    )
    height = call(
        functools.partial(height_kernel, len(grams_a)),
        jax.ShapeDtypeStruct(elevation.shape, F32),
        [pltpu.VMEM((16, LANES), F32), pltpu.VMEM((ROWS, LANES), F32)],
        (),
        (*grams_a, forcing, basis_a),
        "height",
    )
    return height, gradient


def solution(mesh):
    placed = (
        P(("ens", "tile"), None, None),
        P("tile", None, None),
        P("tile", None),
        P("tile", None),
        P("tile", None),
        P("tile", None),
        P(("ens", "tile"), None, None),
        P(("ens", "tile"), None),
    )
    return jax.shard_map(
        functools.partial(shards, tiles=mesh.shape["tile"]),
        mesh=mesh,
        in_specs=placed,
        out_specs=(P(("ens", "tile"), None), P(("ens", "tile"), None, None)),
        check_vma=False,
    )
```

```python
import functools
import math

import jax
import jax.numpy as jnp
from jax import lax
from jax.experimental import pallas as pl
from jax.experimental.pallas import tpu as pltpu
from jax.sharding import PartitionSpec as P

SIDE = 90
CELLS = SIDE * SIDE
ROWS = 64
LANES = 128
ITERS = 4
ROW_TILES = 8
SPREAD = 0.2
CENTRE = 4.1
BLOCK = 88
F32 = jnp.float32
I32 = jnp.int32


def grid_iotas():
    row = lax.broadcasted_iota(I32, (ROWS, LANES), 0)
    lane = lax.broadcasted_iota(I32, (ROWS, LANES), 1)
    cell = row * LANES + lane
    i = (cell * 46604) >> 22
    j = cell - SIDE * i
    return row, lane, cell, i, j


def ahead(x, n):
    lane = lax.broadcasted_iota(I32, x.shape, 1)
    y = pltpu.roll(x, LANES - n, 1)
    return jnp.where(lane < LANES - n, y, pltpu.roll(y, ROWS - 1, 0))


def behind(x, n):
    lane = lax.broadcasted_iota(I32, x.shape, 1)
    y = pltpu.roll(x, n, 1)
    return jnp.where(lane >= n, y, pltpu.roll(y, 1, 0))


def take(x, index):
    pieces = []
    for first in range(0, x.shape[0], 8):
        part = index if index.shape[0] == 8 else index[first : first + 8]
        pieces.append(jnp.take_along_axis(x[first : first + 8], part, axis=1, mode="promise_in_bounds"))
    return pieces[0] if len(pieces) == 1 else jnp.concatenate(pieces, axis=0)


def lanes8():
    return lax.broadcasted_iota(I32, (8, LANES), 1)


def column_owner(lane):
    odd = lane & 1
    half = (lane - 89 * odd) >> 1
    return (37 * half) & 63


def lines_23(za, zb, depth_row):
    lane = lanes8()
    near = (SIDE * lane + depth_row) & 127
    far = (SIDE * lane + SIDE - 1 - depth_row) & 127
    wide = lax.broadcasted_iota(I32, za.shape, 1)
    first = wide < 64
    return (
        jnp.where(first, take(za, near), take(zb, near)),
        jnp.where(first, take(za, far), take(zb, far)),
    )


def spread_lines(side2, side3, side1):
    lane = lanes8()
    owner = column_owner(lane)
    later = (owner + 64) & 127
    even = (lax.broadcasted_iota(I32, side2.shape, 1) & 1) == 0
    wa = jnp.where(even, take(side2, owner), take(side3, owner))
    wb = jnp.where(even, take(side2, later), take(side3, later))
    return wa, wb, pltpu.roll(side1, 74, 1)


def scatter_masks():
    row, lane, cell, i, j = grid_iotas()
    column = (j == 0) | (j == SIDE - 1)
    return (
        column & (i < 64),
        column & (i >= 64) & (i < SIDE),
        cell < SIDE,
        i == SIDE - 1,
    )


def scatter_rows(masks, wa, wb, side0, w1):
    zero = jnp.zeros((ROWS, LANES), F32)
    out = jnp.where(masks[0], wa, zero) + jnp.where(masks[1], wb, zero)
    return out + jnp.where(masks[2], side0, zero) + jnp.where(masks[3], w1, zero)


def scatter_lines(masks, lines):
    wa, wb, w1 = spread_lines(
        jnp.broadcast_to(lines[2:3], (8, LANES)),
        jnp.broadcast_to(lines[3:4], (8, LANES)),
        jnp.broadcast_to(lines[1:2], (8, LANES)),
    )
    return scatter_rows(masks, wa[0:1], wb[0:1], lines[0:1], w1[0:1])


def row_line(ref, base, first_cell):
    row, off = divmod(first_cell, LANES)
    top = ref[pl.ds(base + row, 1), :]
    if off == 0:
        return top
    lane = lax.broadcasted_iota(I32, (1, LANES), 1)
    top = pltpu.roll(top, LANES - off, 1)
    if off + SIDE <= LANES:
        return top
    low = pltpu.roll(ref[pl.ds(base + row + 1, 1), :], LANES - off, 1)
    return jnp.where(lane < LANES - off, top, low)


def write_frames(field_ref, base, out_ref, first_row, za_ref, zb_ref):
    field = field_ref[base : base + ROWS, :]
    row, lane, cell, i, j = grid_iotas()
    zero = jnp.zeros_like(field)
    for depth in range(4):
        column = (j == depth) | (j == SIDE - 1 - depth)
        za = jnp.where(column & (i < 64), field, zero)
        zb = jnp.where(column & (i >= 64), field, zero)
        za_ref[depth : depth + 1, :] = jnp.sum(za, axis=0, keepdims=True)
        zb_ref[depth : depth + 1, :] = jnp.sum(zb, axis=0, keepdims=True)
        out_ref[first_row + depth * 4 : first_row + depth * 4 + 1, :] = row_line(
            field_ref, base, depth * SIDE
        )
        out_ref[first_row + depth * 4 + 1 : first_row + depth * 4 + 2, :] = row_line(
            field_ref, base, (SIDE - 1 - depth) * SIDE
        )
    for depth in range(4, 8):
        za_ref[depth : depth + 1, :] = jnp.zeros((1, LANES), F32)
        zb_ref[depth : depth + 1, :] = jnp.zeros((1, LANES), F32)
    depth_row = lax.broadcasted_iota(I32, (8, LANES), 0) & 3
    side2, side3 = lines_23(za_ref[0:8, :], zb_ref[0:8, :], depth_row)
    for depth in range(4):
        at = first_row + depth * 4
        out_ref[at + 2 : at + 3, :] = side2[depth : depth + 1]
        out_ref[at + 3 : at + 4, :] = side3[depth : depth + 1]


def level_rows(ref, level):
    whole = (CELLS // LANES // 8) * 8
    rows = CELLS // LANES
    window = ref[level, :, CELLS - LANES : CELLS]
    return jnp.concatenate(
        [
            ref[level, :, 0 : whole * LANES].reshape(whole, LANES),
            ref[level, :, whole * LANES : rows * LANES].reshape(rows - whole, LANES),
            pltpu.roll(window, CELLS - rows * LANES, 1),
        ],
        axis=0,
    )


def surface_rows(ref):
    whole = (CELLS // LANES // 8) * 8
    rows = CELLS // LANES
    window = ref[:, CELLS - LANES : CELLS]
    return jnp.concatenate(
        [
            ref[:, 0 : whole * LANES].reshape(whole, LANES),
            ref[:, whole * LANES : rows * LANES].reshape(rows - whole, LANES),
            pltpu.roll(window, CELLS - rows * LANES, 1),
        ],
        axis=0,
    )


def interior_reach(depth):
    row, lane, cell, i, j = grid_iotas()
    zero = jnp.zeros_like(depth)
    along = jnp.where(j < SIDE - 1, jnp.minimum(depth, ahead(depth, 1)), zero)
    across = jnp.where(cell < CELLS - SIDE, jnp.minimum(depth, ahead(depth, SIDE)), zero)
    return along, across


def interior_spread(x, along, across, level):
    zero = jnp.zeros_like(x)
    flux1 = jnp.where(along > level, ahead(x, 1) - x, zero)
    flux2 = jnp.where(across > level, ahead(x, SIDE) - x, zero)
    return (flux1 - behind(flux1, 1)) + (flux2 - behind(flux2, SIDE))


def columns_kernel(
    levels,
    adj_ref,
    flag_ref,
    k_ref,
    s_ref,
    t_ref,
    depth_ref,
    d_ref,
    b_ref,
    a_ref,
    q_ref,
    f_ref,
    ts_ref,
    aq_ref,
    blk_ref,
    dense_ref,
    g_ref,
    z_ref,
):
    row, lane, cell, i, j = grid_iotas()
    inside = cell < CELLS
    for number, ref in enumerate((b_ref, d_ref, depth_ref)):
        rows = slice(number * ROWS, (number + 1) * ROWS)
        dense_ref[rows, :] = jnp.where(inside, surface_rows(ref).astype(F32), 0.0)
        write_frames(dense_ref, number * ROWS, blk_ref, number * 16, z_ref.at[0], z_ref.at[1])
    at = 48
    for sides in ((0, 1, 2, 3), (2, 2, 0, 0), (3, 3, 1, 1)):
        for ref in (adj_ref, flag_ref):
            for side in sides:
                blk_ref[at : at + 1, :] = jnp.full((1, LANES), ref[0, side], I32).astype(F32)
                at += 1
    depth = dense_ref[2 * ROWS : 3 * ROWS, :]
    along, across = interior_reach(depth)
    zero = jnp.zeros((ROWS, LANES), F32)

    def down(level, carry):
        link, below, va, vq = carry
        at = pl.ds(pl.multiple_of(level * ROWS, ROWS), ROWS)
        here = level.astype(F32)
        r = jnp.where(depth > here + 1.0, level_rows(k_ref, level), zero)
        wet = jnp.where(depth > here, 1.0, zero)
        upper = 1.0 + below
        inverse = 1.0 / (upper + r)
        ratio = r * inverse
        va = (level_rows(s_ref, level) + link * va) * inverse
        vq = (wet + link * vq) * inverse
        g_ref[at, :] = ratio
        a_ref[at, :] = va
        q_ref[at, :] = vq
        return r, upper * ratio, va, vq

    lax.fori_loop(0, levels, down, (zero, zero, zero, zero), unroll=2)
    column = ((j == 0) | (j == SIDE - 1)) & (i < SIDE)
    first = (column & (i < 64))[0:48]
    second = (column & (i >= 64))[40:ROWS]

    def up(step, carry):
        xa, xq, total = carry
        level = levels - 1 - step
        at = pl.ds(pl.multiple_of(level * ROWS, ROWS), ROWS)
        ratio = g_ref[at, :]
        xa = a_ref[at, :] + ratio * xa
        xq = q_ref[at, :] + ratio * xq
        a_ref[at, :] = xa
        q_ref[at, :] = xq
        t = level_rows(t_ref, level)
        here = pl.ds(level, 1)
        for number, x in enumerate((t, xa, xq)):
            base = number * 4
            z_ref[base, here, :] = jnp.sum(jnp.where(first, x[0:48], 0.0), axis=0, keepdims=True)
            z_ref[base + 1, here, :] = jnp.sum(jnp.where(second, x[40:ROWS], 0.0), axis=0, keepdims=True)
            out, side0 = (ts_ref, 0) if number == 0 else (aq_ref, (number - 1) * 4)
            out[side0, here, :] = x[0:1]
            z_ref[base + 2, here, :] = x[ROWS - 2 : ROWS - 1]
            z_ref[base + 3, here, :] = x[ROWS - 1 : ROWS]
        mixed_h = t + SPREAD * interior_spread(t, along, across, level.astype(F32))
        return xa, xq, total + xq * mixed_h

    xa, xq, total = lax.fori_loop(0, levels, up, (zero, zero, zero), unroll=2)
    f_ref[...] = jnp.where(inside, total, zero)
    spare = z_ref.shape[1] - levels
    for number in range(3):
        base = number * 4
        out, at = (ts_ref, 0) if number == 0 else (aq_ref, (number - 1) * 4)
        for part in range(4):
            z_ref[base + part, levels:, :] = jnp.zeros((spare, LANES), F32)
        out[at, levels:, :] = jnp.zeros((spare, LANES), F32)
        side2, side3 = lines_23(z_ref[base], z_ref[base + 1], 0)
        out[at + 2] = side2
        out[at + 3] = side3
        low, high = z_ref[base + 2], z_ref[base + 3]
        wide = lax.broadcasted_iota(I32, low.shape, 1)
        out[at + 1] = jnp.where(wide < 54, pltpu.roll(low, 54, 1), pltpu.roll(high, 54, 1))
    for side in range(4):
        ts_ref[side, levels : levels + 1, :] = blk_ref[32 + side : 33 + side, :]


def pick(refs, shifts, tiles, me, neighbour, first, side_met):
    value = refs[0][first + side_met]
    for number in range(1, len(shifts)):
        hit = neighbour == lax.rem(me + tiles - shifts[number], tiles)
        value = jnp.where(hit, refs[number][first + side_met], value)
    return value


def seam_index(flag):
    lane = lanes8()
    return jnp.where((flag & 1) == 1, SIDE - 1 - lane, lane) & 127


def forcing_kernel(shifts, tiles, levels, me_ref, adj_ref, flag_ref, f_ref, ts_ref, aq_ref, blk_ref, *rest):
    refs = rest[: len(shifts)]
    out_ref, frame_ref, reach_ref, za_ref, zb_ref = rest[len(shifts) :]
    me = me_ref[0]
    level = lax.broadcasted_iota(I32, (32, LANES), 0).astype(F32)
    lines = []
    for side in range(4):
        neighbour = adj_ref[0, side]
        flag = flag_ref[0, side]
        other = take(pick(refs, shifts, tiles, me, neighbour, 0, flag >> 1), seam_index(flag))
        own = ts_ref[side]
        reach = jnp.minimum(other[levels : levels + 1], own[levels : levels + 1])
        reach = jnp.where(neighbour >= 0, reach, 0.0)
        reach_ref[side : side + 1, :] = reach
        flux = jnp.where(reach > level, other - own, 0.0)
        lines.append(jnp.sum(aq_ref[4 + side] * flux, axis=0, keepdims=True))
    reach_ref[4:8, :] = jnp.zeros((4, LANES), F32)
    seams = scatter_lines(scatter_masks(), jnp.concatenate(lines + lines, axis=0))
    out_ref[...] = (f_ref[...] + SPREAD * seams) * (1.0 / math.sqrt(levels))
    frame_ref[0:72, :] = blk_ref[...]
    write_frames(out_ref, 0, frame_ref, 72, za_ref, zb_ref)


def block_rows(refs, counts, block, first, size):
    position = 0
    for ref, count in zip(refs, counts):
        for number in range(count):
            at = number * block + first
            yield position, ref[at : at + size, :]
            position += 1


def gather_lines(p, lines):
    high = lines.astype(jnp.bfloat16)
    rest = lines - high.astype(F32)
    middle = rest.astype(jnp.bfloat16)
    low = (rest - middle.astype(F32)).astype(jnp.bfloat16)
    out = jnp.dot(p, high, preferred_element_type=F32)
    out = out + jnp.dot(p, middle, preferred_element_type=F32)
    return out + jnp.dot(p, low, preferred_element_type=F32)


def ends(x, low, high, low_parity, high_parity, depth):
    lane = lax.broadcasted_iota(I32, x.shape, 1)
    low_end = take(low, jnp.where(low_parity == 1, SIDE - 1 - depth, depth))
    high_end = take(high, jnp.where(high_parity == 1, SIDE - 1 - depth, depth))
    return (
        jnp.where(lane == 0, low_end, pltpu.roll(x, 1, 1)),
        jnp.where(lane == SIDE - 1, high_end, pltpu.roll(x, LANES - 1, 1)),
    )


def krylov_kernel(counts, lines, me_ref, dense_ref, forcing_ref, *rest):
    refs = rest[: len(counts)]
    va_ref, vb_ref, line_ref, gram_ref = rest[len(counts) : len(counts) + 4]
    p_ref, index_ref, frame_ref, work_ref, depth_ref, d_ref, x_ref = rest[len(counts) + 4 :]
    me = me_ref[0]
    for number in range(6):
        for position, rows in block_rows(refs, counts, BLOCK, 48 + 4 * number, 4):
            work_ref[number, position * 4 : position * 4 + 4, :] = rows
    for depth in range(4):
        for position, rows in block_rows(refs, counts, BLOCK, 16 + 4 * depth, 4):
            d_ref[depth, position * 4 : position * 4 + 4, :] = rows
        for position, rows in block_rows(refs, counts, BLOCK, 32 + 4 * depth, 4):
            depth_ref[depth, position * 4 : position * 4 + 4, :] = rows
    lane = lax.broadcasted_iota(I32, (lines, LANES), 1)
    odd = lax.broadcasted_iota(I32, (lines, LANES), 0) & 1
    column = lax.broadcasted_iota(I32, (lines, lines), 1)
    for number in range(3):
        tile = work_ref[2 * number, :, 0:1].astype(I32)
        flag = work_ref[2 * number + 1, :, 0:1].astype(I32)
        at = jnp.where(tile >= 0, 4 * (tile ^ me) + (flag >> 1), -1)
        p = jnp.where(jnp.broadcast_to(at, (lines, lines)) == column, 1.0, 0.0)
        p_ref[number * lines : (number + 1) * lines, :] = p.astype(jnp.bfloat16)
        parity = work_ref[2 * number + 1].astype(I32) & 1
        if number == 0:
            index_ref[0:lines, :] = jnp.where(parity == 1, SIDE - 1 - lane, lane) & 127
        else:
            index_ref[number * lines : (number + 1) * lines, :] = parity ^ odd
    wet = [jnp.where(depth_ref[depth] > 0.0, 1.0, 0.0) for depth in range(4)]
    met = gather_lines(p_ref[...], wet[0])
    facing = take(met[0:lines], index_ref[0:lines, :])
    for depth in range(3):
        low, high = ends(
            wet[depth],
            met[lines : 2 * lines],
            met[2 * lines : 3 * lines],
            index_ref[lines : 2 * lines, :],
            index_ref[2 * lines : 3 * lines, :],
            depth,
        )
        masks = [
            wet[depth] * (facing if depth == 0 else wet[depth - 1]),
            wet[depth] * wet[depth + 1],
            wet[depth] * low,
            wet[depth] * high,
        ]
        frame_ref[depth, 0] = d_ref[depth] + ((masks[0] + masks[1]) + (masks[2] + masks[3]))
        for number in range(4):
            frame_ref[depth, 1 + number] = masks[number]
        if depth == 0:
            seam = masks[0][0:8]
    surface = jnp.minimum(dense_ref[2 * ROWS : 3 * ROWS, :], 1.0)
    along, across = interior_reach(surface)
    degree = (along + behind(along, 1)) + (across + behind(across, SIDE))
    masks = scatter_masks()
    diagonal = dense_ref[ROWS : 2 * ROWS, :] + (degree + scatter_lines(masks, seam))
    p = p_ref[...]
    facing_at = index_ref[0:lines, :]
    low_parity = index_ref[lines : 2 * lines, :]
    high_parity = index_ref[2 * lines : 3 * lines, :]
    scale = 2.0 / CENTRE
    row, lane, cell, i, j = grid_iotas()
    inside = cell < CELLS
    frames = []
    own = []
    for solve, first in enumerate((0, 72)):
        for depth in range(4):
            for position, rows in block_rows(refs, counts, BLOCK, first + 4 * depth, 4):
                x_ref[solve * 4 + depth, position * 4 : position * 4 + 4, :] = rows
        frames.append([[x_ref[solve * 4 + depth] for depth in range(4)]])
        own.append([(dense_ref if solve == 0 else forcing_ref)[0:ROWS, :]])
    for step in range(ITERS):
        for solve in range(2):
            x = frames[solve][-1]
            met = gather_lines(p, x[0])
            facing = take(met[0:lines], facing_at)
            if solve == 0:
                line_ref[step] = facing[0:8]
            mine = own[solve][-1]
            flow = (along * ahead(mine, 1) + behind(along * mine, 1)) + (
                across * ahead(mine, SIDE) + behind(across * mine, SIDE)
            )
            image = diagonal * mine - flow - scatter_lines(masks, seam * facing[0:8])
            image = jnp.where(inside, scale * image - 2.0 * mine, 0.0)
            own[solve].append(0.5 * image if step == 0 else image - own[solve][-2])
            following = []
            for depth in range(ITERS - 1 - step):
                low, high = ends(
                    x[depth],
                    met[lines : 2 * lines],
                    met[2 * lines : 3 * lines],
                    low_parity,
                    high_parity,
                    depth,
                )
                before = facing if depth == 0 else x[depth - 1]
                flow = (frame_ref[depth, 1] * before + frame_ref[depth, 2] * x[depth + 1]) + (
                    frame_ref[depth, 3] * low + frame_ref[depth, 4] * high
                )
                image = scale * (frame_ref[depth, 0] * x[depth] - flow) - 2.0 * x[depth]
                following.append(0.5 * image if step == 0 else image - frames[solve][-2][depth])
            frames[solve].append(following)
            if step < ITERS - 1:
                (vb_ref if solve == 0 else va_ref)[step] = own[solve][-1]
    for solve in range(2):
        at = 16 * solve
        for first in range(ITERS + 1):
            for second in range(first + 1):
                gram_ref[at : at + 1, :] = jnp.sum(own[solve][first] * own[solve][second], axis=0, keepdims=True)
                at += 1
        gram_ref[at : at + 1, :] = jnp.zeros((1, LANES), F32)


def image_of(p):
    out = [None] * (len(p) + 1)

    def add(at, value):
        out[at] = value if out[at] is None else out[at] + value

    for at, value in enumerate(p):
        add(at, CENTRE * value)
        if at == 0:
            add(1, CENTRE * value)
        else:
            add(at + 1, 0.5 * CENTRE * value)
            add(at - 1, 0.5 * CENTRE * value)
    return out


def form(left, gram, right):
    total = None
    for first, x in enumerate(left):
        inner = None
        for second, y in enumerate(right):
            term = gram[max(first, second)][min(first, second)] * y
            inner = term if inner is None else inner + term
        total = x * inner if total is None else total + x * inner
    return total


def total_gram(refs, sum_ref):
    total = refs[0][...]
    for ref in refs[1:]:
        total = total + ref[...]
    sum_ref[...] = jnp.broadcast_to(jnp.sum(total, axis=1, keepdims=True), sum_ref.shape)


def coefficients(sum_ref, at):
    gram = []
    for first in range(ITERS + 1):
        gram.append([sum_ref[at + second : at + second + 1, :] for second in range(first + 1)])
        at += first + 1
    one = jnp.ones((1, LANES), F32)
    x = []
    r = [one]
    p = [one]
    rr = gram[0][0]
    for step in range(ITERS):
        image = image_of(p)
        curve = form(p, gram, image)
        alpha = jnp.where(curve > 0.0, rr / curve, 0.0)
        x = [x[n] + alpha * p[n] if n < len(x) else alpha * p[n] for n in range(len(p))]
        r = [r[n] - alpha * image[n] if n < len(r) else -alpha * image[n] for n in range(len(image))]
        if step < ITERS - 1:
            new = jnp.maximum(form(r, gram, r), 0.0)
            beta = jnp.where(rr > 0.0, new / rr, 0.0)
            p = [r[n] + beta * p[n] if n < len(p) else r[n] for n in range(len(r))]
            rr = new
    return x


def store_rows(ref, rows):
    last = CELLS // LANES
    ref[:, 0 : last * LANES] = rows[0:last].reshape(1, last * LANES)
    ref[:, last * LANES : CELLS] = rows[last : last + 1, 0 : CELLS - last * LANES]


def combine(x, b_ref, v_ref):
    out = x[0] * b_ref[0:ROWS, :]
    for number in range(1, ITERS):
        out = out + x[number] * v_ref[number - 1]
    return out


def gradient_kernel(shifts, tiles, levels, grams, me_ref, adj_ref, flag_ref, *rest):
    gram_refs = rest[:grams]
    rest = rest[grams:]
    dense_ref, forcing_ref, va_ref, v_ref, line_ref, blk_ref, reach_ref, a_ref, q_ref, aq_ref = rest[:10]
    refs = rest[10 : 10 + len(shifts)]
    height_ref, out_ref, gram_ref, sum_ref, w_ref, h_ref = rest[10 + len(shifts) :]
    me = me_ref[0]
    total_gram(gram_refs, gram_ref)
    store_rows(height_ref, combine(coefficients(gram_ref, 16), forcing_ref, va_ref))
    x = coefficients(gram_ref, 0)
    level_scale = 1.0 / math.sqrt(levels)
    adjoint = combine(x, dense_ref, v_ref) * level_scale
    met_line = x[0] * line_ref[0]
    depth = dense_ref[2 * ROWS : 3 * ROWS, :]
    along, across = interior_reach(depth)
    sum_ref[0:8, :] = met_line + x[1] * line_ref[1] + x[2] * line_ref[2] + x[3] * line_ref[3]
    h_ref[0:ROWS, :] = adjoint
    w_ref[4, 8:9, :] = h_ref[0:1, :]
    w_ref[4, 9:10, :] = row_line(h_ref, 0, (SIDE - 1) * SIDE)
    row, lane, cell, i, j = grid_iotas()
    column = (j == 0) | (j == SIDE - 1)
    zero = jnp.zeros((ROWS, LANES), F32)
    za = jnp.sum(jnp.where(column & (i < 64), adjoint, zero), axis=0, keepdims=True)
    zb = jnp.sum(jnp.where(column & (i >= 64), adjoint, zero), axis=0, keepdims=True)
    side2, side3 = lines_23(jnp.broadcast_to(za, (8, LANES)), jnp.broadcast_to(zb, (8, LANES)), 0)
    w_ref[4, 10:11, :] = side2[0:1]
    w_ref[4, 11:12, :] = side3[0:1]
    level = lax.broadcasted_iota(I32, (32, LANES), 0).astype(F32)
    fluxes = []
    for side in range(4):
        neighbour = adj_ref[0, side]
        flag = flag_ref[0, side]
        index = seam_index(flag)
        a_other = take(pick(refs, shifts, tiles, me, neighbour, 0, flag >> 1), index)
        q_other = take(pick(refs, shifts, tiles, me, neighbour, 4, flag >> 1), index)
        other = a_other + (sum_ref[side : side + 1, :] * level_scale) * q_other
        own = aq_ref[side] + w_ref[4, 8 + side : 9 + side, :] * aq_ref[4 + side]
        fluxes.append(jnp.where(reach_ref[side : side + 1, :] > level, other - own, 0.0))
    wa, wb, w1 = spread_lines(fluxes[2], fluxes[3], fluxes[1])
    w_ref[0] = wa
    w_ref[1] = wb
    w_ref[2] = fluxes[0]
    w_ref[3] = w1
    masks = scatter_masks()

    def per_level(number, carry):
        at = pl.ds(pl.multiple_of(number * ROWS, ROWS), ROWS)
        here = pl.ds(number, 1)
        h = a_ref[at, :] + adjoint * q_ref[at, :]
        spread = interior_spread(h, along, across, number.astype(F32))
        spread = spread + scatter_rows(
            masks, w_ref[0, here, :], w_ref[1, here, :], w_ref[2, here, :], w_ref[3, here, :]
        )
        store_rows(out_ref.at[number], h + SPREAD * spread)
        return carry

    lax.fori_loop(0, levels, per_level, 0, unroll=2)


def rounds(tiles):
    out = []
    stride = 1
    while stride < tiles:
        radix = 4 if (tiles // stride) % 4 == 0 else 2
        out.append((stride, radix))
        stride *= radix
    return out


def swap(x, tiles, offset):
    return lax.ppermute(x, "tile", [(t, t ^ offset) for t in range(tiles)])


def gather_tiles(block, tiles):
    held = [block]
    counts = [1]
    for stride, radix in rounds(tiles):
        whole = held[0] if len(held) == 1 else jnp.concatenate(held, axis=0)
        for number in range(1, radix):
            held.append(swap(whole, tiles, number * stride))
            counts.append(stride)
    return held, tuple(counts)


def sum_tiles(block, tiles):
    held = [block]
    for stride, radix in rounds(tiles):
        whole = functools.reduce(jnp.add, held)
        held = [whole] + [swap(whole, tiles, number * stride) for number in range(1, radix)]
    return held


def shards(thermal, stirring, depth, adjacent, flags, main_entry, sensitivity, elevation, tiles):
    levels = thermal.shape[1]
    me = lax.axis_index("tile").astype(I32).reshape(1)
    smem = pl.BlockSpec(memory_space=pltpu.SMEM)
    vmem = pl.BlockSpec(memory_space=pltpu.VMEM)
    params = pltpu.CompilerParams(vmem_limit_bytes=48 * 1024 * 1024)

    def shape(*dims):
        return jax.ShapeDtypeStruct(dims, F32)

    def call(kernel, outs, scratch, scalars, arrays, name, flops=1e6, traffic=1e6):
        return pl.pallas_call(
            kernel,
            out_shape=outs,
            in_specs=[smem] * len(scalars) + [vmem] * len(arrays),
            out_specs=jax.tree.map(lambda _: vmem, outs),
            scratch_shapes=scratch,
            compiler_params=params,
            cost_estimate=pl.CostEstimate(flops=int(flops), bytes_accessed=int(traffic), transcendentals=0),
            name=name,
        )(*scalars, *arrays)

    offsets = []
    for offset in (1, -1, ROW_TILES, -ROW_TILES, tiles // 2):
        if offset % tiles not in [o % tiles for o in offsets] and offset % tiles:
            offsets.append(offset)
    shifts = tuple(offset % tiles for offset in offsets)

    def to_neighbours(x):
        out = []
        for offset in offsets:
            pairs = [(t, t + offset) for t in range(tiles) if 0 <= t + offset < tiles]
            if 2 * offset == tiles or 2 * offset == -tiles:
                pairs = [(t, (t + offset) % tiles) for t in range(tiles)]
            out.append(lax.ppermute(x, "tile", pairs))
        return out

    def by_level(x):
        return jnp.transpose(x, (1, 0, 2))

    big = pltpu.VMEM((levels * ROWS, LANES), F32)
    solved, weight, forcing_inside, strips, edge_lines, block, dense = call(
        functools.partial(columns_kernel, levels),
        (
            shape(levels * ROWS, LANES),
            shape(levels * ROWS, LANES),
            shape(ROWS, LANES),
            shape(4, 32, LANES),
            shape(8, 32, LANES),
            shape(72, LANES),
            shape(3 * ROWS, LANES),
        ),
        [big, pltpu.VMEM((12, 32, LANES), F32)],
        (adjacent, flags),
        (by_level(stirring), by_level(sensitivity), by_level(thermal), depth, main_entry, elevation),
        "columns",
        2e7,
        8e6,
    )
    strips_met = to_neighbours(strips)
    forcing, frames, reach = call(
        functools.partial(forcing_kernel, shifts, tiles, levels),
        (shape(ROWS, LANES), shape(BLOCK, LANES), shape(8, LANES)),
        [pltpu.VMEM((8, LANES), F32), pltpu.VMEM((8, LANES), F32)],
        (me, adjacent, flags),
        (forcing_inside, strips, edge_lines, block, *strips_met),
        "forcing",
    )
    blocks, counts = gather_tiles(frames, tiles)
    edge_lines_met = to_neighbours(edge_lines)
    lines = 4 * tiles
    frame = pltpu.VMEM((4, lines, LANES), F32)
    basis = shape(ITERS - 1, ROWS, LANES)
    basis_a, basis_b, lines_b, gram = call(
        functools.partial(krylov_kernel, counts, lines),
        (basis, basis, shape(ITERS, 8, LANES), shape(32, LANES)),
        [
            pltpu.VMEM((3 * lines, lines), jnp.bfloat16),
            pltpu.VMEM((3 * lines, LANES), I32),
            pltpu.VMEM((3, 5, lines, LANES), F32),
            pltpu.VMEM((6, lines, LANES), F32),
            frame,
            frame,
            pltpu.VMEM((8, lines, LANES), F32),
        ],
        (me,),
        (dense, forcing, *blocks),
        "krylov",
    )
    grams = sum_tiles(gram, tiles)
    height, gradient = call(
        functools.partial(gradient_kernel, shifts, tiles, levels, len(grams)),
        (jax.ShapeDtypeStruct(elevation.shape, F32), shape(levels, 1, CELLS)),
        [
            pltpu.VMEM((32, LANES), F32),
            pltpu.VMEM((16, LANES), F32),
            pltpu.VMEM((5, 32, LANES), F32),
            pltpu.VMEM((ROWS, LANES), F32),
        ],
        (me, adjacent, flags),
        (
            *grams,
            dense,
            forcing,
            basis_a,
            basis_b,
            lines_b,
            block,
            reach,
            solved,
            weight,
            edge_lines,
            *edge_lines_met,
        ),
        "gradient",
        1e7,
        4e6,
    )
    gradient = by_level(gradient)
    return height, gradient


def solution(mesh):
    placed = (
        P(("ens", "tile"), None, None),
        P("tile", None, None),
        P("tile", None),
        P("tile", None),
        P("tile", None),
        P("tile", None),
        P(("ens", "tile"), None, None),
        P(("ens", "tile"), None),
    )
    return jax.shard_map(
        functools.partial(shards, tiles=mesh.shape["tile"]),
        mesh=mesh,
        in_specs=placed,
        out_specs=(P(("ens", "tile"), None), P(("ens", "tile"), None, None)),
        check_vma=False,
    )
```

```python
import functools
import math

import jax
import jax.numpy as jnp
from jax import lax
from jax.experimental import pallas as pl
from jax.experimental.pallas import tpu as pltpu
from jax.sharding import PartitionSpec as P

SIDE = 90
CELLS = SIDE * SIDE
ROWS = 64
LANES = 128
ITERS = 4
ROW_TILES = 8
SPREAD = 0.2
CENTRE = 4.1
BLOCK = 68
F32 = jnp.float32
I32 = jnp.int32


def grid_iotas():
    row = lax.broadcasted_iota(I32, (ROWS, LANES), 0)
    lane = lax.broadcasted_iota(I32, (ROWS, LANES), 1)
    cell = row * LANES + lane
    i = (cell * 46604) >> 22
    j = cell - SIDE * i
    return row, lane, cell, i, j


def ahead(x, n):
    lane = lax.broadcasted_iota(I32, x.shape, 1)
    y = pltpu.roll(x, LANES - n, 1)
    return jnp.where(lane < LANES - n, y, pltpu.roll(y, ROWS - 1, 0))


def behind(x, n):
    lane = lax.broadcasted_iota(I32, x.shape, 1)
    y = pltpu.roll(x, n, 1)
    return jnp.where(lane >= n, y, pltpu.roll(y, 1, 0))


def take(x, index):
    pieces = []
    for first in range(0, x.shape[0], 8):
        part = index if index.shape[0] == 8 else index[first : first + 8]
        pieces.append(jnp.take_along_axis(x[first : first + 8], part, axis=1, mode="promise_in_bounds"))
    return pieces[0] if len(pieces) == 1 else jnp.concatenate(pieces, axis=0)


def lanes8():
    return lax.broadcasted_iota(I32, (8, LANES), 1)


def column_owner(lane):
    odd = lane & 1
    half = (lane - 89 * odd) >> 1
    return (37 * half) & 63


def lines_23(za, zb, depth_row):
    lane = lanes8()
    near = (SIDE * lane + depth_row) & 127
    far = (SIDE * lane + SIDE - 1 - depth_row) & 127
    wide = lax.broadcasted_iota(I32, za.shape, 1)
    first = wide < 64
    return (
        jnp.where(first, take(za, near), take(zb, near)),
        jnp.where(first, take(za, far), take(zb, far)),
    )


def spread_lines(side2, side3, side1):
    lane = lanes8()
    owner = column_owner(lane)
    later = (owner + 64) & 127
    even = (lax.broadcasted_iota(I32, side2.shape, 1) & 1) == 0
    wa = jnp.where(even, take(side2, owner), take(side3, owner))
    wb = jnp.where(even, take(side2, later), take(side3, later))
    return wa, wb, pltpu.roll(side1, 74, 1)


def scatter_masks():
    row, lane, cell, i, j = grid_iotas()
    column = (j == 0) | (j == SIDE - 1)
    return (
        column & (i < 64),
        column & (i >= 64) & (i < SIDE),
        cell < SIDE,
        i == SIDE - 1,
    )


def scatter_rows(masks, wa, wb, side0, w1):
    zero = jnp.zeros((ROWS, LANES), F32)
    out = jnp.where(masks[0], wa, zero) + jnp.where(masks[1], wb, zero)
    return out + jnp.where(masks[2], side0, zero) + jnp.where(masks[3], w1, zero)


def scatter_lines(masks, lines):
    wa, wb, w1 = spread_lines(
        jnp.broadcast_to(lines[2:3], (8, LANES)),
        jnp.broadcast_to(lines[3:4], (8, LANES)),
        jnp.broadcast_to(lines[1:2], (8, LANES)),
    )
    return scatter_rows(masks, wa[0:1], wb[0:1], lines[0:1], w1[0:1])


def row_line(ref, base, first_cell):
    row, off = divmod(first_cell, LANES)
    top = ref[pl.ds(base + row, 1), :]
    if off == 0:
        return top
    lane = lax.broadcasted_iota(I32, (1, LANES), 1)
    top = pltpu.roll(top, LANES - off, 1)
    if off + SIDE <= LANES:
        return top
    low = pltpu.roll(ref[pl.ds(base + row + 1, 1), :], LANES - off, 1)
    return jnp.where(lane < LANES - off, top, low)


def write_frames(field_ref, base, out_ref, first_row, za_ref, zb_ref, depths):
    field = field_ref[base : base + ROWS, :]
    row, lane, cell, i, j = grid_iotas()
    za_ref[0:8, :] = jnp.zeros((8, LANES), F32)
    zb_ref[0:8, :] = jnp.zeros((8, LANES), F32)
    for depth in range(depths):
        column = ((j == depth) | (j == SIDE - 1 - depth)) & (i < SIDE)
        za_ref[depth : depth + 1, :] = jnp.sum(
            jnp.where(column & (i < 64), field, 0.0)[0:48], axis=0, keepdims=True
        )
        zb_ref[depth : depth + 1, :] = jnp.sum(
            jnp.where(column & (i >= 64), field, 0.0)[40:ROWS], axis=0, keepdims=True
        )
        at = first_row + depth * 4
        out_ref[at : at + 1, :] = row_line(field_ref, base, depth * SIDE)
        out_ref[at + 1 : at + 2, :] = row_line(field_ref, base, (SIDE - 1 - depth) * SIDE)
    depth_row = lax.broadcasted_iota(I32, (8, LANES), 0) & 3
    side2, side3 = lines_23(za_ref[0:8, :], zb_ref[0:8, :], depth_row)
    for depth in range(depths):
        at = first_row + depth * 4
        out_ref[at + 2 : at + 3, :] = side2[depth : depth + 1]
        out_ref[at + 3 : at + 4, :] = side3[depth : depth + 1]


def level_rows(ref, level):
    whole = (CELLS // LANES // 8) * 8
    rows = CELLS // LANES
    window = ref[level, :, CELLS - LANES : CELLS]
    return jnp.concatenate(
        [
            ref[level, :, 0 : whole * LANES].reshape(whole, LANES),
            ref[level, :, whole * LANES : rows * LANES].reshape(rows - whole, LANES),
            pltpu.roll(window, CELLS - rows * LANES, 1),
        ],
        axis=0,
    )


def surface_rows(ref):
    whole = (CELLS // LANES // 8) * 8
    rows = CELLS // LANES
    window = ref[:, CELLS - LANES : CELLS]
    return jnp.concatenate(
        [
            ref[:, 0 : whole * LANES].reshape(whole, LANES),
            ref[:, whole * LANES : rows * LANES].reshape(rows - whole, LANES),
            pltpu.roll(window, CELLS - rows * LANES, 1),
        ],
        axis=0,
    )


def interior_reach(depth):
    row, lane, cell, i, j = grid_iotas()
    zero = jnp.zeros_like(depth)
    along = jnp.where(j < SIDE - 1, jnp.minimum(depth, ahead(depth, 1)), zero)
    across = jnp.where(cell < CELLS - SIDE, jnp.minimum(depth, ahead(depth, SIDE)), zero)
    return along, across


def interior_spread(x, along, across, level):
    zero = jnp.zeros_like(x)
    flux1 = jnp.where(along > level, ahead(x, 1) - x, zero)
    flux2 = jnp.where(across > level, ahead(x, SIDE) - x, zero)
    return (flux1 - behind(flux1, 1)) + (flux2 - behind(flux2, SIDE))


def depths_kernel(depth_ref, out_ref, dense_ref, z_ref):
    row, lane, cell, i, j = grid_iotas()
    dense_ref[...] = jnp.where(cell < CELLS, surface_rows(depth_ref).astype(F32), 0.0)
    write_frames(dense_ref, 0, out_ref, 0, z_ref.at[0], z_ref.at[1], 1)
    out_ref[4:8, :] = jnp.zeros((4, LANES), F32)


def columns_kernel(shifts, tiles, levels, me_ref, adj_ref, flag_ref, own_ref, *rest):
    met_refs = rest[: len(shifts)]
    k_hbm, s_hbm, t_hbm, depth_hbm, d_hbm, b_hbm = rest[len(shifts) : len(shifts) + 6]
    a_ref, q_ref, as_ref, blk_ref, dense_ref, reach_ref = rest[len(shifts) + 6 : len(shifts) + 12]
    k_ref, s_ref, t_ref, depth_ref, d_ref, b_ref, g_ref, z_ref, ts_ref, sems = rest[len(shifts) + 12 :]
    parts = 3
    third = levels // parts
    surface = [
        pltpu.make_async_copy(source, target, sems.at[number])
        for number, (source, target) in enumerate(((depth_hbm, depth_ref), (b_hbm, b_ref), (d_hbm, d_ref)))
    ]
    for copy in surface:
        copy.start()
    columns = []
    for part in range(parts):
        at = pl.ds(part * third, third if part < parts - 1 else levels - part * third)
        for number, (source, target) in enumerate(((k_hbm, k_ref), (s_hbm, s_ref))):
            columns.append(pltpu.make_async_copy(source.at[at], target.at[at], sems.at[3 + 2 * part + number]))
            columns[-1].start()
    tracer = pltpu.make_async_copy(t_hbm, t_ref, sems.at[3 + 2 * parts])
    tracer.start()
    me = me_ref[0]
    row, lane, cell, i, j = grid_iotas()
    inside = cell < CELLS
    for number, ref in enumerate((depth_ref, b_ref, d_ref)):
        surface[number].wait()
        place = (2, 0, 1)[number]
        rows = slice(place * ROWS, (place + 1) * ROWS)
        dense_ref[rows, :] = jnp.where(inside, surface_rows(ref).astype(F32), 0.0)
    depth = dense_ref[2 * ROWS : 3 * ROWS, :]
    along, across = interior_reach(depth)
    zero = jnp.zeros((ROWS, LANES), F32)

    def down(level, carry):
        link, below, va, vq = carry
        at = pl.ds(pl.multiple_of(level * ROWS, ROWS), ROWS)
        here = level.astype(F32)
        r = jnp.where(depth > here + 1.0, level_rows(k_ref, level), zero)
        wet = jnp.where(depth > here, 1.0, zero)
        upper = 1.0 + below
        inverse = 1.0 / (upper + r)
        ratio = r * inverse
        va = (level_rows(s_ref, level) + link * va) * inverse
        vq = (wet + link * vq) * inverse
        g_ref[at, :] = ratio
        a_ref[at, :] = va
        q_ref[at, :] = vq
        return r, upper * ratio, va, vq

    carry = (zero, zero, zero, zero)
    for part in range(parts):
        columns[2 * part].wait()
        columns[2 * part + 1].wait()
        last = (part + 1) * third if part < parts - 1 else levels
        carry = lax.fori_loop(part * third, last, down, carry, unroll=2)
    tracer.wait()
    column = ((j == 0) | (j == SIDE - 1)) & (i < SIDE)
    first = (column & (i < 64))[0:48]
    second = (column & (i >= 64))[40:ROWS]

    def up(step, carry):
        xa, xq, total, flux1, flux2 = carry
        level = levels - 1 - step
        here = level.astype(F32)
        at = pl.ds(pl.multiple_of(level * ROWS, ROWS), ROWS)
        ratio = g_ref[at, :]
        xa = a_ref[at, :] + ratio * xa
        xq = q_ref[at, :] + ratio * xq
        a_ref[at, :] = xa
        q_ref[at, :] = xq
        t = level_rows(t_ref, level)
        line = pl.ds(level, 1)
        for number, (x, out) in enumerate(((t, ts_ref), (xa, as_ref))):
            base = number * 4
            z_ref[base, line, :] = jnp.sum(jnp.where(first, x[0:48], 0.0), axis=0, keepdims=True)
            z_ref[base + 1, line, :] = jnp.sum(jnp.where(second, x[40:ROWS], 0.0), axis=0, keepdims=True)
            out[0, line, :] = x[0:1]
            z_ref[base + 2, line, :] = x[ROWS - 2 : ROWS - 1]
            z_ref[base + 3, line, :] = x[ROWS - 1 : ROWS]
        flux1 = flux1 + jnp.where(along > here, xq * (ahead(t, 1) - t), zero)
        flux2 = flux2 + jnp.where(across > here, xq * (ahead(t, SIDE) - t), zero)
        return xa, xq, total + xq * t, flux1, flux2

    xa, xq, total, flux1, flux2 = lax.fori_loop(0, levels, up, (zero,) * 5, unroll=2)
    level_scale = 1.0 / math.sqrt(levels)
    spread = (flux1 - behind(flux1, 1)) + (flux2 - behind(flux2, SIDE))
    dense_ref[3 * ROWS : 4 * ROWS, :] = jnp.where(inside, (total + SPREAD * spread) * level_scale, zero)
    spare = z_ref.shape[1] - levels
    for number, out in enumerate((ts_ref, as_ref)):
        base = number * 4
        for part in range(4):
            z_ref[base + part, levels:, :] = jnp.zeros((spare, LANES), F32)
        out[0, levels:, :] = jnp.zeros((spare, LANES), F32)
        side2, side3 = lines_23(z_ref[base], z_ref[base + 1], 0)
        out[2] = side2
        out[3] = side3
        low, high = z_ref[base + 2], z_ref[base + 3]
        wide = lax.broadcasted_iota(I32, low.shape, 1)
        out[1] = jnp.where(wide < 54, pltpu.roll(low, 54, 1), pltpu.roll(high, 54, 1))
    level = lax.broadcasted_iota(I32, (32, LANES), 0).astype(F32)
    reach_ref[4:8, :] = jnp.zeros((4, LANES), F32)
    for side in range(4):
        neighbour = adj_ref[0, side]
        flag = flag_ref[0, side]
        met = met_refs[0][pl.ds(flag >> 1, 1), :]
        for number in range(1, len(shifts)):
            hit = neighbour == lax.rem(me + tiles - shifts[number], tiles)
            met = jnp.where(hit, met_refs[number][pl.ds(flag >> 1, 1), :], met)
        met = take(jnp.broadcast_to(met, (8, LANES)), seam_index(flag))[0:1]
        reach = jnp.where(neighbour >= 0, jnp.minimum(met, own_ref[side : side + 1, :]), 0.0)
        reach_ref[side : side + 1, :] = reach
        shared = jnp.sum(jnp.where(reach > level, ts_ref[side], 0.0), axis=0, keepdims=True)
        blk_ref[60 + side : 61 + side, :] = (SPREAD * level_scale) * shared
        table = jnp.zeros((1, LANES), F32)
        where = lax.broadcasted_iota(I32, (1, LANES), 1)
        for number, of in enumerate((side, 2 if side < 2 else 0, 3 if side < 2 else 1)):
            table = jnp.where(where == 2 * number, adj_ref[0, of].astype(F32), table)
            table = jnp.where(where == 2 * number + 1, flag_ref[0, of].astype(F32), table)
        blk_ref[64 + side : 65 + side, :] = table
    g_ref[0:ROWS, :] = jnp.minimum(depth, 1.0)
    za_ref, zb_ref = z_ref.at[0], z_ref.at[1]
    write_frames(dense_ref, 0, blk_ref, 0, za_ref, zb_ref, 4)
    write_frames(dense_ref, 3 * ROWS, blk_ref, 16, za_ref, zb_ref, 4)
    write_frames(g_ref, 0, blk_ref, 32, za_ref, zb_ref, 4)
    write_frames(dense_ref, ROWS, blk_ref, 48, za_ref, zb_ref, 3)


def pick(refs, shifts, tiles, me, neighbour, side_met):
    value = refs[0][side_met]
    for number in range(1, len(shifts)):
        hit = neighbour == lax.rem(me + tiles - shifts[number], tiles)
        value = jnp.where(hit, refs[number][side_met], value)
    return value


def seam_index(flag):
    lane = lanes8()
    return jnp.where((flag & 1) == 1, SIDE - 1 - lane, lane) & 127


def block_rows(refs, places, first, size):
    for ref, held in zip(refs, places):
        for number, position in enumerate(held):
            at = number * BLOCK + first
            yield position, ref[at : at + size, :]


def gather_lines(p, lines):
    high = lines.astype(jnp.bfloat16)
    rest = lines - high.astype(F32)
    middle = rest.astype(jnp.bfloat16)
    low = (rest - middle.astype(F32)).astype(jnp.bfloat16)
    out = jnp.dot(p, high, preferred_element_type=F32)
    out = out + jnp.dot(p, middle, preferred_element_type=F32)
    return out + jnp.dot(p, low, preferred_element_type=F32)


def ends(x, low, high, low_parity, high_parity, depth):
    lane = lax.broadcasted_iota(I32, x.shape, 1)
    low_end = take(low, jnp.where(low_parity == 1, SIDE - 1 - depth, depth))
    high_end = take(high, jnp.where(high_parity == 1, SIDE - 1 - depth, depth))
    return (
        jnp.where(lane == 0, low_end, pltpu.roll(x, 1, 1)),
        jnp.where(lane == SIDE - 1, high_end, pltpu.roll(x, LANES - 1, 1)),
    )


def krylov_kernel(places, lines, me_ref, dense_ref, *rest):
    refs = rest[: len(places)]
    va_ref, vb_ref, line_ref, gram_ref = rest[len(places) : len(places) + 4]
    p_ref, index_ref, frame_ref, work_ref, wet_ref, d_ref, x_ref = rest[len(places) + 4 :]
    me = me_ref[0]

    def collect(out, first):
        for position, rows in block_rows(refs, places, first, 4):
            out[position * 4 : position * 4 + 4, :] = rows

    collect(work_ref.at[0], 60)
    collect(work_ref.at[1], 64)
    for depth in range(4):
        collect(x_ref.at[depth], 4 * depth)
        collect(x_ref.at[4 + depth], 16 + 4 * depth)
        collect(wet_ref.at[depth], 32 + 4 * depth)
        if depth < 3:
            collect(d_ref.at[depth], 48 + 4 * depth)
    lane = lax.broadcasted_iota(I32, (lines, LANES), 1)
    line = lax.broadcasted_iota(I32, (lines, LANES), 0)
    odd = line & 1
    column = lax.broadcasted_iota(I32, (lines, lines), 1)
    line_of = lax.broadcasted_iota(I32, (lines, lines), 0)
    for number in range(3):
        tile = work_ref[1, :, 2 * number : 2 * number + 1].astype(I32)
        flag = work_ref[1, :, 2 * number + 1 : 2 * number + 2].astype(I32)
        at = jnp.where(tile >= 0, 4 * (tile ^ me) + (flag >> 1), -1)
        p = jnp.where(jnp.broadcast_to(at, (lines, lines)) == column, 1.0, 0.0)
        p_ref[number * lines : (number + 1) * lines, :] = p.astype(jnp.bfloat16)
        parity = jnp.broadcast_to(flag & 1, (lines, LANES))
        if number == 0:
            index_ref[0:lines, :] = jnp.where(parity == 1, SIDE - 1 - lane, lane) & 127
        else:
            index_ref[number * lines : (number + 1) * lines, :] = parity ^ odd
    first_half = (line_of & 2) == 0
    for number in range(2):
        at = (line_of & -4) + jnp.where(first_half, 2, 0) + number
        p = jnp.where(at == column, 1.0, 0.0)
        p_ref[(3 + number) * lines : (4 + number) * lines, :] = p.astype(jnp.bfloat16)
    p = p_ref[0 : 3 * lines, :]
    facing_at = index_ref[0:lines, :]
    low_parity = index_ref[lines : 2 * lines, :]
    high_parity = index_ref[2 * lines : 3 * lines, :]
    wet = [wet_ref[depth] for depth in range(4)]
    met = gather_lines(p, wet[0])
    facing = take(met[0:lines], facing_at)
    for depth in range(3):
        low, high = ends(
            wet[depth], met[lines : 2 * lines], met[2 * lines : 3 * lines], low_parity, high_parity, depth
        )
        masks = [
            wet[depth] * (facing if depth == 0 else wet[depth - 1]),
            wet[depth] * wet[depth + 1],
            wet[depth] * low,
            wet[depth] * high,
        ]
        frame_ref[depth, 0] = d_ref[depth] + ((masks[0] + masks[1]) + (masks[2] + masks[3]))
        for number in range(4):
            frame_ref[depth, 1 + number] = masks[number]
        if depth == 0:
            seam = masks[0][0:8]
    shared = work_ref[0]
    gain = take(gather_lines(p_ref[0:lines, :], shared), facing_at) - shared
    moved = gather_lines(p_ref[3 * lines : 5 * lines, :], gain)
    zero_line = jnp.zeros((lines, LANES), F32)
    for depth in range(4):
        end = jnp.where(odd == 1, SIDE - 1 - depth, depth)
        extra = jnp.where(lane == 0, take(moved[0:lines], end), zero_line)
        extra = extra + jnp.where(lane == SIDE - 1, take(moved[lines : 2 * lines], end), zero_line)
        if depth == 0:
            extra = extra + gain
        x_ref[4 + depth] = x_ref[4 + depth] + extra
    surface = jnp.minimum(dense_ref[2 * ROWS : 3 * ROWS, :], 1.0)
    along, across = interior_reach(surface)
    degree = (along + behind(along, 1)) + (across + behind(across, SIDE))
    masks = scatter_masks()
    diagonal = dense_ref[ROWS : 2 * ROWS, :] + (degree + scatter_lines(masks, seam))
    scale = 2.0 / CENTRE
    row, lane, cell, i, j = grid_iotas()
    inside = cell < CELLS
    forcing = dense_ref[3 * ROWS : 4 * ROWS, :] + scatter_lines(masks, gain[0:8])
    va_ref[0] = forcing
    vb_ref[0] = dense_ref[0:ROWS, :]
    frames = [[[x_ref[4 * solve + depth] for depth in range(4)]] for solve in range(2)]
    own = [[dense_ref[0:ROWS, :]], [forcing]]
    for step in range(ITERS):
        for solve in range(2):
            x = frames[solve][-1]
            met = gather_lines(p, x[0])
            facing = take(met[0:lines], facing_at)
            if solve == 0:
                line_ref[step] = facing[0:8]
            mine = own[solve][-1]
            flow = (along * ahead(mine, 1) + behind(along * mine, 1)) + (
                across * ahead(mine, SIDE) + behind(across * mine, SIDE)
            )
            image = diagonal * mine - flow - scatter_lines(masks, seam * facing[0:8])
            image = jnp.where(inside, scale * image - 2.0 * mine, 0.0)
            own[solve].append(0.5 * image if step == 0 else image - own[solve][-2])
            following = []
            for depth in range(ITERS - 1 - step):
                low, high = ends(
                    x[depth],
                    met[lines : 2 * lines],
                    met[2 * lines : 3 * lines],
                    low_parity,
                    high_parity,
                    depth,
                )
                before = facing if depth == 0 else x[depth - 1]
                flow = (frame_ref[depth, 1] * before + frame_ref[depth, 2] * x[depth + 1]) + (
                    frame_ref[depth, 3] * low + frame_ref[depth, 4] * high
                )
                image = scale * (frame_ref[depth, 0] * x[depth] - flow) - 2.0 * x[depth]
                following.append(0.5 * image if step == 0 else image - frames[solve][-2][depth])
            frames[solve].append(following)
            if step < ITERS - 1:
                (vb_ref if solve == 0 else va_ref)[step + 1] = own[solve][-1]
    for solve in range(2):
        at = 16 * solve
        for first in range(ITERS + 1):
            for second in range(first + 1):
                gram_ref[at : at + 1, :] = jnp.sum(own[solve][first] * own[solve][second], axis=0, keepdims=True)
                at += 1
        gram_ref[at : at + 1, :] = jnp.zeros((1, LANES), F32)


def image_of(p):
    out = [None] * (len(p) + 1)

    def add(at, value):
        out[at] = value if out[at] is None else out[at] + value

    for at, value in enumerate(p):
        add(at, CENTRE * value)
        if at == 0:
            add(1, CENTRE * value)
        else:
            add(at + 1, 0.5 * CENTRE * value)
            add(at - 1, 0.5 * CENTRE * value)
    return out


def form(left, gram, right):
    total = None
    for first, x in enumerate(left):
        inner = None
        for second, y in enumerate(right):
            term = gram[max(first, second)][min(first, second)] * y
            inner = term if inner is None else inner + term
        total = x * inner if total is None else total + x * inner
    return total


def total_gram(refs, sum_ref):
    total = refs[0][...]
    for ref in refs[1:]:
        total = total + ref[...]
    sum_ref[...] = jnp.broadcast_to(jnp.sum(total, axis=1, keepdims=True), sum_ref.shape)


def coefficients(sum_ref, at):
    gram = []
    for first in range(ITERS + 1):
        gram.append([sum_ref[at + second : at + second + 1, :] for second in range(first + 1)])
        at += first + 1
    one = jnp.ones((1, LANES), F32)
    x = []
    r = [one]
    p = [one]
    rr = gram[0][0]
    for step in range(ITERS):
        image = image_of(p)
        curve = form(p, gram, image)
        alpha = jnp.where(curve > 0.0, rr / curve, 0.0)
        x = [x[n] + alpha * p[n] if n < len(x) else alpha * p[n] for n in range(len(p))]
        r = [r[n] - alpha * image[n] if n < len(r) else -alpha * image[n] for n in range(len(image))]
        if step < ITERS - 1:
            new = jnp.maximum(form(r, gram, r), 0.0)
            beta = jnp.where(rr > 0.0, new / rr, 0.0)
            p = [r[n] + beta * p[n] if n < len(p) else r[n] for n in range(len(r))]
            rr = new
    return x


def store_rows(ref, rows):
    last = CELLS // LANES
    ref[:, 0 : last * LANES] = rows[0:last].reshape(1, last * LANES)
    ref[:, last * LANES : CELLS] = rows[last : last + 1, 0 : CELLS - last * LANES]


def combine(x, v_ref):
    out = x[0] * v_ref[0]
    for number in range(1, ITERS):
        out = out + x[number] * v_ref[number]
    return out


def gradient_kernel(shifts, tiles, levels, grams, me_ref, adj_ref, flag_ref, *rest):
    gram_refs = rest[:grams]
    rest = rest[grams:]
    dense_ref, va_ref, v_ref, line_ref, reach_ref, a_ref, q_ref, as_ref = rest[:8]
    refs = rest[8 : 8 + len(shifts)]
    height_ref, out_ref, gram_ref, sum_ref, w_ref, h_ref = rest[8 + len(shifts) :]
    me = me_ref[0]
    total_gram(gram_refs, gram_ref)
    store_rows(height_ref, combine(coefficients(gram_ref, 16), va_ref))
    x = coefficients(gram_ref, 0)
    level_scale = 1.0 / math.sqrt(levels)
    adjoint = combine(x, v_ref) * level_scale
    met_line = x[0] * line_ref[0]
    depth = dense_ref[2 * ROWS : 3 * ROWS, :]
    along, across = interior_reach(depth)
    sum_ref[0:8, :] = met_line + x[1] * line_ref[1] + x[2] * line_ref[2] + x[3] * line_ref[3]
    h_ref[0:ROWS, :] = adjoint
    w_ref[4, 8:9, :] = h_ref[0:1, :]
    w_ref[4, 9:10, :] = row_line(h_ref, 0, (SIDE - 1) * SIDE)
    row, lane, cell, i, j = grid_iotas()
    column = (j == 0) | (j == SIDE - 1)
    zero = jnp.zeros((ROWS, LANES), F32)
    za = jnp.sum(jnp.where(column & (i < 64), adjoint, zero), axis=0, keepdims=True)
    zb = jnp.sum(jnp.where(column & (i >= 64), adjoint, zero), axis=0, keepdims=True)
    side2, side3 = lines_23(jnp.broadcast_to(za, (8, LANES)), jnp.broadcast_to(zb, (8, LANES)), 0)
    w_ref[4, 10:11, :] = side2[0:1]
    w_ref[4, 11:12, :] = side3[0:1]
    level = lax.broadcasted_iota(I32, (32, LANES), 0).astype(F32)
    fluxes = []
    for side in range(4):
        neighbour = adj_ref[0, side]
        flag = flag_ref[0, side]
        index = seam_index(flag)
        other = take(pick(refs, shifts, tiles, me, neighbour, flag >> 1), index)
        other = other + sum_ref[side : side + 1, :] * level_scale
        own = as_ref[side] + w_ref[4, 8 + side : 9 + side, :]
        fluxes.append(jnp.where(reach_ref[side : side + 1, :] > level, other - own, 0.0))
    wa, wb, w1 = spread_lines(fluxes[2], fluxes[3], fluxes[1])
    w_ref[0] = wa
    w_ref[1] = wb
    w_ref[2] = fluxes[0]
    w_ref[3] = w1
    masks = scatter_masks()

    def per_level(number, carry):
        at = pl.ds(pl.multiple_of(number * ROWS, ROWS), ROWS)
        here = pl.ds(number, 1)
        h = a_ref[at, :] + adjoint * q_ref[at, :]
        spread = interior_spread(h, along, across, number.astype(F32))
        spread = spread + scatter_rows(
            masks, w_ref[0, here, :], w_ref[1, here, :], w_ref[2, here, :], w_ref[3, here, :]
        )
        store_rows(out_ref.at[number], h + SPREAD * spread)
        return carry

    lax.fori_loop(0, levels, per_level, 0, unroll=2)


def rounds(tiles):
    out = []
    stride = tiles
    while stride > 1:
        radix = 4 if stride >= 16 else 2
        stride //= radix
        out.append((stride, radix))
    return out


def swap(x, tiles, offset):
    return lax.ppermute(x, "tile", [(t, t ^ offset) for t in range(tiles)])


def gather_tiles(block, tiles):
    held = [block]
    places = [(0,)]
    for stride, radix in rounds(tiles):
        whole = held[0] if len(held) == 1 else jnp.concatenate(held, axis=0)
        covered = tuple(n for place in places for n in place)
        for number in range(1, radix):
            held.append(swap(whole, tiles, number * stride))
            places.append(tuple(n ^ (number * stride) for n in covered))
    return held, tuple(places)


def sum_tiles(block, tiles):
    held = [block]
    for stride, radix in rounds(tiles):
        whole = functools.reduce(jnp.add, held)
        held = [whole] + [swap(whole, tiles, number * stride) for number in range(1, radix)]
    return held


def shards(thermal, stirring, depth, adjacent, flags, main_entry, sensitivity, elevation, tiles):
    levels = thermal.shape[1]
    me = lax.axis_index("tile").astype(I32).reshape(1)
    smem = pl.BlockSpec(memory_space=pltpu.SMEM)
    vmem = pl.BlockSpec(memory_space=pltpu.VMEM)
    params = pltpu.CompilerParams(vmem_limit_bytes=48 * 1024 * 1024)

    def shape(*dims):
        return jax.ShapeDtypeStruct(dims, F32)

    hbm = pl.BlockSpec(memory_space=pltpu.HBM)

    def call(kernel, outs, scratch, scalars, arrays, name, flops=1e6, traffic=1e6, far=()):
        return pl.pallas_call(
            kernel,
            out_shape=outs,
            in_specs=[smem] * len(scalars) + [vmem] * len(arrays) + [hbm] * len(far),
            out_specs=jax.tree.map(lambda _: vmem, outs),
            scratch_shapes=scratch,
            compiler_params=params,
            cost_estimate=pl.CostEstimate(flops=int(flops), bytes_accessed=int(traffic), transcendentals=0),
            name=name,
        )(*scalars, *arrays, *far)

    offsets = []
    for offset in (1, -1, ROW_TILES, -ROW_TILES, tiles // 2):
        if offset % tiles not in [o % tiles for o in offsets] and offset % tiles:
            offsets.append(offset)
    shifts = tuple(offset % tiles for offset in offsets)

    def to_neighbours(x):
        out = []
        for offset in offsets:
            pairs = [(t, t + offset) for t in range(tiles) if 0 <= t + offset < tiles]
            if 2 * offset == tiles or 2 * offset == -tiles:
                pairs = [(t, (t + offset) % tiles) for t in range(tiles)]
            out.append(lax.ppermute(x, "tile", pairs))
        return out

    def by_level(x):
        return jnp.transpose(x, (1, 0, 2))

    own_depths = call(
        depths_kernel,
        shape(8, LANES),
        [pltpu.VMEM((ROWS, LANES), F32), pltpu.VMEM((2, 8, LANES), F32)],
        (),
        (depth,),
        "depths",
    )
    depths_met = to_neighbours(own_depths)
    far = pltpu.VMEM((levels, 1, CELLS), F32)
    solved, weight, strips, block, dense, reach = call(
        functools.partial(columns_kernel, shifts, tiles, levels),
        (
            shape(levels * ROWS, LANES),
            shape(levels * ROWS, LANES),
            shape(4, 32, LANES),
            shape(BLOCK, LANES),
            shape(4 * ROWS, LANES),
            shape(8, LANES),
        ),
        [
            far,
            far,
            far,
            pltpu.VMEM((1, CELLS), I32),
            pltpu.VMEM((1, CELLS), F32),
            pltpu.VMEM((1, CELLS), F32),
            pltpu.VMEM((levels * ROWS, LANES), F32),
            pltpu.VMEM((8, 32, LANES), F32),
            pltpu.VMEM((4, 32, LANES), F32),
            pltpu.SemaphoreType.DMA((10,)),
        ],
        (me, adjacent, flags),
        (own_depths, *depths_met),
        "columns",
        2e7,
        8e6,
        (by_level(stirring), by_level(sensitivity), by_level(thermal), depth, main_entry, elevation),
    )
    blocks, places = gather_tiles(block, tiles)
    strips_met = to_neighbours(strips)
    lines = 4 * tiles
    frame = pltpu.VMEM((4, lines, LANES), F32)
    basis = shape(ITERS, ROWS, LANES)
    basis_a, basis_b, lines_b, gram = call(
        functools.partial(krylov_kernel, places, lines),
        (basis, basis, shape(ITERS, 8, LANES), shape(32, LANES)),
        [
            pltpu.VMEM((5 * lines, lines), jnp.bfloat16),
            pltpu.VMEM((3 * lines, LANES), I32),
            pltpu.VMEM((3, 5, lines, LANES), F32),
            pltpu.VMEM((2, lines, LANES), F32),
            frame,
            frame,
            pltpu.VMEM((8, lines, LANES), F32),
        ],
        (me,),
        (dense, *blocks),
        "krylov",
    )
    grams = sum_tiles(gram, tiles)
    height, gradient = call(
        functools.partial(gradient_kernel, shifts, tiles, levels, len(grams)),
        (jax.ShapeDtypeStruct(elevation.shape, F32), shape(levels, 1, CELLS)),
        [
            pltpu.VMEM((32, LANES), F32),
            pltpu.VMEM((16, LANES), F32),
            pltpu.VMEM((5, 32, LANES), F32),
            pltpu.VMEM((ROWS, LANES), F32),
        ],
        (me, adjacent, flags),
        (
            *grams,
            dense,
            basis_a,
            basis_b,
            lines_b,
            reach,
            solved,
            weight,
            strips,
            *strips_met,
        ),
        "gradient",
        1e7,
        4e6,
    )
    gradient = by_level(gradient)
    return height, gradient


def solution(mesh):
    placed = (
        P(("ens", "tile"), None, None),
        P("tile", None, None),
        P("tile", None),
        P("tile", None),
        P("tile", None),
        P("tile", None),
        P(("ens", "tile"), None, None),
        P(("ens", "tile"), None),
    )
    return jax.shard_map(
        functools.partial(shards, tiles=mesh.shape["tile"]),
        mesh=mesh,
        in_specs=placed,
        out_specs=(P(("ens", "tile"), None), P(("ens", "tile"), None, None)),
        check_vma=False,
    )
```

```python
import functools
import math

import jax
import jax.numpy as jnp
from jax import lax
from jax.experimental import pallas as pl
from jax.experimental.pallas import tpu as pltpu
from jax.sharding import PartitionSpec as P

SIDE = 90
CELLS = SIDE * SIDE
ROWS = 64
LANES = 128
ITERS = 4
ROW_TILES = 8
SPREAD = 0.2
CENTRE = 4.1
BLOCK = 68
F32 = jnp.float32
I32 = jnp.int32


def grid_iotas():
    row = lax.broadcasted_iota(I32, (ROWS, LANES), 0)
    lane = lax.broadcasted_iota(I32, (ROWS, LANES), 1)
    cell = row * LANES + lane
    i = (cell * 46604) >> 22
    j = cell - SIDE * i
    return row, lane, cell, i, j


def ahead(x, n):
    lane = lax.broadcasted_iota(I32, x.shape, 1)
    y = pltpu.roll(x, LANES - n, 1)
    return jnp.where(lane < LANES - n, y, pltpu.roll(y, ROWS - 1, 0))


def behind(x, n):
    lane = lax.broadcasted_iota(I32, x.shape, 1)
    y = pltpu.roll(x, n, 1)
    return jnp.where(lane >= n, y, pltpu.roll(y, 1, 0))


def take(x, index):
    pieces = []
    for first in range(0, x.shape[0], 8):
        part = index if index.shape[0] == 8 else index[first : first + 8]
        pieces.append(jnp.take_along_axis(x[first : first + 8], part, axis=1, mode="promise_in_bounds"))
    return pieces[0] if len(pieces) == 1 else jnp.concatenate(pieces, axis=0)


def lanes8():
    return lax.broadcasted_iota(I32, (8, LANES), 1)


def column_owner(lane):
    odd = lane & 1
    half = (lane - 89 * odd) >> 1
    return (37 * half) & 63


def lines_23(za, zb, depth_row):
    lane = lanes8()
    near = (SIDE * lane + depth_row) & 127
    far = (SIDE * lane + SIDE - 1 - depth_row) & 127
    wide = lax.broadcasted_iota(I32, za.shape, 1)
    first = wide < 64
    return (
        jnp.where(first, take(za, near), take(zb, near)),
        jnp.where(first, take(za, far), take(zb, far)),
    )


def spread_lines(side2, side3, side1):
    lane = lanes8()
    owner = column_owner(lane)
    later = (owner + 64) & 127
    even = (lax.broadcasted_iota(I32, side2.shape, 1) & 1) == 0
    wa = jnp.where(even, take(side2, owner), take(side3, owner))
    wb = jnp.where(even, take(side2, later), take(side3, later))
    return wa, wb, pltpu.roll(side1, 74, 1)


def scatter_masks():
    row, lane, cell, i, j = grid_iotas()
    column = (j == 0) | (j == SIDE - 1)
    return (
        column & (i < 64),
        column & (i >= 64) & (i < SIDE),
        cell < SIDE,
        i == SIDE - 1,
    )


def scatter_rows(masks, wa, wb, side0, w1):
    zero = jnp.zeros((ROWS, LANES), F32)
    out = jnp.where(masks[0], wa, zero) + jnp.where(masks[1], wb, zero)
    return out + jnp.where(masks[2], side0, zero) + jnp.where(masks[3], w1, zero)


def scatter_lines(masks, lines):
    wa, wb, w1 = spread_lines(
        jnp.broadcast_to(lines[2:3], (8, LANES)),
        jnp.broadcast_to(lines[3:4], (8, LANES)),
        jnp.broadcast_to(lines[1:2], (8, LANES)),
    )
    return scatter_rows(masks, wa[0:1], wb[0:1], lines[0:1], w1[0:1])


def row_line(ref, base, first_cell):
    row, off = divmod(first_cell, LANES)
    top = ref[pl.ds(base + row, 1), :]
    if off == 0:
        return top
    lane = lax.broadcasted_iota(I32, (1, LANES), 1)
    top = pltpu.roll(top, LANES - off, 1)
    if off + SIDE <= LANES:
        return top
    low = pltpu.roll(ref[pl.ds(base + row + 1, 1), :], LANES - off, 1)
    return jnp.where(lane < LANES - off, top, low)


def write_frames(field_ref, base, out_ref, first_row, za_ref, zb_ref, depths):
    field = field_ref[base : base + ROWS, :]
    row, lane, cell, i, j = grid_iotas()
    za_ref[0:8, :] = jnp.zeros((8, LANES), F32)
    zb_ref[0:8, :] = jnp.zeros((8, LANES), F32)
    for depth in range(depths):
        column = ((j == depth) | (j == SIDE - 1 - depth)) & (i < SIDE)
        za_ref[depth : depth + 1, :] = jnp.sum(
            jnp.where(column & (i < 64), field, 0.0)[0:48], axis=0, keepdims=True
        )
        zb_ref[depth : depth + 1, :] = jnp.sum(
            jnp.where(column & (i >= 64), field, 0.0)[40:ROWS], axis=0, keepdims=True
        )
        at = first_row + depth * 4
        out_ref[at : at + 1, :] = row_line(field_ref, base, depth * SIDE)
        out_ref[at + 1 : at + 2, :] = row_line(field_ref, base, (SIDE - 1 - depth) * SIDE)
    depth_row = lax.broadcasted_iota(I32, (8, LANES), 0) & 3
    side2, side3 = lines_23(za_ref[0:8, :], zb_ref[0:8, :], depth_row)
    for depth in range(depths):
        at = first_row + depth * 4
        out_ref[at + 2 : at + 3, :] = side2[depth : depth + 1]
        out_ref[at + 3 : at + 4, :] = side3[depth : depth + 1]


def level_rows(ref, level):
    whole = (CELLS // LANES // 8) * 8
    rows = CELLS // LANES
    window = ref[level, :, CELLS - LANES : CELLS]
    return jnp.concatenate(
        [
            ref[level, :, 0 : whole * LANES].reshape(whole, LANES),
            ref[level, :, whole * LANES : rows * LANES].reshape(rows - whole, LANES),
            pltpu.roll(window, CELLS - rows * LANES, 1),
        ],
        axis=0,
    )


def surface_rows(ref):
    whole = (CELLS // LANES // 8) * 8
    rows = CELLS // LANES
    window = ref[:, CELLS - LANES : CELLS]
    return jnp.concatenate(
        [
            ref[:, 0 : whole * LANES].reshape(whole, LANES),
            ref[:, whole * LANES : rows * LANES].reshape(rows - whole, LANES),
            pltpu.roll(window, CELLS - rows * LANES, 1),
        ],
        axis=0,
    )


def interior_reach(depth):
    row, lane, cell, i, j = grid_iotas()
    zero = jnp.zeros_like(depth)
    along = jnp.where(j < SIDE - 1, jnp.minimum(depth, ahead(depth, 1)), zero)
    across = jnp.where(cell < CELLS - SIDE, jnp.minimum(depth, ahead(depth, SIDE)), zero)
    return along, across


def interior_spread(x, along, across, level):
    zero = jnp.zeros_like(x)
    flux1 = jnp.where(along > level, ahead(x, 1) - x, zero)
    flux2 = jnp.where(across > level, ahead(x, SIDE) - x, zero)
    return (flux1 - behind(flux1, 1)) + (flux2 - behind(flux2, SIDE))


def depths_kernel(depth_ref, out_ref, dense_ref, z_ref):
    row, lane, cell, i, j = grid_iotas()
    dense_ref[...] = jnp.where(cell < CELLS, surface_rows(depth_ref).astype(F32), 0.0)
    write_frames(dense_ref, 0, out_ref, 0, z_ref.at[0], z_ref.at[1], 1)
    out_ref[4:8, :] = jnp.zeros((4, LANES), F32)


def columns_kernel(shifts, tiles, levels, me_ref, adj_ref, flag_ref, own_ref, *rest):
    met_refs = rest[: len(shifts)]
    k_hbm, s_hbm, t_hbm, depth_hbm, d_hbm, b_hbm = rest[len(shifts) : len(shifts) + 6]
    a_ref, q_ref, as_ref, blk_ref, dense_ref, reach_ref = rest[len(shifts) + 6 : len(shifts) + 12]
    k_ref, s_ref, t_ref, depth_ref, d_ref, b_ref, g_ref, z_ref, ts_ref, sems = rest[len(shifts) + 12 :]
    parts = 3
    third = levels // parts
    surface = [
        pltpu.make_async_copy(source, target, sems.at[number])
        for number, (source, target) in enumerate(((depth_hbm, depth_ref), (b_hbm, b_ref), (d_hbm, d_ref)))
    ]
    for copy in surface:
        copy.start()
    columns = []
    for part in range(parts):
        at = pl.ds(part * third, third if part < parts - 1 else levels - part * third)
        for number, (source, target) in enumerate(((k_hbm, k_ref), (s_hbm, s_ref))):
            columns.append(pltpu.make_async_copy(source.at[at], target.at[at], sems.at[3 + 2 * part + number]))
            columns[-1].start()
    tracer = pltpu.make_async_copy(t_hbm, t_ref, sems.at[3 + 2 * parts])
    tracer.start()
    me = me_ref[0]
    row, lane, cell, i, j = grid_iotas()
    inside = cell < CELLS
    for number, ref in enumerate((depth_ref, b_ref, d_ref)):
        surface[number].wait()
        place = (2, 0, 1)[number]
        rows = slice(place * ROWS, (place + 1) * ROWS)
        dense_ref[rows, :] = jnp.where(inside, surface_rows(ref).astype(F32), 0.0)
    depth = dense_ref[2 * ROWS : 3 * ROWS, :]
    along, across = interior_reach(depth)
    zero = jnp.zeros((ROWS, LANES), F32)

    def down(level, carry):
        link, below, va, vq = carry
        at = pl.ds(pl.multiple_of(level * ROWS, ROWS), ROWS)
        here = level.astype(F32)
        r = jnp.where(depth > here + 1.0, level_rows(k_ref, level), zero)
        wet = jnp.where(depth > here, 1.0, zero)
        upper = 1.0 + below
        inverse = 1.0 / (upper + r)
        ratio = r * inverse
        va = (level_rows(s_ref, level) + link * va) * inverse
        vq = (wet + link * vq) * inverse
        g_ref[at, :] = ratio
        a_ref[at, :] = va
        q_ref[at, :] = vq
        return r, upper * ratio, va, vq

    carry = (zero, zero, zero, zero)
    for part in range(parts):
        columns[2 * part].wait()
        columns[2 * part + 1].wait()
        last = (part + 1) * third if part < parts - 1 else levels
        carry = lax.fori_loop(part * third, last, down, carry, unroll=2)
    tracer.wait()
    column = ((j == 0) | (j == SIDE - 1)) & (i < SIDE)
    first = (column & (i < 64))[0:48]
    second = (column & (i >= 64))[40:ROWS]

    def up(step, carry):
        xa, xq, total, flux1, flux2 = carry
        level = levels - 1 - step
        here = level.astype(F32)
        at = pl.ds(pl.multiple_of(level * ROWS, ROWS), ROWS)
        ratio = g_ref[at, :]
        xa = a_ref[at, :] + ratio * xa
        xq = q_ref[at, :] + ratio * xq
        a_ref[at, :] = xa
        q_ref[at, :] = xq
        t = level_rows(t_ref, level)
        line = pl.ds(level, 1)
        for number, (x, out) in enumerate(((t, ts_ref), (xa, as_ref))):
            base = number * 4
            z_ref[base, line, :] = jnp.sum(jnp.where(first, x[0:48], 0.0), axis=0, keepdims=True)
            z_ref[base + 1, line, :] = jnp.sum(jnp.where(second, x[40:ROWS], 0.0), axis=0, keepdims=True)
            out[0, line, :] = x[0:1]
            z_ref[base + 2, line, :] = x[ROWS - 2 : ROWS - 1]
            z_ref[base + 3, line, :] = x[ROWS - 1 : ROWS]
        flux1 = flux1 + jnp.where(along > here, xq * (ahead(t, 1) - t), zero)
        flux2 = flux2 + jnp.where(across > here, xq * (ahead(t, SIDE) - t), zero)
        return xa, xq, total + xq * t, flux1, flux2

    xa, xq, total, flux1, flux2 = lax.fori_loop(0, levels, up, (zero,) * 5, unroll=2)
    level_scale = 1.0 / math.sqrt(levels)
    spread = (flux1 - behind(flux1, 1)) + (flux2 - behind(flux2, SIDE))
    dense_ref[3 * ROWS : 4 * ROWS, :] = jnp.where(inside, (total + SPREAD * spread) * level_scale, zero)
    spare = z_ref.shape[1] - levels
    for number, out in enumerate((ts_ref, as_ref)):
        base = number * 4
        for part in range(4):
            z_ref[base + part, levels:, :] = jnp.zeros((spare, LANES), F32)
        out[0, levels:, :] = jnp.zeros((spare, LANES), F32)
        side2, side3 = lines_23(z_ref[base], z_ref[base + 1], 0)
        out[2] = side2
        out[3] = side3
        low, high = z_ref[base + 2], z_ref[base + 3]
        wide = lax.broadcasted_iota(I32, low.shape, 1)
        out[1] = jnp.where(wide < 54, pltpu.roll(low, 54, 1), pltpu.roll(high, 54, 1))
    level = lax.broadcasted_iota(I32, (32, LANES), 0).astype(F32)
    reach_ref[4:8, :] = jnp.zeros((4, LANES), F32)
    for side in range(4):
        neighbour = adj_ref[0, side]
        flag = flag_ref[0, side]
        met = met_refs[0][pl.ds(flag >> 1, 1), :]
        for number in range(1, len(shifts)):
            hit = neighbour == lax.rem(me + tiles - shifts[number], tiles)
            met = jnp.where(hit, met_refs[number][pl.ds(flag >> 1, 1), :], met)
        met = take(jnp.broadcast_to(met, (8, LANES)), seam_index(flag))[0:1]
        reach = jnp.where(neighbour >= 0, jnp.minimum(met, own_ref[side : side + 1, :]), 0.0)
        reach_ref[side : side + 1, :] = reach
        shared = jnp.sum(jnp.where(reach > level, ts_ref[side], 0.0), axis=0, keepdims=True)
        blk_ref[60 + side : 61 + side, :] = (SPREAD * level_scale) * shared
        table = jnp.zeros((1, LANES), F32)
        where = lax.broadcasted_iota(I32, (1, LANES), 1)
        for number, of in enumerate((side, 2 if side < 2 else 0, 3 if side < 2 else 1)):
            table = jnp.where(where == 2 * number, adj_ref[0, of].astype(F32), table)
            table = jnp.where(where == 2 * number + 1, flag_ref[0, of].astype(F32), table)
        blk_ref[64 + side : 65 + side, :] = table
    g_ref[0:ROWS, :] = jnp.minimum(depth, 1.0)
    za_ref, zb_ref = z_ref.at[0], z_ref.at[1]
    write_frames(dense_ref, 0, blk_ref, 0, za_ref, zb_ref, 4)
    write_frames(dense_ref, 3 * ROWS, blk_ref, 16, za_ref, zb_ref, 4)
    write_frames(g_ref, 0, blk_ref, 32, za_ref, zb_ref, 4)
    write_frames(dense_ref, ROWS, blk_ref, 48, za_ref, zb_ref, 3)


def pick(refs, shifts, tiles, me, neighbour, side_met):
    value = refs[0][side_met]
    for number in range(1, len(shifts)):
        hit = neighbour == lax.rem(me + tiles - shifts[number], tiles)
        value = jnp.where(hit, refs[number][side_met], value)
    return value


def seam_index(flag):
    lane = lanes8()
    return jnp.where((flag & 1) == 1, SIDE - 1 - lane, lane) & 127


def block_rows(refs, places, first, size):
    for ref, held in zip(refs, places):
        for number, position in enumerate(held):
            at = number * BLOCK + first
            yield position, ref[at : at + size, :]


def gather_lines(p, lines):
    high = lines.astype(jnp.bfloat16)
    rest = lines - high.astype(F32)
    middle = rest.astype(jnp.bfloat16)
    low = (rest - middle.astype(F32)).astype(jnp.bfloat16)
    out = jnp.dot(p, high, preferred_element_type=F32)
    out = out + jnp.dot(p, middle, preferred_element_type=F32)
    return out + jnp.dot(p, low, preferred_element_type=F32)


def ends(x, low, high, low_parity, high_parity, depth):
    lane = lax.broadcasted_iota(I32, x.shape, 1)
    low_end = take(low, jnp.where(low_parity == 1, SIDE - 1 - depth, depth))
    high_end = take(high, jnp.where(high_parity == 1, SIDE - 1 - depth, depth))
    return (
        jnp.where(lane == 0, low_end, pltpu.roll(x, 1, 1)),
        jnp.where(lane == SIDE - 1, high_end, pltpu.roll(x, LANES - 1, 1)),
    )


def krylov_kernel(places, lines, me_ref, dense_ref, *rest):
    refs = rest[: len(places)]
    va_ref, vb_ref, line_ref, gram_ref = rest[len(places) : len(places) + 4]
    p_ref, index_ref, frame_ref, work_ref, wet_ref, d_ref, x_ref = rest[len(places) + 4 :]
    me = me_ref[0]

    def collect(out, first):
        for position, rows in block_rows(refs, places, first, 4):
            out[position * 4 : position * 4 + 4, :] = rows

    collect(work_ref.at[0], 60)
    collect(work_ref.at[1], 64)
    for depth in range(4):
        collect(x_ref.at[depth], 4 * depth)
        collect(x_ref.at[4 + depth], 16 + 4 * depth)
        collect(wet_ref.at[depth], 32 + 4 * depth)
        if depth < 3:
            collect(d_ref.at[depth], 48 + 4 * depth)
    lane = lax.broadcasted_iota(I32, (lines, LANES), 1)
    line = lax.broadcasted_iota(I32, (lines, LANES), 0)
    odd = line & 1
    column = lax.broadcasted_iota(I32, (lines, lines), 1)
    line_of = lax.broadcasted_iota(I32, (lines, lines), 0)
    for number in range(3):
        tile = work_ref[1, :, 2 * number : 2 * number + 1].astype(I32)
        flag = work_ref[1, :, 2 * number + 1 : 2 * number + 2].astype(I32)
        at = jnp.where(tile >= 0, 4 * (tile ^ me) + (flag >> 1), -1)
        p = jnp.where(jnp.broadcast_to(at, (lines, lines)) == column, 1.0, 0.0)
        p_ref[number * lines : (number + 1) * lines, :] = p.astype(jnp.bfloat16)
        parity = jnp.broadcast_to(flag & 1, (lines, LANES))
        if number == 0:
            index_ref[0:lines, :] = jnp.where(parity == 1, SIDE - 1 - lane, lane) & 127
        else:
            index_ref[number * lines : (number + 1) * lines, :] = parity ^ odd
    first_half = (line_of & 2) == 0
    for number in range(2):
        at = (line_of & -4) + jnp.where(first_half, 2, 0) + number
        p = jnp.where(at == column, 1.0, 0.0)
        p_ref[(3 + number) * lines : (4 + number) * lines, :] = p.astype(jnp.bfloat16)
    p = p_ref[0 : 3 * lines, :]
    facing_at = index_ref[0:lines, :]
    low_parity = index_ref[lines : 2 * lines, :]
    high_parity = index_ref[2 * lines : 3 * lines, :]
    wet = [wet_ref[depth] for depth in range(4)]
    met = gather_lines(p, wet[0])
    facing = take(met[0:lines], facing_at)
    for depth in range(3):
        low, high = ends(
            wet[depth], met[lines : 2 * lines], met[2 * lines : 3 * lines], low_parity, high_parity, depth
        )
        masks = [
            wet[depth] * (facing if depth == 0 else wet[depth - 1]),
            wet[depth] * wet[depth + 1],
            wet[depth] * low,
            wet[depth] * high,
        ]
        frame_ref[depth, 0] = d_ref[depth] + ((masks[0] + masks[1]) + (masks[2] + masks[3]))
        for number in range(4):
            frame_ref[depth, 1 + number] = masks[number]
        if depth == 0:
            seam = masks[0][0:8]
    shared = work_ref[0]
    gain = take(gather_lines(p_ref[0:lines, :], shared), facing_at) - shared
    moved = gather_lines(p_ref[3 * lines : 5 * lines, :], gain)
    zero_line = jnp.zeros((lines, LANES), F32)
    for depth in range(4):
        end = jnp.where(odd == 1, SIDE - 1 - depth, depth)
        extra = jnp.where(lane == 0, take(moved[0:lines], end), zero_line)
        extra = extra + jnp.where(lane == SIDE - 1, take(moved[lines : 2 * lines], end), zero_line)
        if depth == 0:
            extra = extra + gain
        x_ref[4 + depth] = x_ref[4 + depth] + extra
    surface = jnp.minimum(dense_ref[2 * ROWS : 3 * ROWS, :], 1.0)
    along, across = interior_reach(surface)
    degree = (along + behind(along, 1)) + (across + behind(across, SIDE))
    masks = scatter_masks()
    diagonal = dense_ref[ROWS : 2 * ROWS, :] + (degree + scatter_lines(masks, seam))
    scale = 2.0 / CENTRE
    row, lane, cell, i, j = grid_iotas()
    inside = cell < CELLS
    forcing = dense_ref[3 * ROWS : 4 * ROWS, :] + scatter_lines(masks, gain[0:8])
    va_ref[0] = forcing
    vb_ref[0] = dense_ref[0:ROWS, :]
    frames = [[[x_ref[4 * solve + depth] for depth in range(4)]] for solve in range(2)]
    own = [[dense_ref[0:ROWS, :]], [forcing]]
    for step in range(ITERS):
        for solve in range(2):
            x = frames[solve][-1]
            met = gather_lines(p, x[0])
            facing = take(met[0:lines], facing_at)
            if solve == 0:
                line_ref[step] = facing[0:8]
            mine = own[solve][-1]
            flow = (along * ahead(mine, 1) + behind(along * mine, 1)) + (
                across * ahead(mine, SIDE) + behind(across * mine, SIDE)
            )
            image = diagonal * mine - flow - scatter_lines(masks, seam * facing[0:8])
            image = jnp.where(inside, scale * image - 2.0 * mine, 0.0)
            own[solve].append(0.5 * image if step == 0 else image - own[solve][-2])
            following = []
            for depth in range(ITERS - 1 - step):
                low, high = ends(
                    x[depth],
                    met[lines : 2 * lines],
                    met[2 * lines : 3 * lines],
                    low_parity,
                    high_parity,
                    depth,
                )
                before = facing if depth == 0 else x[depth - 1]
                flow = (frame_ref[depth, 1] * before + frame_ref[depth, 2] * x[depth + 1]) + (
                    frame_ref[depth, 3] * low + frame_ref[depth, 4] * high
                )
                image = scale * (frame_ref[depth, 0] * x[depth] - flow) - 2.0 * x[depth]
                following.append(0.5 * image if step == 0 else image - frames[solve][-2][depth])
            frames[solve].append(following)
            if step < ITERS - 1:
                (vb_ref if solve == 0 else va_ref)[step + 1] = own[solve][-1]
    for solve in range(2):
        at = 16 * solve
        for first in range(ITERS + 1):
            for second in range(first + 1):
                gram_ref[at : at + 1, :] = jnp.sum(own[solve][first] * own[solve][second], axis=0, keepdims=True)
                at += 1
        gram_ref[at : at + 1, :] = jnp.zeros((1, LANES), F32)


def image_of(p):
    out = [None] * (len(p) + 1)

    def add(at, value):
        out[at] = value if out[at] is None else out[at] + value

    for at, value in enumerate(p):
        add(at, CENTRE * value)
        if at == 0:
            add(1, CENTRE * value)
        else:
            add(at + 1, 0.5 * CENTRE * value)
            add(at - 1, 0.5 * CENTRE * value)
    return out


def form(left, gram, right):
    total = None
    for first, x in enumerate(left):
        inner = None
        for second, y in enumerate(right):
            term = gram[max(first, second)][min(first, second)] * y
            inner = term if inner is None else inner + term
        total = x * inner if total is None else total + x * inner
    return total


def total_gram(refs, sum_ref):
    total = refs[0][...]
    for ref in refs[1:]:
        total = total + ref[...]
    sum_ref[...] = jnp.broadcast_to(jnp.sum(total, axis=1, keepdims=True), sum_ref.shape)


def coefficients(sum_ref, at):
    gram = []
    for first in range(ITERS + 1):
        gram.append([sum_ref[at + second : at + second + 1, :] for second in range(first + 1)])
        at += first + 1
    one = jnp.ones((1, LANES), F32)
    x = []
    r = [one]
    p = [one]
    rr = gram[0][0]
    for step in range(ITERS):
        image = image_of(p)
        curve = form(p, gram, image)
        alpha = jnp.where(curve > 0.0, rr / curve, 0.0)
        x = [x[n] + alpha * p[n] if n < len(x) else alpha * p[n] for n in range(len(p))]
        r = [r[n] - alpha * image[n] if n < len(r) else -alpha * image[n] for n in range(len(image))]
        if step < ITERS - 1:
            new = jnp.maximum(form(r, gram, r), 0.0)
            beta = jnp.where(rr > 0.0, new / rr, 0.0)
            p = [r[n] + beta * p[n] if n < len(p) else r[n] for n in range(len(r))]
            rr = new
    return x


def store_rows(ref, rows):
    last = CELLS // LANES
    ref[:, 0 : last * LANES] = rows[0:last].reshape(1, last * LANES)
    ref[:, last * LANES : CELLS] = rows[last : last + 1, 0 : CELLS - last * LANES]


def combine(x, v_ref):
    out = x[0] * v_ref[0]
    for number in range(1, ITERS):
        out = out + x[number] * v_ref[number]
    return out


def gradient_kernel(shifts, tiles, levels, grams, me_ref, adj_ref, flag_ref, *rest):
    gram_refs = rest[:grams]
    rest = rest[grams:]
    dense_ref, va_ref, v_ref, line_ref, reach_ref, a_ref, q_ref, as_ref = rest[:8]
    refs = rest[8 : 8 + len(shifts)]
    height_ref, out_ref, gram_ref, sum_ref, w_ref, h_ref = rest[8 + len(shifts) :]
    me = me_ref[0]
    total_gram(gram_refs, gram_ref)
    store_rows(height_ref, combine(coefficients(gram_ref, 16), va_ref))
    x = coefficients(gram_ref, 0)
    level_scale = 1.0 / math.sqrt(levels)
    adjoint = combine(x, v_ref) * level_scale
    met_line = x[0] * line_ref[0]
    depth = dense_ref[2 * ROWS : 3 * ROWS, :]
    along, across = interior_reach(depth)
    sum_ref[0:8, :] = met_line + x[1] * line_ref[1] + x[2] * line_ref[2] + x[3] * line_ref[3]
    h_ref[0:ROWS, :] = adjoint
    w_ref[4, 8:9, :] = h_ref[0:1, :]
    w_ref[4, 9:10, :] = row_line(h_ref, 0, (SIDE - 1) * SIDE)
    row, lane, cell, i, j = grid_iotas()
    column = (j == 0) | (j == SIDE - 1)
    zero = jnp.zeros((ROWS, LANES), F32)
    za = jnp.sum(jnp.where(column & (i < 64), adjoint, zero), axis=0, keepdims=True)
    zb = jnp.sum(jnp.where(column & (i >= 64), adjoint, zero), axis=0, keepdims=True)
    side2, side3 = lines_23(jnp.broadcast_to(za, (8, LANES)), jnp.broadcast_to(zb, (8, LANES)), 0)
    w_ref[4, 10:11, :] = side2[0:1]
    w_ref[4, 11:12, :] = side3[0:1]
    level = lax.broadcasted_iota(I32, (32, LANES), 0).astype(F32)
    fluxes = []
    for side in range(4):
        neighbour = adj_ref[0, side]
        flag = flag_ref[0, side]
        index = seam_index(flag)
        other = take(pick(refs, shifts, tiles, me, neighbour, flag >> 1), index)
        other = other + sum_ref[side : side + 1, :] * level_scale
        own = as_ref[side] + w_ref[4, 8 + side : 9 + side, :]
        fluxes.append(jnp.where(reach_ref[side : side + 1, :] > level, other - own, 0.0))
    wa, wb, w1 = spread_lines(fluxes[2], fluxes[3], fluxes[1])
    w_ref[0] = wa
    w_ref[1] = wb
    w_ref[2] = fluxes[0]
    w_ref[3] = w1
    masks = scatter_masks()

    def per_level(number, carry):
        at = pl.ds(pl.multiple_of(number * ROWS, ROWS), ROWS)
        here = pl.ds(number, 1)
        h = a_ref[at, :] + adjoint * q_ref[at, :]
        spread = interior_spread(h, along, across, number.astype(F32))
        spread = spread + scatter_rows(
            masks, w_ref[0, here, :], w_ref[1, here, :], w_ref[2, here, :], w_ref[3, here, :]
        )
        store_rows(out_ref.at[number], h + SPREAD * spread)
        return carry

    lax.fori_loop(0, levels, per_level, 0, unroll=2)


def rounds(tiles):
    out = []
    stride = tiles
    while stride > 1:
        stride //= 2
        out.append((stride, 2))
    return out


def swap(x, tiles, offset):
    return lax.ppermute(x, "tile", [(t, t ^ offset) for t in range(tiles)])


def gather_tiles(block, tiles):
    held = [block]
    places = [(0,)]
    for stride, radix in rounds(tiles):
        whole = held[0] if len(held) == 1 else jnp.concatenate(held, axis=0)
        covered = tuple(n for place in places for n in place)
        for number in range(1, radix):
            held.append(swap(whole, tiles, number * stride))
            places.append(tuple(n ^ (number * stride) for n in covered))
    return held, tuple(places)


def sum_tiles(block, tiles):
    held = [block]
    for stride, radix in rounds(tiles):
        whole = functools.reduce(jnp.add, held)
        held = [whole] + [swap(whole, tiles, number * stride) for number in range(1, radix)]
    return held


def shards(thermal, stirring, depth, adjacent, flags, main_entry, sensitivity, elevation, tiles):
    levels = thermal.shape[1]
    me = lax.axis_index("tile").astype(I32).reshape(1)
    smem = pl.BlockSpec(memory_space=pltpu.SMEM)
    vmem = pl.BlockSpec(memory_space=pltpu.VMEM)

    def shape(*dims):
        return jax.ShapeDtypeStruct(dims, F32)

    hbm = pl.BlockSpec(memory_space=pltpu.HBM)

    def call(kernel, outs, scratch, scalars, arrays, name, flops=1e6, traffic=1e6, far=(), grant=48):
        return pl.pallas_call(
            kernel,
            out_shape=outs,
            in_specs=[smem] * len(scalars) + [vmem] * len(arrays) + [hbm] * len(far),
            out_specs=jax.tree.map(lambda _: vmem, outs),
            scratch_shapes=scratch,
            compiler_params=pltpu.CompilerParams(vmem_limit_bytes=grant * 1024 * 1024),
            cost_estimate=pl.CostEstimate(flops=int(flops), bytes_accessed=int(traffic), transcendentals=0),
            name=name,
        )(*scalars, *arrays, *far)

    offsets = []
    for offset in (1, -1, ROW_TILES, -ROW_TILES, tiles // 2):
        if offset % tiles not in [o % tiles for o in offsets] and offset % tiles:
            offsets.append(offset)
    shifts = tuple(offset % tiles for offset in offsets)

    def to_neighbours(x):
        out = []
        for offset in offsets:
            pairs = [(t, t + offset) for t in range(tiles) if 0 <= t + offset < tiles]
            if 2 * offset == tiles or 2 * offset == -tiles:
                pairs = [(t, (t + offset) % tiles) for t in range(tiles)]
            out.append(lax.ppermute(x, "tile", pairs))
        return out

    def by_level(x):
        return jnp.transpose(x, (1, 0, 2))

    own_depths = call(
        depths_kernel,
        shape(8, LANES),
        [pltpu.VMEM((ROWS, LANES), F32), pltpu.VMEM((2, 8, LANES), F32)],
        (),
        (depth,),
        "depths",
    )
    depths_met = to_neighbours(own_depths)
    far = pltpu.VMEM((levels, 1, CELLS), F32)
    solved, weight, strips, block, dense, reach = call(
        functools.partial(columns_kernel, shifts, tiles, levels),
        (
            shape(levels * ROWS, LANES),
            shape(levels * ROWS, LANES),
            shape(4, 32, LANES),
            shape(BLOCK, LANES),
            shape(4 * ROWS, LANES),
            shape(8, LANES),
        ),
        [
            far,
            far,
            far,
            pltpu.VMEM((1, CELLS), I32),
            pltpu.VMEM((1, CELLS), F32),
            pltpu.VMEM((1, CELLS), F32),
            pltpu.VMEM((levels * ROWS, LANES), F32),
            pltpu.VMEM((8, 32, LANES), F32),
            pltpu.VMEM((4, 32, LANES), F32),
            pltpu.SemaphoreType.DMA((10,)),
        ],
        (me, adjacent, flags),
        (own_depths, *depths_met),
        "columns",
        2e7,
        8e6,
        tuple(pltpu.with_memory_space_constraint(v, pltpu.HBM) for v in (by_level(stirring), by_level(sensitivity), by_level(thermal), depth, main_entry, elevation)),
        48,
    )
    blocks, places = gather_tiles(block, tiles)
    strips_met = to_neighbours(strips)
    lines = 4 * tiles
    frame = pltpu.VMEM((4, lines, LANES), F32)
    basis = shape(ITERS, ROWS, LANES)
    basis_a, basis_b, lines_b, gram = call(
        functools.partial(krylov_kernel, places, lines),
        (basis, basis, shape(ITERS, 8, LANES), shape(32, LANES)),
        [
            pltpu.VMEM((5 * lines, lines), jnp.bfloat16),
            pltpu.VMEM((3 * lines, LANES), I32),
            pltpu.VMEM((3, 5, lines, LANES), F32),
            pltpu.VMEM((2, lines, LANES), F32),
            frame,
            frame,
            pltpu.VMEM((8, lines, LANES), F32),
        ],
        (me,),
        (dense, *blocks),
        "krylov",
    )
    grams = sum_tiles(gram, tiles)
    height, gradient = call(
        functools.partial(gradient_kernel, shifts, tiles, levels, len(grams)),
        (jax.ShapeDtypeStruct(elevation.shape, F32), shape(levels, 1, CELLS)),
        [
            pltpu.VMEM((32, LANES), F32),
            pltpu.VMEM((16, LANES), F32),
            pltpu.VMEM((5, 32, LANES), F32),
            pltpu.VMEM((ROWS, LANES), F32),
        ],
        (me, adjacent, flags),
        (
            *grams,
            dense,
            basis_a,
            basis_b,
            lines_b,
            reach,
            solved,
            weight,
            strips,
            *strips_met,
        ),
        "gradient",
        1e7,
        4e6,
    )
    gradient = by_level(gradient)
    return height, gradient


def solution(mesh):
    placed = (
        P(("ens", "tile"), None, None),
        P("tile", None, None),
        P("tile", None),
        P("tile", None),
        P("tile", None),
        P("tile", None),
        P(("ens", "tile"), None, None),
        P(("ens", "tile"), None),
    )
    return jax.shard_map(
        functools.partial(shards, tiles=mesh.shape["tile"]),
        mesh=mesh,
        in_specs=placed,
        out_specs=(P(("ens", "tile"), None), P(("ens", "tile"), None, None)),
        check_vma=False,
    )
```

```python
import functools
import math

import jax
import jax.numpy as jnp
from jax import lax
from jax.experimental import pallas as pl
from jax.experimental.pallas import tpu as pltpu
from jax.sharding import PartitionSpec as P

SIDE = 90
CELLS = SIDE * SIDE
ROWS = 64
LANES = 128
ITERS = 4
ROW_TILES = 8
SPREAD = 0.2
CENTRE = 4.1
BLOCK = 68
F32 = jnp.float32
I32 = jnp.int32


def grid_iotas():
    row = lax.broadcasted_iota(I32, (ROWS, LANES), 0)
    lane = lax.broadcasted_iota(I32, (ROWS, LANES), 1)
    cell = row * LANES + lane
    i = (cell * 46604) >> 22
    j = cell - SIDE * i
    return row, lane, cell, i, j


def ahead(x, n):
    lane = lax.broadcasted_iota(I32, x.shape, 1)
    y = pltpu.roll(x, LANES - n, 1)
    return jnp.where(lane < LANES - n, y, pltpu.roll(y, ROWS - 1, 0))


def behind(x, n):
    lane = lax.broadcasted_iota(I32, x.shape, 1)
    y = pltpu.roll(x, n, 1)
    return jnp.where(lane >= n, y, pltpu.roll(y, 1, 0))


def take(x, index):
    pieces = []
    for first in range(0, x.shape[0], 8):
        part = index if index.shape[0] == 8 else index[first : first + 8]
        pieces.append(jnp.take_along_axis(x[first : first + 8], part, axis=1, mode="promise_in_bounds"))
    return pieces[0] if len(pieces) == 1 else jnp.concatenate(pieces, axis=0)


def lanes8():
    return lax.broadcasted_iota(I32, (8, LANES), 1)


def column_owner(lane):
    odd = lane & 1
    half = (lane - 89 * odd) >> 1
    return (37 * half) & 63


def lines_23(za, zb, depth_row):
    lane = lanes8()
    near = (SIDE * lane + depth_row) & 127
    far = (SIDE * lane + SIDE - 1 - depth_row) & 127
    wide = lax.broadcasted_iota(I32, za.shape, 1)
    first = wide < 64
    return (
        jnp.where(first, take(za, near), take(zb, near)),
        jnp.where(first, take(za, far), take(zb, far)),
    )


def spread_lines(side2, side3, side1):
    lane = lanes8()
    owner = column_owner(lane)
    later = (owner + 64) & 127
    even = (lax.broadcasted_iota(I32, side2.shape, 1) & 1) == 0
    wa = jnp.where(even, take(side2, owner), take(side3, owner))
    wb = jnp.where(even, take(side2, later), take(side3, later))
    return wa, wb, pltpu.roll(side1, 74, 1)


def scatter_masks():
    row, lane, cell, i, j = grid_iotas()
    column = (j == 0) | (j == SIDE - 1)
    return (
        column & (i < 64),
        column & (i >= 64) & (i < SIDE),
        cell < SIDE,
        i == SIDE - 1,
    )


def scatter_rows(masks, wa, wb, side0, w1):
    zero = jnp.zeros((ROWS, LANES), F32)
    out = jnp.where(masks[0], wa, zero) + jnp.where(masks[1], wb, zero)
    return out + jnp.where(masks[2], side0, zero) + jnp.where(masks[3], w1, zero)


def scatter_lines(masks, lines):
    wa, wb, w1 = spread_lines(
        jnp.broadcast_to(lines[2:3], (8, LANES)),
        jnp.broadcast_to(lines[3:4], (8, LANES)),
        jnp.broadcast_to(lines[1:2], (8, LANES)),
    )
    return scatter_rows(masks, wa[0:1], wb[0:1], lines[0:1], w1[0:1])


def row_line(ref, base, first_cell):
    row, off = divmod(first_cell, LANES)
    top = ref[pl.ds(base + row, 1), :]
    if off == 0:
        return top
    lane = lax.broadcasted_iota(I32, (1, LANES), 1)
    top = pltpu.roll(top, LANES - off, 1)
    if off + SIDE <= LANES:
        return top
    low = pltpu.roll(ref[pl.ds(base + row + 1, 1), :], LANES - off, 1)
    return jnp.where(lane < LANES - off, top, low)


def write_frames(field_ref, base, out_ref, first_row, za_ref, zb_ref, depths):
    field = field_ref[base : base + ROWS, :]
    row, lane, cell, i, j = grid_iotas()
    za_ref[0:8, :] = jnp.zeros((8, LANES), F32)
    zb_ref[0:8, :] = jnp.zeros((8, LANES), F32)
    for depth in range(depths):
        column = ((j == depth) | (j == SIDE - 1 - depth)) & (i < SIDE)
        za_ref[depth : depth + 1, :] = jnp.sum(
            jnp.where(column & (i < 64), field, 0.0)[0:48], axis=0, keepdims=True
        )
        zb_ref[depth : depth + 1, :] = jnp.sum(
            jnp.where(column & (i >= 64), field, 0.0)[40:ROWS], axis=0, keepdims=True
        )
        at = first_row + depth * 4
        out_ref[at : at + 1, :] = row_line(field_ref, base, depth * SIDE)
        out_ref[at + 1 : at + 2, :] = row_line(field_ref, base, (SIDE - 1 - depth) * SIDE)
    depth_row = lax.broadcasted_iota(I32, (8, LANES), 0) & 3
    side2, side3 = lines_23(za_ref[0:8, :], zb_ref[0:8, :], depth_row)
    for depth in range(depths):
        at = first_row + depth * 4
        out_ref[at + 2 : at + 3, :] = side2[depth : depth + 1]
        out_ref[at + 3 : at + 4, :] = side3[depth : depth + 1]


def level_rows(ref, level):
    whole = (CELLS // LANES // 8) * 8
    rows = CELLS // LANES
    window = ref[level, :, CELLS - LANES : CELLS]
    return jnp.concatenate(
        [
            ref[level, :, 0 : whole * LANES].reshape(whole, LANES),
            ref[level, :, whole * LANES : rows * LANES].reshape(rows - whole, LANES),
            pltpu.roll(window, CELLS - rows * LANES, 1),
        ],
        axis=0,
    )


def surface_rows(ref):
    whole = (CELLS // LANES // 8) * 8
    rows = CELLS // LANES
    window = ref[:, CELLS - LANES : CELLS]
    return jnp.concatenate(
        [
            ref[:, 0 : whole * LANES].reshape(whole, LANES),
            ref[:, whole * LANES : rows * LANES].reshape(rows - whole, LANES),
            pltpu.roll(window, CELLS - rows * LANES, 1),
        ],
        axis=0,
    )


def interior_reach(depth):
    row, lane, cell, i, j = grid_iotas()
    zero = jnp.zeros_like(depth)
    along = jnp.where(j < SIDE - 1, jnp.minimum(depth, ahead(depth, 1)), zero)
    across = jnp.where(cell < CELLS - SIDE, jnp.minimum(depth, ahead(depth, SIDE)), zero)
    return along, across


def interior_spread(x, along, across, level):
    zero = jnp.zeros_like(x)
    flux1 = jnp.where(along > level, ahead(x, 1) - x, zero)
    flux2 = jnp.where(across > level, ahead(x, SIDE) - x, zero)
    return (flux1 - behind(flux1, 1)) + (flux2 - behind(flux2, SIDE))


def depths_kernel(depth_ref, out_ref, dense_ref, z_ref):
    row, lane, cell, i, j = grid_iotas()
    dense_ref[...] = jnp.where(cell < CELLS, surface_rows(depth_ref).astype(F32), 0.0)
    write_frames(dense_ref, 0, out_ref, 0, z_ref.at[0], z_ref.at[1], 1)
    out_ref[4:8, :] = jnp.zeros((4, LANES), F32)


def columns_kernel(exchanges, levels, me_ref, adj_ref, flag_ref, own_ref, *rest):
    met_refs = rest[: len(exchanges)]
    k_hbm, s_hbm, t_hbm, depth_hbm, d_hbm, b_hbm = rest[len(exchanges) : len(exchanges) + 6]
    a_ref, q_ref, as_ref, blk_ref, dense_ref, reach_ref = rest[len(exchanges) + 6 : len(exchanges) + 12]
    k_ref, s_ref, t_ref, depth_ref, d_ref, b_ref, g_ref, z_ref, ts_ref, sems = rest[len(exchanges) + 12 :]
    parts = 3
    third = levels // parts
    surface = [
        pltpu.make_async_copy(source, target, sems.at[number])
        for number, (source, target) in enumerate(((depth_hbm, depth_ref), (b_hbm, b_ref), (d_hbm, d_ref)))
    ]
    for copy in surface:
        copy.start()
    columns = []
    for part in range(parts):
        at = pl.ds(part * third, third if part < parts - 1 else levels - part * third)
        for number, (source, target) in enumerate(((k_hbm, k_ref), (s_hbm, s_ref))):
            columns.append(pltpu.make_async_copy(source.at[at], target.at[at], sems.at[3 + 2 * part + number]))
            columns[-1].start()
    tracer = pltpu.make_async_copy(t_hbm, t_ref, sems.at[3 + 2 * parts])
    tracer.start()
    me = me_ref[0]
    row, lane, cell, i, j = grid_iotas()
    inside = cell < CELLS
    for number, ref in enumerate((depth_ref, b_ref, d_ref)):
        surface[number].wait()
        place = (2, 0, 1)[number]
        rows = slice(place * ROWS, (place + 1) * ROWS)
        dense_ref[rows, :] = jnp.where(inside, surface_rows(ref).astype(F32), 0.0)
    depth = dense_ref[2 * ROWS : 3 * ROWS, :]
    along, across = interior_reach(depth)
    zero = jnp.zeros((ROWS, LANES), F32)

    def down(level, carry):
        link, below, va, vq = carry
        at = pl.ds(pl.multiple_of(level * ROWS, ROWS), ROWS)
        here = level.astype(F32)
        r = jnp.where(depth > here + 1.0, level_rows(k_ref, level), zero)
        wet = jnp.where(depth > here, 1.0, zero)
        upper = 1.0 + below
        inverse = 1.0 / (upper + r)
        ratio = r * inverse
        va = (level_rows(s_ref, level) + link * va) * inverse
        vq = (wet + link * vq) * inverse
        g_ref[at, :] = ratio
        a_ref[at, :] = va
        q_ref[at, :] = vq
        return r, upper * ratio, va, vq

    carry = (zero, zero, zero, zero)
    for part in range(parts):
        columns[2 * part].wait()
        columns[2 * part + 1].wait()
        last = (part + 1) * third if part < parts - 1 else levels
        carry = lax.fori_loop(part * third, last, down, carry, unroll=2)
    tracer.wait()
    column = ((j == 0) | (j == SIDE - 1)) & (i < SIDE)
    first = (column & (i < 64))[0:48]
    second = (column & (i >= 64))[40:ROWS]

    def up(step, carry):
        xa, xq, total, flux1, flux2 = carry
        level = levels - 1 - step
        here = level.astype(F32)
        at = pl.ds(pl.multiple_of(level * ROWS, ROWS), ROWS)
        ratio = g_ref[at, :]
        xa = a_ref[at, :] + ratio * xa
        xq = q_ref[at, :] + ratio * xq
        a_ref[at, :] = xa
        q_ref[at, :] = xq
        t = level_rows(t_ref, level)
        line = pl.ds(level, 1)
        for number, (x, out) in enumerate(((t, ts_ref), (xa, as_ref))):
            base = number * 4
            z_ref[base, line, :] = jnp.sum(jnp.where(first, x[0:48], 0.0), axis=0, keepdims=True)
            z_ref[base + 1, line, :] = jnp.sum(jnp.where(second, x[40:ROWS], 0.0), axis=0, keepdims=True)
            out[0, line, :] = x[0:1]
            z_ref[base + 2, line, :] = x[ROWS - 2 : ROWS - 1]
            z_ref[base + 3, line, :] = x[ROWS - 1 : ROWS]
        flux1 = flux1 + jnp.where(along > here, xq * (ahead(t, 1) - t), zero)
        flux2 = flux2 + jnp.where(across > here, xq * (ahead(t, SIDE) - t), zero)
        return xa, xq, total + xq * t, flux1, flux2

    xa, xq, total, flux1, flux2 = lax.fori_loop(0, levels, up, (zero,) * 5, unroll=2)
    level_scale = 1.0 / math.sqrt(levels)
    spread = (flux1 - behind(flux1, 1)) + (flux2 - behind(flux2, SIDE))
    dense_ref[3 * ROWS : 4 * ROWS, :] = jnp.where(inside, (total + SPREAD * spread) * level_scale, zero)
    spare = z_ref.shape[1] - levels
    for number, out in enumerate((ts_ref, as_ref)):
        base = number * 4
        for part in range(4):
            z_ref[base + part, levels:, :] = jnp.zeros((spare, LANES), F32)
        out[0, levels:, :] = jnp.zeros((spare, LANES), F32)
        side2, side3 = lines_23(z_ref[base], z_ref[base + 1], 0)
        out[2] = side2
        out[3] = side3
        low, high = z_ref[base + 2], z_ref[base + 3]
        wide = lax.broadcasted_iota(I32, low.shape, 1)
        out[1] = jnp.where(wide < 54, pltpu.roll(low, 54, 1), pltpu.roll(high, 54, 1))
    level = lax.broadcasted_iota(I32, (32, LANES), 0).astype(F32)
    reach_ref[4:8, :] = jnp.zeros((4, LANES), F32)
    for side in range(4):
        neighbour = adj_ref[0, side]
        flag = flag_ref[0, side]
        met = pick(exchanges, me, neighbour, lambda n: met_refs[n][pl.ds(flag >> 1, 1), :])
        met = take(jnp.broadcast_to(met, (8, LANES)), seam_index(flag))[0:1]
        reach = jnp.where(neighbour >= 0, jnp.minimum(met, own_ref[side : side + 1, :]), 0.0)
        reach_ref[side : side + 1, :] = reach
        shared = jnp.sum(jnp.where(reach > level, ts_ref[side], 0.0), axis=0, keepdims=True)
        blk_ref[60 + side : 61 + side, :] = (SPREAD * level_scale) * shared
        table = jnp.zeros((1, LANES), F32)
        where = lax.broadcasted_iota(I32, (1, LANES), 1)
        for number, of in enumerate((side, 2 if side < 2 else 0, 3 if side < 2 else 1)):
            table = jnp.where(where == 2 * number, adj_ref[0, of].astype(F32), table)
            table = jnp.where(where == 2 * number + 1, flag_ref[0, of].astype(F32), table)
        blk_ref[64 + side : 65 + side, :] = table
    g_ref[0:ROWS, :] = jnp.minimum(depth, 1.0)
    za_ref, zb_ref = z_ref.at[0], z_ref.at[1]
    write_frames(dense_ref, 0, blk_ref, 0, za_ref, zb_ref, 4)
    write_frames(dense_ref, 3 * ROWS, blk_ref, 16, za_ref, zb_ref, 4)
    write_frames(g_ref, 0, blk_ref, 32, za_ref, zb_ref, 4)
    write_frames(dense_ref, ROWS, blk_ref, 48, za_ref, zb_ref, 3)


def partner(exchange, me):
    stride, odd = exchange
    if not odd:
        return me ^ stride
    return jnp.where(((me // stride) & 1) == 1, me + stride, me - stride)


def pick(exchanges, me, neighbour, lines_of):
    value = lines_of(0)
    for number in range(1, len(exchanges)):
        value = jnp.where(neighbour == partner(exchanges[number], me), lines_of(number), value)
    return value


def seam_index(flag):
    lane = lanes8()
    return jnp.where((flag & 1) == 1, SIDE - 1 - lane, lane) & 127


def block_rows(refs, places, first, size):
    for ref, held in zip(refs, places):
        for number, position in enumerate(held):
            at = number * BLOCK + first
            yield position, ref[at : at + size, :]


def gather_lines(p, lines):
    high = lines.astype(jnp.bfloat16)
    rest = lines - high.astype(F32)
    middle = rest.astype(jnp.bfloat16)
    low = (rest - middle.astype(F32)).astype(jnp.bfloat16)
    out = jnp.dot(p, high, preferred_element_type=F32)
    out = out + jnp.dot(p, middle, preferred_element_type=F32)
    return out + jnp.dot(p, low, preferred_element_type=F32)


def ends(x, low, high, low_parity, high_parity, depth):
    lane = lax.broadcasted_iota(I32, x.shape, 1)
    low_end = take(low, jnp.where(low_parity == 1, SIDE - 1 - depth, depth))
    high_end = take(high, jnp.where(high_parity == 1, SIDE - 1 - depth, depth))
    return (
        jnp.where(lane == 0, low_end, pltpu.roll(x, 1, 1)),
        jnp.where(lane == SIDE - 1, high_end, pltpu.roll(x, LANES - 1, 1)),
    )


def krylov_kernel(places, lines, me_ref, dense_ref, *rest):
    refs = rest[: len(places)]
    va_ref, vb_ref, line_ref, gram_ref = rest[len(places) : len(places) + 4]
    p_ref, index_ref, frame_ref, work_ref, wet_ref, d_ref, x_ref = rest[len(places) + 4 :]
    me = me_ref[0]

    def collect(out, first):
        for position, rows in block_rows(refs, places, first, 4):
            out[position * 4 : position * 4 + 4, :] = rows

    collect(work_ref.at[0], 60)
    collect(work_ref.at[1], 64)
    for depth in range(4):
        collect(x_ref.at[depth], 4 * depth)
        collect(x_ref.at[4 + depth], 16 + 4 * depth)
        collect(wet_ref.at[depth], 32 + 4 * depth)
        if depth < 3:
            collect(d_ref.at[depth], 48 + 4 * depth)
    lane = lax.broadcasted_iota(I32, (lines, LANES), 1)
    line = lax.broadcasted_iota(I32, (lines, LANES), 0)
    odd = line & 1
    column = lax.broadcasted_iota(I32, (lines, lines), 1)
    line_of = lax.broadcasted_iota(I32, (lines, lines), 0)
    for number in range(3):
        tile = work_ref[1, :, 2 * number : 2 * number + 1].astype(I32)
        flag = work_ref[1, :, 2 * number + 1 : 2 * number + 2].astype(I32)
        at = jnp.where(tile >= 0, 4 * (tile ^ me) + (flag >> 1), -1)
        p = jnp.where(jnp.broadcast_to(at, (lines, lines)) == column, 1.0, 0.0)
        p_ref[number * lines : (number + 1) * lines, :] = p.astype(jnp.bfloat16)
        parity = jnp.broadcast_to(flag & 1, (lines, LANES))
        if number == 0:
            index_ref[0:lines, :] = jnp.where(parity == 1, SIDE - 1 - lane, lane) & 127
        else:
            index_ref[number * lines : (number + 1) * lines, :] = parity ^ odd
    first_half = (line_of & 2) == 0
    for number in range(2):
        at = (line_of & -4) + jnp.where(first_half, 2, 0) + number
        p = jnp.where(at == column, 1.0, 0.0)
        p_ref[(3 + number) * lines : (4 + number) * lines, :] = p.astype(jnp.bfloat16)
    p = p_ref[0 : 3 * lines, :]
    facing_at = index_ref[0:lines, :]
    low_parity = index_ref[lines : 2 * lines, :]
    high_parity = index_ref[2 * lines : 3 * lines, :]
    wet = [wet_ref[depth] for depth in range(4)]
    met = gather_lines(p, wet[0])
    facing = take(met[0:lines], facing_at)
    for depth in range(3):
        low, high = ends(
            wet[depth], met[lines : 2 * lines], met[2 * lines : 3 * lines], low_parity, high_parity, depth
        )
        masks = [
            wet[depth] * (facing if depth == 0 else wet[depth - 1]),
            wet[depth] * wet[depth + 1],
            wet[depth] * low,
            wet[depth] * high,
        ]
        frame_ref[depth, 0] = d_ref[depth] + ((masks[0] + masks[1]) + (masks[2] + masks[3]))
        for number in range(4):
            frame_ref[depth, 1 + number] = masks[number]
        if depth == 0:
            seam = masks[0][0:8]
    shared = work_ref[0]
    gain = take(gather_lines(p_ref[0:lines, :], shared), facing_at) - shared
    moved = gather_lines(p_ref[3 * lines : 5 * lines, :], gain)
    zero_line = jnp.zeros((lines, LANES), F32)
    for depth in range(4):
        end = jnp.where(odd == 1, SIDE - 1 - depth, depth)
        extra = jnp.where(lane == 0, take(moved[0:lines], end), zero_line)
        extra = extra + jnp.where(lane == SIDE - 1, take(moved[lines : 2 * lines], end), zero_line)
        if depth == 0:
            extra = extra + gain
        x_ref[4 + depth] = x_ref[4 + depth] + extra
    surface = jnp.minimum(dense_ref[2 * ROWS : 3 * ROWS, :], 1.0)
    along, across = interior_reach(surface)
    degree = (along + behind(along, 1)) + (across + behind(across, SIDE))
    masks = scatter_masks()
    diagonal = dense_ref[ROWS : 2 * ROWS, :] + (degree + scatter_lines(masks, seam))
    scale = 2.0 / CENTRE
    row, lane, cell, i, j = grid_iotas()
    inside = cell < CELLS
    forcing = dense_ref[3 * ROWS : 4 * ROWS, :] + scatter_lines(masks, gain[0:8])
    va_ref[0] = forcing
    vb_ref[0] = dense_ref[0:ROWS, :]
    frames = [[[x_ref[4 * solve + depth] for depth in range(4)]] for solve in range(2)]
    own = [[dense_ref[0:ROWS, :]], [forcing]]
    for step in range(ITERS):
        for solve in range(2):
            x = frames[solve][-1]
            met = gather_lines(p, x[0])
            facing = take(met[0:lines], facing_at)
            if solve == 0:
                line_ref[step] = facing[0:8]
            mine = own[solve][-1]
            flow = (along * ahead(mine, 1) + behind(along * mine, 1)) + (
                across * ahead(mine, SIDE) + behind(across * mine, SIDE)
            )
            image = diagonal * mine - flow - scatter_lines(masks, seam * facing[0:8])
            image = jnp.where(inside, scale * image - 2.0 * mine, 0.0)
            own[solve].append(0.5 * image if step == 0 else image - own[solve][-2])
            following = []
            for depth in range(ITERS - 1 - step):
                low, high = ends(
                    x[depth],
                    met[lines : 2 * lines],
                    met[2 * lines : 3 * lines],
                    low_parity,
                    high_parity,
                    depth,
                )
                before = facing if depth == 0 else x[depth - 1]
                flow = (frame_ref[depth, 1] * before + frame_ref[depth, 2] * x[depth + 1]) + (
                    frame_ref[depth, 3] * low + frame_ref[depth, 4] * high
                )
                image = scale * (frame_ref[depth, 0] * x[depth] - flow) - 2.0 * x[depth]
                following.append(0.5 * image if step == 0 else image - frames[solve][-2][depth])
            frames[solve].append(following)
            if step < ITERS - 1:
                (vb_ref if solve == 0 else va_ref)[step + 1] = own[solve][-1]
    for solve in range(2):
        at = 16 * solve
        for first in range(ITERS + 1):
            for second in range(first + 1):
                gram_ref[at : at + 1, :] = jnp.sum(own[solve][first] * own[solve][second], axis=0, keepdims=True)
                at += 1
        gram_ref[at : at + 1, :] = jnp.zeros((1, LANES), F32)


def image_of(p):
    out = [None] * (len(p) + 1)

    def add(at, value):
        out[at] = value if out[at] is None else out[at] + value

    for at, value in enumerate(p):
        add(at, CENTRE * value)
        if at == 0:
            add(1, CENTRE * value)
        else:
            add(at + 1, 0.5 * CENTRE * value)
            add(at - 1, 0.5 * CENTRE * value)
    return out


def form(left, gram, right):
    total = None
    for first, x in enumerate(left):
        inner = None
        for second, y in enumerate(right):
            term = gram[max(first, second)][min(first, second)] * y
            inner = term if inner is None else inner + term
        total = x * inner if total is None else total + x * inner
    return total


def total_gram(refs, sum_ref):
    total = refs[0][...]
    for ref in refs[1:]:
        total = total + ref[...]
    sum_ref[...] = jnp.broadcast_to(jnp.sum(total, axis=1, keepdims=True), sum_ref.shape)


def coefficients(sum_ref, at):
    gram = []
    for first in range(ITERS + 1):
        gram.append([sum_ref[at + second : at + second + 1, :] for second in range(first + 1)])
        at += first + 1
    one = jnp.ones((1, LANES), F32)
    x = []
    r = [one]
    p = [one]
    rr = gram[0][0]
    for step in range(ITERS):
        image = image_of(p)
        curve = form(p, gram, image)
        alpha = jnp.where(curve > 0.0, rr / curve, 0.0)
        x = [x[n] + alpha * p[n] if n < len(x) else alpha * p[n] for n in range(len(p))]
        r = [r[n] - alpha * image[n] if n < len(r) else -alpha * image[n] for n in range(len(image))]
        if step < ITERS - 1:
            new = jnp.maximum(form(r, gram, r), 0.0)
            beta = jnp.where(rr > 0.0, new / rr, 0.0)
            p = [r[n] + beta * p[n] if n < len(p) else r[n] for n in range(len(r))]
            rr = new
    return x


def store_rows(ref, rows):
    last = CELLS // LANES
    ref[:, 0 : last * LANES] = rows[0:last].reshape(1, last * LANES)
    ref[:, last * LANES : CELLS] = rows[last : last + 1, 0 : CELLS - last * LANES]


def combine(x, v_ref):
    out = x[0] * v_ref[0]
    for number in range(1, ITERS):
        out = out + x[number] * v_ref[number]
    return out


def gradient_kernel(exchanges, levels, grams, me_ref, adj_ref, flag_ref, *rest):
    gram_refs = rest[:grams]
    rest = rest[grams:]
    dense_ref, va_ref, v_ref, line_ref, reach_ref, a_ref, q_ref, as_ref = rest[:8]
    refs = rest[8 : 8 + len(exchanges)]
    height_ref, out_ref, gram_ref, sum_ref, w_ref, h_ref = rest[8 + len(exchanges) :]
    me = me_ref[0]
    total_gram(gram_refs, gram_ref)
    store_rows(height_ref, combine(coefficients(gram_ref, 16), va_ref))
    x = coefficients(gram_ref, 0)
    level_scale = 1.0 / math.sqrt(levels)
    adjoint = combine(x, v_ref) * level_scale
    met_line = x[0] * line_ref[0]
    depth = dense_ref[2 * ROWS : 3 * ROWS, :]
    along, across = interior_reach(depth)
    sum_ref[0:8, :] = met_line + x[1] * line_ref[1] + x[2] * line_ref[2] + x[3] * line_ref[3]
    h_ref[0:ROWS, :] = adjoint
    w_ref[4, 8:9, :] = h_ref[0:1, :]
    w_ref[4, 9:10, :] = row_line(h_ref, 0, (SIDE - 1) * SIDE)
    row, lane, cell, i, j = grid_iotas()
    column = (j == 0) | (j == SIDE - 1)
    zero = jnp.zeros((ROWS, LANES), F32)
    za = jnp.sum(jnp.where(column & (i < 64), adjoint, zero), axis=0, keepdims=True)
    zb = jnp.sum(jnp.where(column & (i >= 64), adjoint, zero), axis=0, keepdims=True)
    side2, side3 = lines_23(jnp.broadcast_to(za, (8, LANES)), jnp.broadcast_to(zb, (8, LANES)), 0)
    w_ref[4, 10:11, :] = side2[0:1]
    w_ref[4, 11:12, :] = side3[0:1]
    level = lax.broadcasted_iota(I32, (32, LANES), 0).astype(F32)
    fluxes = []
    for side in range(4):
        neighbour = adj_ref[0, side]
        flag = flag_ref[0, side]
        index = seam_index(flag)
        other = take(pick(exchanges, me, neighbour, lambda n: refs[n][flag >> 1]), index)
        other = other + sum_ref[side : side + 1, :] * level_scale
        own = as_ref[side] + w_ref[4, 8 + side : 9 + side, :]
        fluxes.append(jnp.where(reach_ref[side : side + 1, :] > level, other - own, 0.0))
    wa, wb, w1 = spread_lines(fluxes[2], fluxes[3], fluxes[1])
    w_ref[0] = wa
    w_ref[1] = wb
    w_ref[2] = fluxes[0]
    w_ref[3] = w1
    masks = scatter_masks()

    def per_level(number, carry):
        at = pl.ds(pl.multiple_of(number * ROWS, ROWS), ROWS)
        here = pl.ds(number, 1)
        h = a_ref[at, :] + adjoint * q_ref[at, :]
        spread = interior_spread(h, along, across, number.astype(F32))
        spread = spread + scatter_rows(
            masks, w_ref[0, here, :], w_ref[1, here, :], w_ref[2, here, :], w_ref[3, here, :]
        )
        store_rows(out_ref.at[number], h + SPREAD * spread)
        return carry

    lax.fori_loop(0, levels, per_level, 0, unroll=2)


def rounds(tiles):
    out = []
    stride = tiles
    while stride > 1:
        radix = 4 if stride >= 16 else 2
        stride //= radix
        out.append((stride, radix))
    return out


def swap(x, tiles, offset):
    return lax.ppermute(x, "tile", [(t, t ^ offset) for t in range(tiles)])


def gather_tiles(block, tiles):
    held = [block]
    places = [(0,)]
    for stride, radix in rounds(tiles):
        whole = held[0] if len(held) == 1 else jnp.concatenate(held, axis=0)
        covered = tuple(n for place in places for n in place)
        for number in range(1, radix):
            held.append(swap(whole, tiles, number * stride))
            places.append(tuple(n ^ (number * stride) for n in covered))
    return held, tuple(places)


def sum_tiles(block, tiles):
    held = [block]
    for stride, radix in rounds(tiles):
        whole = functools.reduce(jnp.add, held)
        held = [whole] + [swap(whole, tiles, number * stride) for number in range(1, radix)]
    return held


def shards(thermal, stirring, depth, adjacent, flags, main_entry, sensitivity, elevation, tiles):
    levels = thermal.shape[1]
    me = lax.axis_index("tile").astype(I32).reshape(1)
    smem = pl.BlockSpec(memory_space=pltpu.SMEM)
    vmem = pl.BlockSpec(memory_space=pltpu.VMEM)

    def shape(*dims):
        return jax.ShapeDtypeStruct(dims, F32)

    hbm = pl.BlockSpec(memory_space=pltpu.HBM)

    def call(kernel, outs, scratch, scalars, arrays, name, flops=1e6, traffic=1e6, far=(), grant=48):
        return pl.pallas_call(
            kernel,
            out_shape=outs,
            in_specs=[smem] * len(scalars) + [vmem] * len(arrays) + [hbm] * len(far),
            out_specs=jax.tree.map(lambda _: vmem, outs),
            scratch_shapes=scratch,
            compiler_params=pltpu.CompilerParams(vmem_limit_bytes=grant * 1024 * 1024),
            cost_estimate=pl.CostEstimate(flops=int(flops), bytes_accessed=int(traffic), transcendentals=0),
            name=name,
        )(*scalars, *arrays, *far)

    exchanges = []
    for stride in (1, ROW_TILES, tiles // 2):
        if (stride, False) not in exchanges and stride < tiles:
            exchanges.append((stride, False))
            if stride < ROW_TILES * 2 and stride * 2 < tiles:
                exchanges.append((stride, True))
    exchanges = tuple(exchanges)

    def to_neighbours(x):
        out = []
        for stride, odd in exchanges:
            if odd:
                pairs = [(t, t + stride if (t // stride) % 2 else t - stride) for t in range(tiles)]
                pairs = [(t, u) for t, u in pairs if 0 <= u < tiles]
            else:
                pairs = [(t, t ^ stride) for t in range(tiles)]
            out.append(lax.ppermute(x, "tile", pairs))
        return out

    def by_level(x):
        return jnp.transpose(x, (1, 0, 2))

    own_depths = call(
        depths_kernel,
        shape(8, LANES),
        [pltpu.VMEM((ROWS, LANES), F32), pltpu.VMEM((2, 8, LANES), F32)],
        (),
        (depth,),
        "depths",
    )
    depths_met = to_neighbours(own_depths)
    far = pltpu.VMEM((levels, 1, CELLS), F32)
    solved, weight, strips, block, dense, reach = call(
        functools.partial(columns_kernel, exchanges, levels),
        (
            shape(levels * ROWS, LANES),
            shape(levels * ROWS, LANES),
            shape(4, 32, LANES),
            shape(BLOCK, LANES),
            shape(4 * ROWS, LANES),
            shape(8, LANES),
        ),
        [
            far,
            far,
            far,
            pltpu.VMEM((1, CELLS), I32),
            pltpu.VMEM((1, CELLS), F32),
            pltpu.VMEM((1, CELLS), F32),
            pltpu.VMEM((levels * ROWS, LANES), F32),
            pltpu.VMEM((8, 32, LANES), F32),
            pltpu.VMEM((4, 32, LANES), F32),
            pltpu.SemaphoreType.DMA((10,)),
        ],
        (me, adjacent, flags),
        (own_depths, *depths_met),
        "columns",
        2e7,
        8e6,
        tuple(
            pltpu.with_memory_space_constraint(x, pltpu.HBM)
            for x in (
                by_level(stirring),
                by_level(sensitivity),
                by_level(thermal),
                depth,
                main_entry,
                elevation,
            )
        ),
        48,
    )
    blocks, places = gather_tiles(block, tiles)
    strips_met = to_neighbours(strips)
    lines = 4 * tiles
    frame = pltpu.VMEM((4, lines, LANES), F32)
    basis = shape(ITERS, ROWS, LANES)
    basis_a, basis_b, lines_b, gram = call(
        functools.partial(krylov_kernel, places, lines),
        (basis, basis, shape(ITERS, 8, LANES), shape(32, LANES)),
        [
            pltpu.VMEM((5 * lines, lines), jnp.bfloat16),
            pltpu.VMEM((3 * lines, LANES), I32),
            pltpu.VMEM((3, 5, lines, LANES), F32),
            pltpu.VMEM((2, lines, LANES), F32),
            frame,
            frame,
            pltpu.VMEM((8, lines, LANES), F32),
        ],
        (me,),
        (dense, *blocks),
        "krylov",
    )
    grams = sum_tiles(gram, tiles)
    height, gradient = call(
        functools.partial(gradient_kernel, exchanges, levels, len(grams)),
        (jax.ShapeDtypeStruct(elevation.shape, F32), shape(levels, 1, CELLS)),
        [
            pltpu.VMEM((32, LANES), F32),
            pltpu.VMEM((16, LANES), F32),
            pltpu.VMEM((5, 32, LANES), F32),
            pltpu.VMEM((ROWS, LANES), F32),
        ],
        (me, adjacent, flags),
        (
            *grams,
            dense,
            basis_a,
            basis_b,
            lines_b,
            reach,
            solved,
            weight,
            strips,
            *strips_met,
        ),
        "gradient",
        1e7,
        4e6,
    )
    gradient = by_level(gradient)
    return height, gradient


def solution(mesh):
    placed = (
        P(("ens", "tile"), None, None),
        P("tile", None, None),
        P("tile", None),
        P("tile", None),
        P("tile", None),
        P("tile", None),
        P(("ens", "tile"), None, None),
        P(("ens", "tile"), None),
    )
    return jax.shard_map(
        functools.partial(shards, tiles=mesh.shape["tile"]),
        mesh=mesh,
        in_specs=placed,
        out_specs=(P(("ens", "tile"), None), P(("ens", "tile"), None, None)),
        check_vma=False,
    )
```

```python
import functools
import math

import jax
import jax.numpy as jnp
from jax import lax
from jax.experimental import pallas as pl
from jax.experimental.pallas import tpu as pltpu
from jax.sharding import PartitionSpec as P

SIDE = 90
CELLS = SIDE * SIDE
ROWS = 64
LANES = 128
ITERS = 4
ROW_TILES = 8
SPREAD = 0.2
CENTRE = 4.1
BLOCK = 48
F32 = jnp.float32
I32 = jnp.int32


def grid_iotas():
    row = lax.broadcasted_iota(I32, (ROWS, LANES), 0)
    lane = lax.broadcasted_iota(I32, (ROWS, LANES), 1)
    cell = row * LANES + lane
    i = (cell * 46604) >> 22
    j = cell - SIDE * i
    return row, lane, cell, i, j


def ahead(x, n):
    lane = lax.broadcasted_iota(I32, x.shape, 1)
    y = pltpu.roll(x, LANES - n, 1)
    return jnp.where(lane < LANES - n, y, pltpu.roll(y, ROWS - 1, 0))


def behind(x, n):
    lane = lax.broadcasted_iota(I32, x.shape, 1)
    y = pltpu.roll(x, n, 1)
    return jnp.where(lane >= n, y, pltpu.roll(y, 1, 0))


def take(x, index):
    pieces = []
    for first in range(0, x.shape[0], 8):
        part = index if index.shape[0] == 8 else index[first : first + 8]
        pieces.append(jnp.take_along_axis(x[first : first + 8], part, axis=1, mode="promise_in_bounds"))
    return pieces[0] if len(pieces) == 1 else jnp.concatenate(pieces, axis=0)


def lanes8():
    return lax.broadcasted_iota(I32, (8, LANES), 1)


def column_owner(lane):
    odd = lane & 1
    half = (lane - 89 * odd) >> 1
    return (37 * half) & 63


def lines_23(za, zb, depth_row):
    lane = lanes8()
    near = (SIDE * lane + depth_row) & 127
    far = (SIDE * lane + SIDE - 1 - depth_row) & 127
    wide = lax.broadcasted_iota(I32, za.shape, 1)
    first = wide < 64
    return (
        jnp.where(first, take(za, near), take(zb, near)),
        jnp.where(first, take(za, far), take(zb, far)),
    )


def spread_lines(side2, side3, side1):
    lane = lanes8()
    owner = column_owner(lane)
    later = (owner + 64) & 127
    even = (lax.broadcasted_iota(I32, side2.shape, 1) & 1) == 0
    wa = jnp.where(even, take(side2, owner), take(side3, owner))
    wb = jnp.where(even, take(side2, later), take(side3, later))
    return wa, wb, pltpu.roll(side1, 74, 1)


def scatter_masks():
    row, lane, cell, i, j = grid_iotas()
    column = (j == 0) | (j == SIDE - 1)
    return (
        column & (i < 64),
        column & (i >= 64) & (i < SIDE),
        cell < SIDE,
        i == SIDE - 1,
    )


def scatter_rows(masks, wa, wb, side0, w1):
    zero = jnp.zeros((ROWS, LANES), F32)
    out = jnp.where(masks[0], wa, zero) + jnp.where(masks[1], wb, zero)
    return out + jnp.where(masks[2], side0, zero) + jnp.where(masks[3], w1, zero)


def scatter_lines(masks, lines):
    wa, wb, w1 = spread_lines(
        jnp.broadcast_to(lines[2:3], (8, LANES)),
        jnp.broadcast_to(lines[3:4], (8, LANES)),
        jnp.broadcast_to(lines[1:2], (8, LANES)),
    )
    return scatter_rows(masks, wa[0:1], wb[0:1], lines[0:1], w1[0:1])


def row_line(ref, base, first_cell):
    row, off = divmod(first_cell, LANES)
    top = ref[pl.ds(base + row, 1), :]
    if off == 0:
        return top
    lane = lax.broadcasted_iota(I32, (1, LANES), 1)
    top = pltpu.roll(top, LANES - off, 1)
    if off + SIDE <= LANES:
        return top
    low = pltpu.roll(ref[pl.ds(base + row + 1, 1), :], LANES - off, 1)
    return jnp.where(lane < LANES - off, top, low)


def write_frames(field_ref, base, out_ref, first_row, za_ref, zb_ref, depths):
    field = field_ref[base : base + ROWS, :]
    row, lane, cell, i, j = grid_iotas()
    za_ref[0:8, :] = jnp.zeros((8, LANES), F32)
    zb_ref[0:8, :] = jnp.zeros((8, LANES), F32)
    for depth in range(depths):
        column = ((j == depth) | (j == SIDE - 1 - depth)) & (i < SIDE)
        za_ref[depth : depth + 1, :] = jnp.sum(
            jnp.where(column & (i < 64), field, 0.0)[0:48], axis=0, keepdims=True
        )
        zb_ref[depth : depth + 1, :] = jnp.sum(
            jnp.where(column & (i >= 64), field, 0.0)[40:ROWS], axis=0, keepdims=True
        )
        at = first_row + depth * 4
        out_ref[at : at + 1, :] = row_line(field_ref, base, depth * SIDE)
        out_ref[at + 1 : at + 2, :] = row_line(field_ref, base, (SIDE - 1 - depth) * SIDE)
    depth_row = lax.broadcasted_iota(I32, (8, LANES), 0) & 3
    side2, side3 = lines_23(za_ref[0:8, :], zb_ref[0:8, :], depth_row)
    for depth in range(depths):
        at = first_row + depth * 4
        out_ref[at + 2 : at + 3, :] = side2[depth : depth + 1]
        out_ref[at + 3 : at + 4, :] = side3[depth : depth + 1]


def pack_line(rows, spare, depth):
    lane = lax.broadcasted_iota(I32, rows.shape, 1)
    return jnp.where(lane < SIDE, rows, pltpu.roll(spare, (SIDE - 38 * depth) % LANES, 1))


def unpack_line(first, second, third):
    lane = lax.broadcasted_iota(I32, first.shape, 1)
    out = jnp.where(lane < 38, pltpu.roll(first, 38, 1), pltpu.roll(second, 76, 1))
    return jnp.where(lane < 76, out, pltpu.roll(third, 114, 1))


def level_rows(ref, level):
    whole = (CELLS // LANES // 8) * 8
    rows = CELLS // LANES
    window = ref[level, :, CELLS - LANES : CELLS]
    return jnp.concatenate(
        [
            ref[level, :, 0 : whole * LANES].reshape(whole, LANES),
            ref[level, :, whole * LANES : rows * LANES].reshape(rows - whole, LANES),
            pltpu.roll(window, CELLS - rows * LANES, 1),
        ],
        axis=0,
    )


def surface_rows(ref):
    whole = (CELLS // LANES // 8) * 8
    rows = CELLS // LANES
    window = ref[:, CELLS - LANES : CELLS]
    return jnp.concatenate(
        [
            ref[:, 0 : whole * LANES].reshape(whole, LANES),
            ref[:, whole * LANES : rows * LANES].reshape(rows - whole, LANES),
            pltpu.roll(window, CELLS - rows * LANES, 1),
        ],
        axis=0,
    )


def interior_reach(depth):
    row, lane, cell, i, j = grid_iotas()
    zero = jnp.zeros_like(depth)
    along = jnp.where(j < SIDE - 1, jnp.minimum(depth, ahead(depth, 1)), zero)
    across = jnp.where(cell < CELLS - SIDE, jnp.minimum(depth, ahead(depth, SIDE)), zero)
    return along, across


def interior_spread(x, along, across, level):
    zero = jnp.zeros_like(x)
    flux1 = jnp.where(along > level, ahead(x, 1) - x, zero)
    flux2 = jnp.where(across > level, ahead(x, SIDE) - x, zero)
    return (flux1 - behind(flux1, 1)) + (flux2 - behind(flux2, SIDE))


def depths_kernel(adj_ref, flag_ref, depth_ref, out_ref, dense_ref, z_ref):
    row, lane, cell, i, j = grid_iotas()
    dense_ref[...] = jnp.where(cell < CELLS, surface_rows(depth_ref).astype(F32), 0.0)
    write_frames(dense_ref, 0, out_ref, 0, z_ref.at[0], z_ref.at[1], 1)
    out_ref[4:8, :] = jnp.zeros((4, LANES), F32)


def columns_kernel(exchanges, levels, me_ref, adj_ref, flag_ref, own_ref, *rest):
    met_refs = rest[: len(exchanges)]
    k_hbm, s_hbm, t_hbm, depth_hbm, d_hbm, b_hbm = rest[len(exchanges) : len(exchanges) + 6]
    a_ref, q_ref, as_ref, blk_ref, dense_ref, reach_ref = rest[len(exchanges) + 6 : len(exchanges) + 12]
    k_ref, s_ref, t_ref, depth_ref, d_ref, b_ref, g_ref, z_ref, ts_ref, frame_ref, sems = rest[len(exchanges) + 12 :]
    parts = 3
    third = levels // parts
    surface = [
        pltpu.make_async_copy(source, target, sems.at[number])
        for number, (source, target) in enumerate(((depth_hbm, depth_ref), (b_hbm, b_ref), (d_hbm, d_ref)))
    ]
    for copy in surface:
        copy.start()
    columns = []
    for part in range(parts):
        at = pl.ds(part * third, third if part < parts - 1 else levels - part * third)
        for number, (source, target) in enumerate(((k_hbm, k_ref), (s_hbm, s_ref))):
            columns.append(pltpu.make_async_copy(source.at[at], target.at[at], sems.at[3 + 2 * part + number]))
            columns[-1].start()
    tracer = pltpu.make_async_copy(t_hbm, t_ref, sems.at[3 + 2 * parts])
    tracer.start()
    me = me_ref[0]
    row, lane, cell, i, j = grid_iotas()
    inside = cell < CELLS
    for number, ref in enumerate((depth_ref, b_ref, d_ref)):
        surface[number].wait()
        place = (2, 0, 1)[number]
        rows = slice(place * ROWS, (place + 1) * ROWS)
        dense_ref[rows, :] = jnp.where(inside, surface_rows(ref).astype(F32), 0.0)
    depth = dense_ref[2 * ROWS : 3 * ROWS, :]
    along, across = interior_reach(depth)
    zero = jnp.zeros((ROWS, LANES), F32)

    def down(level, carry):
        link, below, va, vq = carry
        at = pl.ds(pl.multiple_of(level * ROWS, ROWS), ROWS)
        here = level.astype(F32)
        r = jnp.where(depth > here + 1.0, level_rows(k_ref, level), zero)
        wet = jnp.where(depth > here, 1.0, zero)
        upper = 1.0 + below
        centre = upper + r
        inverse = pl.reciprocal(centre, approx=True)
        inverse = inverse * (2.0 - centre * inverse)
        ratio = r * inverse
        va = (level_rows(s_ref, level) + link * va) * inverse
        vq = (wet + link * vq) * inverse
        g_ref[at, :] = ratio
        a_ref[at, :] = va
        q_ref[at, :] = vq
        return r, upper * ratio, va, vq

    carry = (zero, zero, zero, zero)
    for part in range(parts):
        columns[2 * part].wait()
        columns[2 * part + 1].wait()
        last = (part + 1) * third if part < parts - 1 else levels
        carry = lax.fori_loop(part * third, last, down, carry, unroll=2)
    tracer.wait()
    column = ((j == 0) | (j == SIDE - 1)) & (i < SIDE)
    first = (column & (i < 64))[0:48]
    second = (column & (i >= 64))[40:ROWS]

    def up(step, carry):
        xa, xq, total, flux1, flux2 = carry
        level = levels - 1 - step
        here = level.astype(F32)
        at = pl.ds(pl.multiple_of(level * ROWS, ROWS), ROWS)
        ratio = g_ref[at, :]
        xa = a_ref[at, :] + ratio * xa
        xq = q_ref[at, :] + ratio * xq
        a_ref[at, :] = xa
        q_ref[at, :] = xq
        t = level_rows(t_ref, level)
        line = pl.ds(level, 1)
        for number, (x, out) in enumerate(((t, ts_ref), (xa, as_ref))):
            base = number * 4
            z_ref[base, line, :] = jnp.sum(jnp.where(first, x[0:48], 0.0), axis=0, keepdims=True)
            z_ref[base + 1, line, :] = jnp.sum(jnp.where(second, x[40:ROWS], 0.0), axis=0, keepdims=True)
            out[0, line, :] = x[0:1]
            z_ref[base + 2, line, :] = x[ROWS - 2 : ROWS - 1]
            z_ref[base + 3, line, :] = x[ROWS - 1 : ROWS]
        flux1 = flux1 + jnp.where(along > here, xq * (ahead(t, 1) - t), zero)
        flux2 = flux2 + jnp.where(across > here, xq * (ahead(t, SIDE) - t), zero)
        return xa, xq, total + xq * t, flux1, flux2

    xa, xq, total, flux1, flux2 = lax.fori_loop(0, levels, up, (zero,) * 5, unroll=2)
    level_scale = 1.0 / math.sqrt(levels)
    spread = (flux1 - behind(flux1, 1)) + (flux2 - behind(flux2, SIDE))
    dense_ref[3 * ROWS : 4 * ROWS, :] = jnp.where(inside, (total + SPREAD * spread) * level_scale, zero)
    spare = z_ref.shape[1] - levels
    for number, out in enumerate((ts_ref, as_ref)):
        base = number * 4
        for part in range(4):
            z_ref[base + part, levels:, :] = jnp.zeros((spare, LANES), F32)
        out[0, levels:, :] = jnp.zeros((spare, LANES), F32)
        side2, side3 = lines_23(z_ref[base], z_ref[base + 1], 0)
        out[2] = side2
        out[3] = side3
        low, high = z_ref[base + 2], z_ref[base + 3]
        wide = lax.broadcasted_iota(I32, low.shape, 1)
        out[1] = jnp.where(wide < 54, pltpu.roll(low, 54, 1), pltpu.roll(high, 54, 1))
    level = lax.broadcasted_iota(I32, (32, LANES), 0).astype(F32)
    reach_ref[4:8, :] = jnp.zeros((4, LANES), F32)
    for side in range(4):
        neighbour = adj_ref[0, side]
        flag = flag_ref[0, side]
        met = pick(exchanges, me, neighbour, lambda n: met_refs[n][pl.ds(flag >> 1, 1), :])
        met = take(jnp.broadcast_to(met, (8, LANES)), seam_index(flag))[0:1]
        reach = jnp.where(neighbour >= 0, jnp.minimum(met, own_ref[side : side + 1, :]), 0.0)
        reach_ref[side : side + 1, :] = reach
        shared = jnp.sum(jnp.where(reach > level, ts_ref[side], 0.0), axis=0, keepdims=True)
        frame_ref[12 + side : 13 + side, :] = (SPREAD * level_scale) * shared
        table = jnp.zeros((1, LANES), F32)
        where = lax.broadcasted_iota(I32, (1, LANES), 1)
        for number, of in enumerate((side, 2 if side < 2 else 0, 3 if side < 2 else 1)):
            table = jnp.where(where == 104 + 2 * number, adj_ref[0, of].astype(F32), table)
            table = jnp.where(where == 105 + 2 * number, flag_ref[0, of].astype(F32), table)
        frame_ref[16 + side : 17 + side, :] = table
    g_ref[0:ROWS, :] = jnp.minimum(depth, 1.0)
    za_ref, zb_ref = z_ref.at[0], z_ref.at[1]
    sums = frame_ref[12:16, :]
    tables = frame_ref[16:20, :]
    for number, (source, base) in enumerate(((dense_ref, 0), (dense_ref, 3 * ROWS), (g_ref, 0), (dense_ref, ROWS))):
        depths = 4 if number < 3 else 3
        write_frames(source, base, frame_ref, 0, za_ref, zb_ref, depths)
        spare = frame_ref[12:16, :] if number < 3 else sums
        for depth in range(3):
            rows = pack_line(frame_ref[4 * depth : 4 * depth + 4, :], spare, depth)
            if number == 3 and depth == 2:
                rows = jnp.where(lax.broadcasted_iota(I32, (4, LANES), 1) >= 104, tables, rows)
            at = 12 * number + 4 * depth
            blk_ref[at : at + 4, :] = rows


def partner(exchange, me):
    stride, odd = exchange
    if not odd:
        return me ^ stride
    return jnp.where(((me // stride) & 1) == 1, me + stride, me - stride)


def pick(exchanges, me, neighbour, lines_of):
    value = lines_of(0)
    for number in range(1, len(exchanges)):
        value = jnp.where(neighbour == partner(exchanges[number], me), lines_of(number), value)
    return value


def seam_index(flag):
    lane = lanes8()
    return jnp.where((flag & 1) == 1, SIDE - 1 - lane, lane) & 127


def block_rows(refs, places, first, size):
    for ref, held in zip(refs, places):
        for number, position in enumerate(held):
            at = number * BLOCK + first
            yield position, ref[at : at + size, :]


def gather_lines(p, lines):
    high = lines.astype(jnp.bfloat16)
    rest = lines - high.astype(F32)
    middle = rest.astype(jnp.bfloat16)
    low = (rest - middle.astype(F32)).astype(jnp.bfloat16)
    out = jnp.dot(p, high, preferred_element_type=F32)
    out = out + jnp.dot(p, middle, preferred_element_type=F32)
    return out + jnp.dot(p, low, preferred_element_type=F32)


def ends(x, low, high, low_parity, high_parity, depth):
    lane = lax.broadcasted_iota(I32, x.shape, 1)
    low_end = take(low, jnp.where(low_parity == 1, SIDE - 1 - depth, depth))
    high_end = take(high, jnp.where(high_parity == 1, SIDE - 1 - depth, depth))
    return (
        jnp.where(lane == 0, low_end, pltpu.roll(x, 1, 1)),
        jnp.where(lane == SIDE - 1, high_end, pltpu.roll(x, LANES - 1, 1)),
    )


def krylov_kernel(places, lines, me_ref, dense_ref, *rest):
    refs = rest[: len(places)]
    va_ref, vb_ref, line_ref, gram_ref = rest[len(places) : len(places) + 4]
    p_ref, index_ref, frame_ref, wet_ref, d_ref, x_ref = rest[len(places) + 4 :]
    me = me_ref[0]

    def collect(out, first):
        for position, rows in block_rows(refs, places, first, 4):
            out[position * 4 : position * 4 + 4, :] = rows

    for depth in range(3):
        collect(x_ref.at[depth], 4 * depth)
        collect(x_ref.at[4 + depth], 12 + 4 * depth)
        collect(wet_ref.at[depth], 24 + 4 * depth)
        collect(d_ref.at[depth], 36 + 4 * depth)
    x_ref[3] = unpack_line(x_ref[0], x_ref[1], x_ref[2])
    x_ref[7] = unpack_line(x_ref[4], x_ref[5], x_ref[6])
    wet_ref[3] = unpack_line(wet_ref[0], wet_ref[1], wet_ref[2])
    shared = unpack_line(d_ref[0], d_ref[1], d_ref[2])
    lane = lax.broadcasted_iota(I32, (lines, LANES), 1)
    line = lax.broadcasted_iota(I32, (lines, LANES), 0)
    odd = line & 1
    column = lax.broadcasted_iota(I32, (lines, lines), 1)
    line_of = lax.broadcasted_iota(I32, (lines, lines), 0)
    for number in range(3):
        tile = d_ref[2, :, 104 + 2 * number : 105 + 2 * number].astype(I32)
        flag = d_ref[2, :, 105 + 2 * number : 106 + 2 * number].astype(I32)
        at = jnp.where(tile >= 0, 4 * (tile ^ me) + (flag >> 1), -1)
        p = jnp.where(jnp.broadcast_to(at, (lines, lines)) == column, 1.0, 0.0)
        p_ref[number * lines : (number + 1) * lines, :] = p.astype(jnp.bfloat16)
        parity = jnp.broadcast_to(flag & 1, (lines, LANES))
        if number == 0:
            index_ref[0:lines, :] = jnp.where(parity == 1, SIDE - 1 - lane, lane) & 127
        else:
            index_ref[number * lines : (number + 1) * lines, :] = parity ^ odd
    first_half = (line_of & 2) == 0
    for number in range(2):
        at = (line_of & -4) + jnp.where(first_half, 2, 0) + number
        p = jnp.where(at == column, 1.0, 0.0)
        p_ref[(3 + number) * lines : (4 + number) * lines, :] = p.astype(jnp.bfloat16)
    p = p_ref[0 : 3 * lines, :]
    facing_at = index_ref[0:lines, :]
    low_parity = index_ref[lines : 2 * lines, :]
    high_parity = index_ref[2 * lines : 3 * lines, :]
    wet = [wet_ref[depth] for depth in range(4)]
    met = gather_lines(p, wet[0])
    facing = take(met[0:lines], facing_at)
    for depth in range(3):
        low, high = ends(
            wet[depth], met[lines : 2 * lines], met[2 * lines : 3 * lines], low_parity, high_parity, depth
        )
        masks = [
            wet[depth] * (facing if depth == 0 else wet[depth - 1]),
            wet[depth] * wet[depth + 1],
            wet[depth] * low,
            wet[depth] * high,
        ]
        frame_ref[depth, 0] = d_ref[depth] + ((masks[0] + masks[1]) + (masks[2] + masks[3]))
        for number in range(4):
            frame_ref[depth, 1 + number] = masks[number]
        if depth == 0:
            seam = masks[0][0:8]
    gain = take(gather_lines(p_ref[0:lines, :], shared), facing_at) - shared
    moved = gather_lines(p_ref[3 * lines : 5 * lines, :], gain)
    zero_line = jnp.zeros((lines, LANES), F32)
    for depth in range(4):
        end = jnp.where(odd == 1, SIDE - 1 - depth, depth)
        extra = jnp.where(lane == 0, take(moved[0:lines], end), zero_line)
        extra = extra + jnp.where(lane == SIDE - 1, take(moved[lines : 2 * lines], end), zero_line)
        if depth == 0:
            extra = extra + gain
        x_ref[4 + depth] = x_ref[4 + depth] + extra
    surface = jnp.minimum(dense_ref[2 * ROWS : 3 * ROWS, :], 1.0)
    along, across = interior_reach(surface)
    degree = (along + behind(along, 1)) + (across + behind(across, SIDE))
    masks = scatter_masks()
    diagonal = dense_ref[ROWS : 2 * ROWS, :] + (degree + scatter_lines(masks, seam))
    scale = 2.0 / CENTRE
    row, lane, cell, i, j = grid_iotas()
    inside = cell < CELLS
    forcing = dense_ref[3 * ROWS : 4 * ROWS, :] + scatter_lines(masks, gain[0:8])
    va_ref[0] = forcing
    vb_ref[0] = dense_ref[0:ROWS, :]
    frames = [[[x_ref[4 * solve + depth] for depth in range(4)]] for solve in range(2)]
    own = [[dense_ref[0:ROWS, :]], [forcing]]
    for step in range(ITERS):
        for solve in range(2):
            x = frames[solve][-1]
            met = gather_lines(p, x[0])
            facing = take(met[0:lines], facing_at)
            if solve == 0:
                line_ref[step] = facing[0:8]
            mine = own[solve][-1]
            flow = (along * ahead(mine, 1) + behind(along * mine, 1)) + (
                across * ahead(mine, SIDE) + behind(across * mine, SIDE)
            )
            image = diagonal * mine - flow - scatter_lines(masks, seam * facing[0:8])
            image = jnp.where(inside, scale * image - 2.0 * mine, 0.0)
            own[solve].append(0.5 * image if step == 0 else image - own[solve][-2])
            following = []
            for depth in range(ITERS - 1 - step):
                low, high = ends(
                    x[depth],
                    met[lines : 2 * lines],
                    met[2 * lines : 3 * lines],
                    low_parity,
                    high_parity,
                    depth,
                )
                before = facing if depth == 0 else x[depth - 1]
                flow = (frame_ref[depth, 1] * before + frame_ref[depth, 2] * x[depth + 1]) + (
                    frame_ref[depth, 3] * low + frame_ref[depth, 4] * high
                )
                image = scale * (frame_ref[depth, 0] * x[depth] - flow) - 2.0 * x[depth]
                following.append(0.5 * image if step == 0 else image - frames[solve][-2][depth])
            frames[solve].append(following)
            if step < ITERS - 1:
                (vb_ref if solve == 0 else va_ref)[step + 1] = own[solve][-1]
    gram_ref[30:32, :] = jnp.zeros((2, LANES), F32)
    for solve in range(2):
        at = solve
        for first in range(ITERS + 1):
            for second in range(first + 1):
                gram_ref[at : at + 1, :] = jnp.sum(own[solve][first] * own[solve][second], axis=0, keepdims=True)
                at += 2


def image_of(p):
    out = [None] * (len(p) + 1)

    def add(at, value):
        out[at] = value if out[at] is None else out[at] + value

    for at, value in enumerate(p):
        add(at, CENTRE * value)
        if at == 0:
            add(1, CENTRE * value)
        else:
            add(at + 1, 0.5 * CENTRE * value)
            add(at - 1, 0.5 * CENTRE * value)
    return out


def form(left, gram, right):
    total = None
    for first, x in enumerate(left):
        inner = None
        for second, y in enumerate(right):
            term = gram[max(first, second)][min(first, second)] * y
            inner = term if inner is None else inner + term
        total = x * inner if total is None else total + x * inner
    return total


def total_gram(refs, sum_ref):
    total = refs[0][...]
    for ref in refs[1:]:
        total = total + ref[...]
    sum_ref[...] = jnp.broadcast_to(jnp.sum(total, axis=1, keepdims=True), sum_ref.shape)


def coefficients(sum_ref):
    gram = []
    at = 0
    for first in range(ITERS + 1):
        gram.append([sum_ref[at + 2 * second : at + 2 * second + 2, :] for second in range(first + 1)])
        at += 2 * (first + 1)
    one = jnp.ones((2, LANES), F32)
    x = []
    r = [one]
    p = [one]
    rr = gram[0][0]
    for step in range(ITERS):
        image = image_of(p)
        curve = form(p, gram, image)
        alpha = jnp.where(curve > 0.0, rr / curve, 0.0)
        x = [x[n] + alpha * p[n] if n < len(x) else alpha * p[n] for n in range(len(p))]
        r = [r[n] - alpha * image[n] if n < len(r) else -alpha * image[n] for n in range(len(image))]
        if step < ITERS - 1:
            new = jnp.maximum(form(r, gram, r), 0.0)
            beta = jnp.where(rr > 0.0, new / rr, 0.0)
            p = [r[n] + beta * p[n] if n < len(p) else r[n] for n in range(len(r))]
            rr = new
    return x


def store_rows(ref, rows):
    last = CELLS // LANES
    ref[:, 0 : last * LANES] = rows[0:last].reshape(1, last * LANES)
    ref[:, last * LANES : CELLS] = rows[last : last + 1, 0 : CELLS - last * LANES]


def combine(x, v_ref):
    out = x[0] * v_ref[0]
    for number in range(1, ITERS):
        out = out + x[number] * v_ref[number]
    return out


def gradient_kernel(exchanges, levels, grams, me_ref, adj_ref, flag_ref, *rest):
    gram_refs = rest[:grams]
    rest = rest[grams:]
    dense_ref, va_ref, v_ref, line_ref, reach_ref, a_ref, q_ref, as_ref = rest[:8]
    refs = rest[8 : 8 + len(exchanges)]
    height_ref, out_ref, gram_ref, sum_ref, w_ref, h_ref = rest[8 + len(exchanges) :]
    me = me_ref[0]
    total_gram(gram_refs, gram_ref)
    both = coefficients(gram_ref)
    store_rows(height_ref, combine([x[1:2] for x in both], va_ref))
    x = [x[0:1] for x in both]
    level_scale = 1.0 / math.sqrt(levels)
    adjoint = combine(x, v_ref) * level_scale
    met_line = x[0] * line_ref[0]
    depth = dense_ref[2 * ROWS : 3 * ROWS, :]
    along, across = interior_reach(depth)
    sum_ref[0:8, :] = met_line + x[1] * line_ref[1] + x[2] * line_ref[2] + x[3] * line_ref[3]
    h_ref[0:ROWS, :] = adjoint
    w_ref[4, 8:9, :] = h_ref[0:1, :]
    w_ref[4, 9:10, :] = row_line(h_ref, 0, (SIDE - 1) * SIDE)
    row, lane, cell, i, j = grid_iotas()
    column = (j == 0) | (j == SIDE - 1)
    zero = jnp.zeros((ROWS, LANES), F32)
    za = jnp.sum(jnp.where(column & (i < 64), adjoint, zero), axis=0, keepdims=True)
    zb = jnp.sum(jnp.where(column & (i >= 64), adjoint, zero), axis=0, keepdims=True)
    side2, side3 = lines_23(jnp.broadcast_to(za, (8, LANES)), jnp.broadcast_to(zb, (8, LANES)), 0)
    w_ref[4, 10:11, :] = side2[0:1]
    w_ref[4, 11:12, :] = side3[0:1]
    level = lax.broadcasted_iota(I32, (32, LANES), 0).astype(F32)
    fluxes = []
    for side in range(4):
        neighbour = adj_ref[0, side]
        flag = flag_ref[0, side]
        index = seam_index(flag)
        other = take(pick(exchanges, me, neighbour, lambda n: refs[n][flag >> 1]), index)
        other = other + sum_ref[side : side + 1, :] * level_scale
        own = as_ref[side] + w_ref[4, 8 + side : 9 + side, :]
        fluxes.append(jnp.where(reach_ref[side : side + 1, :] > level, other - own, 0.0))
    wa, wb, w1 = spread_lines(fluxes[2], fluxes[3], fluxes[1])
    w_ref[0] = wa
    w_ref[1] = wb
    w_ref[2] = fluxes[0]
    w_ref[3] = w1
    masks = scatter_masks()

    along_back, across_back = behind(along, 1), behind(across, SIDE)
    h_ref[0:ROWS, :] = along
    h_ref[ROWS : 2 * ROWS, :] = across
    h_ref[2 * ROWS : 3 * ROWS, :] = along_back
    h_ref[3 * ROWS : 4 * ROWS, :] = across_back
    for number, step in enumerate((ahead(adjoint, 1), ahead(adjoint, SIDE), behind(adjoint, 1), behind(adjoint, SIDE))):
        h_ref[(4 + number) * ROWS : (5 + number) * ROWS, :] = step - adjoint

    def per_level(number, carry):
        at = pl.ds(pl.multiple_of(number * ROWS, ROWS), ROWS)
        here = pl.ds(number, 1)
        floor = number.astype(F32)
        spread = scatter_rows(
            masks, w_ref[0, here, :], w_ref[1, here, :], w_ref[2, here, :], w_ref[3, here, :]
        )
        for way in range(4):
            reach = h_ref[way * ROWS : (way + 1) * ROWS, :]
            gain = h_ref[(4 + way) * ROWS : (5 + way) * ROWS, :]
            spread = spread + jnp.where(reach > floor, gain, 0.0)
        store_rows(out_ref.at[number], a_ref[at, :] + adjoint * q_ref[at, :] + SPREAD * spread)
        return carry

    lax.fori_loop(0, levels, per_level, 0, unroll=2)


def interior_kernel(levels, dense_ref, a_ref, out_ref):
    along, across = interior_reach(dense_ref[2 * ROWS : 3 * ROWS, :])

    def per_level(number, carry):
        at = pl.ds(pl.multiple_of(number * ROWS, ROWS), ROWS)
        a = a_ref[at, :]
        out_ref[at, :] = a + SPREAD * interior_spread(a, along, across, number.astype(F32))
        return carry

    lax.fori_loop(0, levels, per_level, 0, unroll=2)


def rounds(tiles):
    out = []
    stride = tiles
    while stride > 1:
        radix = 4 if stride >= 16 else 2
        stride //= radix
        out.append((stride, radix))
    return out


def swap(x, tiles, offset):
    return lax.ppermute(x, "tile", [(t, t ^ offset) for t in range(tiles)])


def gather_tiles(block, tiles, beside):
    held = [block]
    places = [(0,)]
    for stride, radix in rounds(tiles):
        whole = held[0] if len(held) == 1 else jnp.concatenate(held, axis=0)
        if stride == 1:
            whole, beside = lax.optimization_barrier((whole, beside))
        covered = tuple(n for place in places for n in place)
        for number in range(1, radix):
            held.append(swap(whole, tiles, number * stride))
            places.append(tuple(n ^ (number * stride) for n in covered))
    return held, tuple(places), beside


def sum_tiles(block, tiles):
    held = [block]
    for stride, radix in rounds(tiles):
        whole = functools.reduce(jnp.add, held)
        held = [whole] + [swap(whole, tiles, number * stride) for number in range(1, radix)]
    return held


def shards(thermal, stirring, depth, adjacent, flags, main_entry, sensitivity, elevation, tiles):
    levels = thermal.shape[1]
    me = lax.axis_index("tile").astype(I32).reshape(1)
    smem = pl.BlockSpec(memory_space=pltpu.SMEM)
    vmem = pl.BlockSpec(memory_space=pltpu.VMEM)

    def shape(*dims):
        return jax.ShapeDtypeStruct(dims, F32)

    hbm = pl.BlockSpec(memory_space=pltpu.HBM)

    def call(kernel, outs, scratch, scalars, arrays, name, flops=1e6, traffic=1e6, far=(), grant=48):
        return pl.pallas_call(
            kernel,
            out_shape=outs,
            in_specs=[smem] * len(scalars) + [vmem] * len(arrays) + [hbm] * len(far),
            out_specs=jax.tree.map(lambda _: vmem, outs),
            scratch_shapes=scratch,
            compiler_params=pltpu.CompilerParams(vmem_limit_bytes=grant * 1024 * 1024),
            cost_estimate=pl.CostEstimate(flops=int(flops), bytes_accessed=int(traffic), transcendentals=0),
            name=name,
        )(*scalars, *arrays, *far)

    exchanges = []
    for stride in (1, ROW_TILES, tiles // 2):
        if (stride, False) not in exchanges and stride < tiles:
            exchanges.append((stride, False))
            if stride < ROW_TILES * 2 and stride * 2 < tiles:
                exchanges.append((stride, True))
    exchanges = tuple(exchanges)

    def to_neighbours(x):
        out = []
        for stride, odd in exchanges:
            if odd:
                pairs = [(t, t + stride if (t // stride) % 2 else t - stride) for t in range(tiles)]
                pairs = [(t, u) for t, u in pairs if 0 <= u < tiles]
            else:
                pairs = [(t, t ^ stride) for t in range(tiles)]
            out.append(lax.ppermute(x, "tile", pairs))
        return out

    def by_level(x):
        return jnp.transpose(x, (1, 0, 2))

    own_depths = call(
        depths_kernel,
        shape(8, LANES),
        [pltpu.VMEM((ROWS, LANES), F32), pltpu.VMEM((2, 8, LANES), F32)],
        (adjacent, flags),
        (depth,),
        "depths",
    )
    depths_met = to_neighbours(own_depths)
    far = pltpu.VMEM((levels, 1, CELLS), F32)
    solved, weight, strips, block, dense, reach = call(
        functools.partial(columns_kernel, exchanges, levels),
        (
            shape(levels * ROWS, LANES),
            shape(levels * ROWS, LANES),
            shape(4, 32, LANES),
            shape(BLOCK, LANES),
            shape(4 * ROWS, LANES),
            shape(8, LANES),
        ),
        [
            far,
            far,
            far,
            pltpu.VMEM((1, CELLS), I32),
            pltpu.VMEM((1, CELLS), F32),
            pltpu.VMEM((1, CELLS), F32),
            pltpu.VMEM((levels * ROWS, LANES), F32),
            pltpu.VMEM((8, 32, LANES), F32),
            pltpu.VMEM((4, 32, LANES), F32),
            pltpu.VMEM((24, LANES), F32),
            pltpu.SemaphoreType.DMA((10,)),
        ],
        (me, adjacent, flags),
        (own_depths, *depths_met),
        "columns",
        2e7,
        8e6,
        tuple(
            pltpu.with_memory_space_constraint(x, pltpu.HBM)
            for x in (
                by_level(stirring),
                by_level(sensitivity),
                by_level(thermal),
                depth,
                main_entry,
                elevation,
            )
        ),
        48,
    )
    inside = call(
        functools.partial(interior_kernel, levels),
        shape(levels * ROWS, LANES),
        [],
        (),
        (dense, solved),
        "interior",
        1e7,
        4e6,
    )
    blocks, places, inside = gather_tiles(block, tiles, inside)
    strips_met = to_neighbours(strips)
    lines = 4 * tiles
    frame = pltpu.VMEM((4, lines, LANES), F32)
    basis = shape(ITERS, ROWS, LANES)
    basis_a, basis_b, lines_b, gram = call(
        functools.partial(krylov_kernel, places, lines),
        (basis, basis, shape(ITERS, 8, LANES), shape(32, LANES)),
        [
            pltpu.VMEM((5 * lines, lines), jnp.bfloat16),
            pltpu.VMEM((3 * lines, LANES), I32),
            pltpu.VMEM((3, 5, lines, LANES), F32),
            frame,
            frame,
            pltpu.VMEM((8, lines, LANES), F32),
        ],
        (me,),
        (dense, *blocks),
        "krylov",
    )
    grams = sum_tiles(gram, tiles)
    height, gradient = call(
        functools.partial(gradient_kernel, exchanges, levels, len(grams)),
        (jax.ShapeDtypeStruct(elevation.shape, F32), shape(levels, 1, CELLS)),
        [
            pltpu.VMEM((32, LANES), F32),
            pltpu.VMEM((16, LANES), F32),
            pltpu.VMEM((5, 32, LANES), F32),
            pltpu.VMEM((8 * ROWS, LANES), F32),
        ],
        (me, adjacent, flags),
        (
            *grams,
            dense,
            basis_a,
            basis_b,
            lines_b,
            reach,
            inside,
            weight,
            strips,
            *strips_met,
        ),
        "gradient",
        1e7,
        4e6,
    )
    gradient = by_level(gradient)
    return height, gradient


def solution(mesh):
    placed = (
        P(("ens", "tile"), None, None),
        P("tile", None, None),
        P("tile", None),
        P("tile", None),
        P("tile", None),
        P("tile", None),
        P(("ens", "tile"), None, None),
        P(("ens", "tile"), None),
    )
    return jax.shard_map(
        functools.partial(shards, tiles=mesh.shape["tile"]),
        mesh=mesh,
        in_specs=placed,
        out_specs=(P(("ens", "tile"), None), P(("ens", "tile"), None, None)),
        check_vma=False,
    )
```

```python
import functools
import math

import jax
import jax.numpy as jnp
from jax import lax
from jax.experimental import pallas as pl
from jax.experimental.pallas import tpu as pltpu
from jax.sharding import PartitionSpec as P

SIDE = 90
CELLS = SIDE * SIDE
ROWS = 64
LANES = 128
ITERS = 4
ROW_TILES = 8
SPREAD = 0.2
CENTRE = 4.1
BLOCK = 48
F32 = jnp.float32
I32 = jnp.int32


def grid_iotas():
    row = lax.broadcasted_iota(I32, (ROWS, LANES), 0)
    lane = lax.broadcasted_iota(I32, (ROWS, LANES), 1)
    cell = row * LANES + lane
    i = (cell * 46604) >> 22
    j = cell - SIDE * i
    return row, lane, cell, i, j


def ahead(x, n):
    lane = lax.broadcasted_iota(I32, x.shape, 1)
    y = pltpu.roll(x, LANES - n, 1)
    return jnp.where(lane < LANES - n, y, pltpu.roll(y, ROWS - 1, 0))


def behind(x, n):
    lane = lax.broadcasted_iota(I32, x.shape, 1)
    y = pltpu.roll(x, n, 1)
    return jnp.where(lane >= n, y, pltpu.roll(y, 1, 0))


def take(x, index):
    pieces = []
    for first in range(0, x.shape[0], 8):
        part = index if index.shape[0] == 8 else index[first : first + 8]
        pieces.append(jnp.take_along_axis(x[first : first + 8], part, axis=1, mode="promise_in_bounds"))
    return pieces[0] if len(pieces) == 1 else jnp.concatenate(pieces, axis=0)


def lanes8():
    return lax.broadcasted_iota(I32, (8, LANES), 1)


def column_owner(lane):
    odd = lane & 1
    half = (lane - 89 * odd) >> 1
    return (37 * half) & 63


def lines_23(za, zb, depth_row):
    lane = lanes8()
    near = (SIDE * lane + depth_row) & 127
    far = (SIDE * lane + SIDE - 1 - depth_row) & 127
    wide = lax.broadcasted_iota(I32, za.shape, 1)
    first = wide < 64
    return (
        jnp.where(first, take(za, near), take(zb, near)),
        jnp.where(first, take(za, far), take(zb, far)),
    )


def spread_lines(side2, side3, side1):
    lane = lanes8()
    owner = column_owner(lane)
    later = (owner + 64) & 127
    even = (lax.broadcasted_iota(I32, side2.shape, 1) & 1) == 0
    wa = jnp.where(even, take(side2, owner), take(side3, owner))
    wb = jnp.where(even, take(side2, later), take(side3, later))
    return wa, wb, pltpu.roll(side1, 74, 1)


def scatter_masks():
    row, lane, cell, i, j = grid_iotas()
    column = (j == 0) | (j == SIDE - 1)
    return (
        column & (i < 64),
        column & (i >= 64) & (i < SIDE),
        cell < SIDE,
        i == SIDE - 1,
    )


def scatter_rows(masks, wa, wb, side0, w1):
    zero = jnp.zeros((ROWS, LANES), F32)
    out = jnp.where(masks[0], wa, zero) + jnp.where(masks[1], wb, zero)
    return out + jnp.where(masks[2], side0, zero) + jnp.where(masks[3], w1, zero)


def scatter_lines(masks, lines):
    wa, wb, w1 = spread_lines(
        jnp.broadcast_to(lines[2:3], (8, LANES)),
        jnp.broadcast_to(lines[3:4], (8, LANES)),
        jnp.broadcast_to(lines[1:2], (8, LANES)),
    )
    return scatter_rows(masks, wa[0:1], wb[0:1], lines[0:1], w1[0:1])


def row_line(ref, base, first_cell):
    row, off = divmod(first_cell, LANES)
    top = ref[pl.ds(base + row, 1), :]
    if off == 0:
        return top
    lane = lax.broadcasted_iota(I32, (1, LANES), 1)
    top = pltpu.roll(top, LANES - off, 1)
    if off + SIDE <= LANES:
        return top
    low = pltpu.roll(ref[pl.ds(base + row + 1, 1), :], LANES - off, 1)
    return jnp.where(lane < LANES - off, top, low)


def write_frames(field_ref, base, out_ref, first_row, za_ref, zb_ref, depths):
    field = field_ref[base : base + ROWS, :]
    row, lane, cell, i, j = grid_iotas()
    za_ref[0:8, :] = jnp.zeros((8, LANES), F32)
    zb_ref[0:8, :] = jnp.zeros((8, LANES), F32)
    for depth in range(depths):
        column = ((j == depth) | (j == SIDE - 1 - depth)) & (i < SIDE)
        za_ref[depth : depth + 1, :] = jnp.sum(
            jnp.where(column & (i < 64), field, 0.0)[0:48], axis=0, keepdims=True
        )
        zb_ref[depth : depth + 1, :] = jnp.sum(
            jnp.where(column & (i >= 64), field, 0.0)[40:ROWS], axis=0, keepdims=True
        )
        at = first_row + depth * 4
        out_ref[at : at + 1, :] = row_line(field_ref, base, depth * SIDE)
        out_ref[at + 1 : at + 2, :] = row_line(field_ref, base, (SIDE - 1 - depth) * SIDE)
    depth_row = lax.broadcasted_iota(I32, (8, LANES), 0) & 3
    side2, side3 = lines_23(za_ref[0:8, :], zb_ref[0:8, :], depth_row)
    for depth in range(depths):
        at = first_row + depth * 4
        out_ref[at + 2 : at + 3, :] = side2[depth : depth + 1]
        out_ref[at + 3 : at + 4, :] = side3[depth : depth + 1]


def pack_line(rows, spare, depth):
    lane = lax.broadcasted_iota(I32, rows.shape, 1)
    return jnp.where(lane < SIDE, rows, pltpu.roll(spare, (SIDE - 38 * depth) % LANES, 1))


def unpack_line(first, second, third):
    lane = lax.broadcasted_iota(I32, first.shape, 1)
    out = jnp.where(lane < 38, pltpu.roll(first, 38, 1), pltpu.roll(second, 76, 1))
    return jnp.where(lane < 76, out, pltpu.roll(third, 114, 1))


def level_rows(ref, level):
    whole = (CELLS // LANES // 8) * 8
    rows = CELLS // LANES
    window = ref[level, :, CELLS - LANES : CELLS]
    return jnp.concatenate(
        [
            ref[level, :, 0 : whole * LANES].reshape(whole, LANES),
            ref[level, :, whole * LANES : rows * LANES].reshape(rows - whole, LANES),
            pltpu.roll(window, CELLS - rows * LANES, 1),
        ],
        axis=0,
    )


def surface_rows(ref):
    whole = (CELLS // LANES // 8) * 8
    rows = CELLS // LANES
    window = ref[:, CELLS - LANES : CELLS]
    return jnp.concatenate(
        [
            ref[:, 0 : whole * LANES].reshape(whole, LANES),
            ref[:, whole * LANES : rows * LANES].reshape(rows - whole, LANES),
            pltpu.roll(window, CELLS - rows * LANES, 1),
        ],
        axis=0,
    )


def interior_reach(depth):
    row, lane, cell, i, j = grid_iotas()
    zero = jnp.zeros_like(depth)
    along = jnp.where(j < SIDE - 1, jnp.minimum(depth, ahead(depth, 1)), zero)
    across = jnp.where(cell < CELLS - SIDE, jnp.minimum(depth, ahead(depth, SIDE)), zero)
    return along, across


def interior_spread(x, along, across, level):
    zero = jnp.zeros_like(x)
    flux1 = jnp.where(along > level, ahead(x, 1) - x, zero)
    flux2 = jnp.where(across > level, ahead(x, SIDE) - x, zero)
    return (flux1 - behind(flux1, 1)) + (flux2 - behind(flux2, SIDE))


def depths_kernel(depth_ref, out_ref, dense_ref, z_ref):
    row, lane, cell, i, j = grid_iotas()
    dense_ref[...] = jnp.where(cell < CELLS, surface_rows(depth_ref).astype(F32), 0.0)
    write_frames(dense_ref, 0, out_ref, 0, z_ref.at[0], z_ref.at[1], 1)
    out_ref[4:8, :] = jnp.zeros((4, LANES), F32)


def columns_kernel(exchanges, levels, me_ref, own_ref, *rest):
    met_refs = rest[: len(exchanges)]
    k_hbm, s_hbm, t_hbm, depth_hbm, d_hbm, b_hbm, adj_hbm, flag_hbm = rest[len(exchanges) : len(exchanges) + 8]
    a_ref, q_ref, as_ref, blk_ref, dense_ref, reach_ref = rest[len(exchanges) + 8 : len(exchanges) + 14]
    k_ref, s_ref, t_ref, depth_ref, d_ref, b_ref, g_ref, z_ref, ts_ref, frame_ref, adj_ref, flag_ref, sems = rest[len(exchanges) + 14 :]
    parts = 3
    third = levels // parts
    surface = [
        pltpu.make_async_copy(source, target, sems.at[number])
        for number, (source, target) in enumerate(((depth_hbm, depth_ref), (b_hbm, b_ref), (d_hbm, d_ref)))
    ]
    for copy in surface:
        copy.start()
    columns = []
    for part in range(parts):
        at = pl.ds(part * third, third if part < parts - 1 else levels - part * third)
        for number, (source, target) in enumerate(((k_hbm, k_ref), (s_hbm, s_ref))):
            columns.append(pltpu.make_async_copy(source.at[at], target.at[at], sems.at[3 + 2 * part + number]))
            columns[-1].start()
    tracer = pltpu.make_async_copy(t_hbm, t_ref, sems.at[3 + 2 * parts])
    tracer.start()
    tables = [
        pltpu.make_async_copy(source, target, sems.at[4 + 2 * parts + number])
        for number, (source, target) in enumerate(((adj_hbm, adj_ref), (flag_hbm, flag_ref)))
    ]
    for copy in tables:
        copy.start()
    me = me_ref[0]
    row, lane, cell, i, j = grid_iotas()
    inside = cell < CELLS
    for number, ref in enumerate((depth_ref, b_ref, d_ref)):
        surface[number].wait()
        place = (2, 0, 1)[number]
        rows = slice(place * ROWS, (place + 1) * ROWS)
        dense_ref[rows, :] = jnp.where(inside, surface_rows(ref).astype(F32), 0.0)
    depth = dense_ref[2 * ROWS : 3 * ROWS, :]
    along, across = interior_reach(depth)
    zero = jnp.zeros((ROWS, LANES), F32)

    def down(level, carry):
        link, below, va, vq = carry
        at = pl.ds(pl.multiple_of(level * ROWS, ROWS), ROWS)
        here = level.astype(F32)
        r = jnp.where(depth > here + 1.0, level_rows(k_ref, level), zero)
        wet = jnp.where(depth > here, 1.0, zero)
        upper = 1.0 + below
        centre = upper + r
        inverse = pl.reciprocal(centre, approx=True)
        inverse = inverse * (2.0 - centre * inverse)
        ratio = r * inverse
        va = (level_rows(s_ref, level) + link * va) * inverse
        vq = (wet + link * vq) * inverse
        g_ref[at, :] = ratio
        a_ref[at, :] = va
        q_ref[at, :] = vq
        return r, upper * ratio, va, vq

    carry = (zero, zero, zero, zero)
    for part in range(parts):
        columns[2 * part].wait()
        columns[2 * part + 1].wait()
        last = (part + 1) * third if part < parts - 1 else levels
        carry = lax.fori_loop(part * third, last, down, carry, unroll=5)
    tracer.wait()
    for copy in tables:
        copy.wait()
    column = ((j == 0) | (j == SIDE - 1)) & (i < SIDE)
    first = (column & (i < 64))[0:48]
    second = (column & (i >= 64))[40:ROWS]

    def up(step, carry):
        xa, xq, total, flux1, flux2 = carry
        level = levels - 1 - step
        here = level.astype(F32)
        at = pl.ds(pl.multiple_of(level * ROWS, ROWS), ROWS)
        ratio = g_ref[at, :]
        xa = a_ref[at, :] + ratio * xa
        xq = q_ref[at, :] + ratio * xq
        a_ref[at, :] = xa
        q_ref[at, :] = xq
        t = level_rows(t_ref, level)
        line = pl.ds(level, 1)
        for number, (x, out) in enumerate(((t, ts_ref), (xa, as_ref))):
            base = number * 4
            z_ref[base, line, :] = jnp.sum(jnp.where(first, x[0:48], 0.0), axis=0, keepdims=True)
            z_ref[base + 1, line, :] = jnp.sum(jnp.where(second, x[40:ROWS], 0.0), axis=0, keepdims=True)
            out[0, line, :] = x[0:1]
            z_ref[base + 2, line, :] = x[ROWS - 2 : ROWS - 1]
            z_ref[base + 3, line, :] = x[ROWS - 1 : ROWS]
        flux1 = flux1 + jnp.where(along > here, xq * (ahead(t, 1) - t), zero)
        flux2 = flux2 + jnp.where(across > here, xq * (ahead(t, SIDE) - t), zero)
        return xa, xq, total + xq * t, flux1, flux2

    xa, xq, total, flux1, flux2 = lax.fori_loop(0, levels, up, (zero,) * 5, unroll=3)
    level_scale = 1.0 / math.sqrt(levels)
    spread = (flux1 - behind(flux1, 1)) + (flux2 - behind(flux2, SIDE))
    dense_ref[3 * ROWS : 4 * ROWS, :] = jnp.where(inside, (total + SPREAD * spread) * level_scale, zero)
    spare = z_ref.shape[1] - levels
    for number, out in enumerate((ts_ref, as_ref)):
        base = number * 4
        for part in range(4):
            z_ref[base + part, levels:, :] = jnp.zeros((spare, LANES), F32)
        out[0, levels:, :] = jnp.zeros((spare, LANES), F32)
        side2, side3 = lines_23(z_ref[base], z_ref[base + 1], 0)
        out[2] = side2
        out[3] = side3
        low, high = z_ref[base + 2], z_ref[base + 3]
        wide = lax.broadcasted_iota(I32, low.shape, 1)
        out[1] = jnp.where(wide < 54, pltpu.roll(low, 54, 1), pltpu.roll(high, 54, 1))
    level = lax.broadcasted_iota(I32, (32, LANES), 0).astype(F32)
    reach_ref[4:8, :] = jnp.zeros((4, LANES), F32)
    for side in range(4):
        neighbour = adj_ref[0, side]
        flag = flag_ref[0, side]
        met = pick(exchanges, me, neighbour, lambda n: met_refs[n][pl.ds(flag >> 1, 1), :])
        met = take(jnp.broadcast_to(met, (8, LANES)), seam_index(flag))[0:1]
        reach = jnp.where(neighbour >= 0, jnp.minimum(met, own_ref[side : side + 1, :]), 0.0)
        reach_ref[side : side + 1, :] = reach
        shared = jnp.sum(jnp.where(reach > level, ts_ref[side], 0.0), axis=0, keepdims=True)
        frame_ref[12 + side : 13 + side, :] = (SPREAD * level_scale) * shared
        table = jnp.zeros((1, LANES), F32)
        where = lax.broadcasted_iota(I32, (1, LANES), 1)
        for number, of in enumerate((side, 2 if side < 2 else 0, 3 if side < 2 else 1)):
            table = jnp.where(where == 104 + 2 * number, adj_ref[0, of].astype(F32), table)
            table = jnp.where(where == 105 + 2 * number, flag_ref[0, of].astype(F32), table)
        frame_ref[16 + side : 17 + side, :] = table
    g_ref[0:ROWS, :] = jnp.minimum(depth, 1.0)
    za_ref, zb_ref = z_ref.at[0], z_ref.at[1]
    sums = frame_ref[12:16, :]
    seams = frame_ref[16:20, :]
    for number, (source, base) in enumerate(((dense_ref, 0), (dense_ref, 3 * ROWS), (g_ref, 0), (dense_ref, ROWS))):
        depths = 4 if number < 3 else 3
        write_frames(source, base, frame_ref, 0, za_ref, zb_ref, depths)
        spare = frame_ref[12:16, :] if number < 3 else sums
        for depth in range(3):
            rows = pack_line(frame_ref[4 * depth : 4 * depth + 4, :], spare, depth)
            if number == 3 and depth == 2:
                rows = jnp.where(lax.broadcasted_iota(I32, (4, LANES), 1) >= 104, seams, rows)
            at = 12 * number + 4 * depth
            blk_ref[at : at + 4, :] = rows


def partner(exchange, me):
    stride, odd = exchange
    if not odd:
        return me ^ stride
    return jnp.where(((me // stride) & 1) == 1, me + stride, me - stride)


def pick(exchanges, me, neighbour, lines_of):
    value = lines_of(0)
    for number in range(1, len(exchanges)):
        value = jnp.where(neighbour == partner(exchanges[number], me), lines_of(number), value)
    return value


def seam_index(flag):
    lane = lanes8()
    return jnp.where((flag & 1) == 1, SIDE - 1 - lane, lane) & 127


def block_rows(refs, places, first, size):
    for ref, held in zip(refs, places):
        for number, position in enumerate(held):
            at = number * BLOCK + first
            yield position, ref[at : at + size, :]


def gather_lines(p, lines):
    high = lines.astype(jnp.bfloat16)
    rest = lines - high.astype(F32)
    middle = rest.astype(jnp.bfloat16)
    low = (rest - middle.astype(F32)).astype(jnp.bfloat16)
    out = jnp.dot(p, high, preferred_element_type=F32)
    out = out + jnp.dot(p, middle, preferred_element_type=F32)
    return out + jnp.dot(p, low, preferred_element_type=F32)


def ends(x, low, high, low_parity, high_parity, depth):
    lane = lax.broadcasted_iota(I32, x.shape, 1)
    low_end = take(low, jnp.where(low_parity == 1, SIDE - 1 - depth, depth))
    high_end = take(high, jnp.where(high_parity == 1, SIDE - 1 - depth, depth))
    return (
        jnp.where(lane == 0, low_end, pltpu.roll(x, 1, 1)),
        jnp.where(lane == SIDE - 1, high_end, pltpu.roll(x, LANES - 1, 1)),
    )


def krylov_kernel(places, lines, me_ref, dense_ref, *rest):
    refs = rest[: len(places)]
    va_ref, vb_ref, line_ref, gram_ref = rest[len(places) : len(places) + 4]
    p_ref, index_ref, frame_ref, wet_ref, d_ref, x_ref = rest[len(places) + 4 :]
    me = me_ref[0]

    def collect(out, first):
        for position, rows in block_rows(refs, places, first, 4):
            out[position * 4 : position * 4 + 4, :] = rows

    for depth in range(3):
        collect(x_ref.at[depth], 4 * depth)
        collect(x_ref.at[4 + depth], 12 + 4 * depth)
        collect(wet_ref.at[depth], 24 + 4 * depth)
        collect(d_ref.at[depth], 36 + 4 * depth)
    x_ref[3] = unpack_line(x_ref[0], x_ref[1], x_ref[2])
    x_ref[7] = unpack_line(x_ref[4], x_ref[5], x_ref[6])
    wet_ref[3] = unpack_line(wet_ref[0], wet_ref[1], wet_ref[2])
    shared = unpack_line(d_ref[0], d_ref[1], d_ref[2])
    lane = lax.broadcasted_iota(I32, (lines, LANES), 1)
    line = lax.broadcasted_iota(I32, (lines, LANES), 0)
    odd = line & 1
    column = lax.broadcasted_iota(I32, (lines, lines), 1)
    line_of = lax.broadcasted_iota(I32, (lines, lines), 0)
    for number in range(3):
        tile = d_ref[2, :, 104 + 2 * number : 105 + 2 * number].astype(I32)
        flag = d_ref[2, :, 105 + 2 * number : 106 + 2 * number].astype(I32)
        at = jnp.where(tile >= 0, 4 * (tile ^ me) + (flag >> 1), -1)
        p = jnp.where(jnp.broadcast_to(at, (lines, lines)) == column, 1.0, 0.0)
        p_ref[number * lines : (number + 1) * lines, :] = p.astype(jnp.bfloat16)
        parity = jnp.broadcast_to(flag & 1, (lines, LANES))
        if number == 0:
            index_ref[0:lines, :] = jnp.where(parity == 1, SIDE - 1 - lane, lane) & 127
        else:
            index_ref[number * lines : (number + 1) * lines, :] = parity ^ odd
    first_half = (line_of & 2) == 0
    for number in range(2):
        at = (line_of & -4) + jnp.where(first_half, 2, 0) + number
        p = jnp.where(at == column, 1.0, 0.0)
        p_ref[(3 + number) * lines : (4 + number) * lines, :] = p.astype(jnp.bfloat16)
    p = p_ref[0 : 3 * lines, :]
    facing_at = index_ref[0:lines, :]
    low_parity = index_ref[lines : 2 * lines, :]
    high_parity = index_ref[2 * lines : 3 * lines, :]
    wet = [wet_ref[depth] for depth in range(4)]
    met = gather_lines(p, wet[0])
    facing = take(met[0:lines], facing_at)
    for depth in range(3):
        low, high = ends(
            wet[depth], met[lines : 2 * lines], met[2 * lines : 3 * lines], low_parity, high_parity, depth
        )
        masks = [
            wet[depth] * (facing if depth == 0 else wet[depth - 1]),
            wet[depth] * wet[depth + 1],
            wet[depth] * low,
            wet[depth] * high,
        ]
        frame_ref[depth, 0] = d_ref[depth] + ((masks[0] + masks[1]) + (masks[2] + masks[3]))
        for number in range(4):
            frame_ref[depth, 1 + number] = masks[number]
        if depth == 0:
            seam = masks[0][0:8]
    gain = take(gather_lines(p_ref[0:lines, :], shared), facing_at) - shared
    moved = gather_lines(p_ref[3 * lines : 5 * lines, :], gain)
    zero_line = jnp.zeros((lines, LANES), F32)
    for depth in range(4):
        end = jnp.where(odd == 1, SIDE - 1 - depth, depth)
        extra = jnp.where(lane == 0, take(moved[0:lines], end), zero_line)
        extra = extra + jnp.where(lane == SIDE - 1, take(moved[lines : 2 * lines], end), zero_line)
        if depth == 0:
            extra = extra + gain
        x_ref[4 + depth] = x_ref[4 + depth] + extra
    surface = jnp.minimum(dense_ref[2 * ROWS : 3 * ROWS, :], 1.0)
    along, across = interior_reach(surface)
    degree = (along + behind(along, 1)) + (across + behind(across, SIDE))
    masks = scatter_masks()
    diagonal = dense_ref[ROWS : 2 * ROWS, :] + (degree + scatter_lines(masks, seam))
    scale = 2.0 / CENTRE
    row, lane, cell, i, j = grid_iotas()
    inside = cell < CELLS
    forcing = dense_ref[3 * ROWS : 4 * ROWS, :] + scatter_lines(masks, gain[0:8])
    va_ref[0] = forcing
    vb_ref[0] = dense_ref[0:ROWS, :]
    frames = [[[x_ref[4 * solve + depth] for depth in range(4)]] for solve in range(2)]
    own = [[dense_ref[0:ROWS, :]], [forcing]]
    for step in range(ITERS):
        for solve in range(2):
            x = frames[solve][-1]
            met = gather_lines(p, x[0])
            facing = take(met[0:lines], facing_at)
            if solve == 0:
                line_ref[step] = facing[0:8]
            mine = own[solve][-1]
            flow = (along * ahead(mine, 1) + behind(along * mine, 1)) + (
                across * ahead(mine, SIDE) + behind(across * mine, SIDE)
            )
            image = diagonal * mine - flow - scatter_lines(masks, seam * facing[0:8])
            image = jnp.where(inside, scale * image - 2.0 * mine, 0.0)
            own[solve].append(0.5 * image if step == 0 else image - own[solve][-2])
            following = []
            for depth in range(ITERS - 1 - step):
                low, high = ends(
                    x[depth],
                    met[lines : 2 * lines],
                    met[2 * lines : 3 * lines],
                    low_parity,
                    high_parity,
                    depth,
                )
                before = facing if depth == 0 else x[depth - 1]
                flow = (frame_ref[depth, 1] * before + frame_ref[depth, 2] * x[depth + 1]) + (
                    frame_ref[depth, 3] * low + frame_ref[depth, 4] * high
                )
                image = scale * (frame_ref[depth, 0] * x[depth] - flow) - 2.0 * x[depth]
                following.append(0.5 * image if step == 0 else image - frames[solve][-2][depth])
            frames[solve].append(following)
            if step < ITERS - 1:
                (vb_ref if solve == 0 else va_ref)[step + 1] = own[solve][-1]
    gram_ref[30:32, :] = jnp.zeros((2, LANES), F32)
    for solve in range(2):
        at = solve
        for first in range(ITERS + 1):
            for second in range(first + 1):
                gram_ref[at : at + 1, :] = jnp.sum(own[solve][first] * own[solve][second], axis=0, keepdims=True)
                at += 2


def image_of(p):
    out = [None] * (len(p) + 1)

    def add(at, value):
        out[at] = value if out[at] is None else out[at] + value

    for at, value in enumerate(p):
        add(at, CENTRE * value)
        if at == 0:
            add(1, CENTRE * value)
        else:
            add(at + 1, 0.5 * CENTRE * value)
            add(at - 1, 0.5 * CENTRE * value)
    return out


def form(left, gram, right):
    total = None
    for first, x in enumerate(left):
        inner = None
        for second, y in enumerate(right):
            term = gram[max(first, second)][min(first, second)] * y
            inner = term if inner is None else inner + term
        total = x * inner if total is None else total + x * inner
    return total


def total_gram(refs, sum_ref):
    total = refs[0][...]
    for ref in refs[1:]:
        total = total + ref[...]
    sum_ref[...] = jnp.broadcast_to(jnp.sum(total, axis=1, keepdims=True), sum_ref.shape)


def coefficients(sum_ref):
    gram = []
    at = 0
    for first in range(ITERS + 1):
        gram.append([sum_ref[at + 2 * second : at + 2 * second + 2, :] for second in range(first + 1)])
        at += 2 * (first + 1)
    one = jnp.ones((2, LANES), F32)
    x = []
    r = [one]
    p = [one]
    rr = gram[0][0]
    for step in range(ITERS):
        image = image_of(p)
        curve = form(p, gram, image)
        alpha = jnp.where(curve > 0.0, rr / curve, 0.0)
        x = [x[n] + alpha * p[n] if n < len(x) else alpha * p[n] for n in range(len(p))]
        r = [r[n] - alpha * image[n] if n < len(r) else -alpha * image[n] for n in range(len(image))]
        if step < ITERS - 1:
            new = jnp.maximum(form(r, gram, r), 0.0)
            beta = jnp.where(rr > 0.0, new / rr, 0.0)
            p = [r[n] + beta * p[n] if n < len(p) else r[n] for n in range(len(r))]
            rr = new
    return x


def store_rows(ref, rows):
    last = CELLS // LANES
    ref[:, 0 : last * LANES] = rows[0:last].reshape(1, last * LANES)
    ref[:, last * LANES : CELLS] = rows[last : last + 1, 0 : CELLS - last * LANES]


def combine(x, v_ref):
    out = x[0] * v_ref[0]
    for number in range(1, ITERS):
        out = out + x[number] * v_ref[number]
    return out


def gradient_kernel(exchanges, levels, grams, me_ref, *rest):
    gram_refs = rest[:grams]
    rest = rest[grams:]
    dense_ref, va_ref, v_ref, line_ref, reach_ref, a_ref, q_ref, as_ref = rest[:8]
    refs = rest[8 : 8 + len(exchanges)]
    adj_hbm, flag_hbm, height_ref, out_ref = rest[8 + len(exchanges) : 12 + len(exchanges)]
    gram_ref, sum_ref, w_ref, h_ref, adj_ref, flag_ref, sems = rest[12 + len(exchanges) :]
    tables = [
        pltpu.make_async_copy(source, target, sems.at[number])
        for number, (source, target) in enumerate(((adj_hbm, adj_ref), (flag_hbm, flag_ref)))
    ]
    for copy in tables:
        copy.start()
    me = me_ref[0]
    total_gram(gram_refs, gram_ref)
    both = coefficients(gram_ref)
    store_rows(height_ref, combine([x[1:2] for x in both], va_ref))
    x = [x[0:1] for x in both]
    level_scale = 1.0 / math.sqrt(levels)
    adjoint = combine(x, v_ref) * level_scale
    met_line = x[0] * line_ref[0]
    depth = dense_ref[2 * ROWS : 3 * ROWS, :]
    along, across = interior_reach(depth)
    sum_ref[0:8, :] = met_line + x[1] * line_ref[1] + x[2] * line_ref[2] + x[3] * line_ref[3]
    h_ref[0:ROWS, :] = adjoint
    w_ref[4, 8:9, :] = h_ref[0:1, :]
    w_ref[4, 9:10, :] = row_line(h_ref, 0, (SIDE - 1) * SIDE)
    row, lane, cell, i, j = grid_iotas()
    column = (j == 0) | (j == SIDE - 1)
    zero = jnp.zeros((ROWS, LANES), F32)
    za = jnp.sum(jnp.where(column & (i < 64), adjoint, zero), axis=0, keepdims=True)
    zb = jnp.sum(jnp.where(column & (i >= 64), adjoint, zero), axis=0, keepdims=True)
    side2, side3 = lines_23(jnp.broadcast_to(za, (8, LANES)), jnp.broadcast_to(zb, (8, LANES)), 0)
    w_ref[4, 10:11, :] = side2[0:1]
    w_ref[4, 11:12, :] = side3[0:1]
    level = lax.broadcasted_iota(I32, (32, LANES), 0).astype(F32)
    fluxes = []
    for copy in tables:
        copy.wait()
    for side in range(4):
        neighbour = adj_ref[0, side]
        flag = flag_ref[0, side]
        index = seam_index(flag)
        other = take(pick(exchanges, me, neighbour, lambda n: refs[n][flag >> 1]), index)
        other = other + sum_ref[side : side + 1, :] * level_scale
        own = as_ref[side] + w_ref[4, 8 + side : 9 + side, :]
        fluxes.append(jnp.where(reach_ref[side : side + 1, :] > level, other - own, 0.0))
    wa, wb, w1 = spread_lines(fluxes[2], fluxes[3], fluxes[1])
    w_ref[0] = wa
    w_ref[1] = wb
    w_ref[2] = fluxes[0]
    w_ref[3] = w1
    masks = scatter_masks()

    along_back, across_back = behind(along, 1), behind(across, SIDE)
    h_ref[0:ROWS, :] = along
    h_ref[ROWS : 2 * ROWS, :] = across
    h_ref[2 * ROWS : 3 * ROWS, :] = along_back
    h_ref[3 * ROWS : 4 * ROWS, :] = across_back
    for number, step in enumerate((ahead(adjoint, 1), ahead(adjoint, SIDE), behind(adjoint, 1), behind(adjoint, SIDE))):
        h_ref[(4 + number) * ROWS : (5 + number) * ROWS, :] = step - adjoint

    def per_level(number, carry):
        at = pl.ds(pl.multiple_of(number * ROWS, ROWS), ROWS)
        here = pl.ds(number, 1)
        floor = number.astype(F32)
        spread = scatter_rows(
            masks, w_ref[0, here, :], w_ref[1, here, :], w_ref[2, here, :], w_ref[3, here, :]
        )
        for way in range(4):
            reach = h_ref[way * ROWS : (way + 1) * ROWS, :]
            gain = h_ref[(4 + way) * ROWS : (5 + way) * ROWS, :]
            spread = spread + jnp.where(reach > floor, gain, 0.0)
        store_rows(out_ref.at[number], a_ref[at, :] + adjoint * q_ref[at, :] + SPREAD * spread)
        return carry

    lax.fori_loop(0, levels, per_level, 0, unroll=2)


def interior_kernel(levels, dense_ref, a_ref, out_ref):
    along, across = interior_reach(dense_ref[2 * ROWS : 3 * ROWS, :])

    def per_level(number, carry):
        at = pl.ds(pl.multiple_of(number * ROWS, ROWS), ROWS)
        a = a_ref[at, :]
        out_ref[at, :] = a + SPREAD * interior_spread(a, along, across, number.astype(F32))
        return carry

    lax.fori_loop(0, levels, per_level, 0, unroll=2)


def rounds(tiles):
    out = []
    stride = tiles
    while stride > 1:
        radix = 4 if stride >= 16 else 2
        stride //= radix
        out.append((stride, radix))
    return out


def swap(x, tiles, offset):
    return lax.ppermute(x, "tile", [(t, t ^ offset) for t in range(tiles)])


def gather_tiles(block, tiles, beside):
    held = [block]
    places = [(0,)]
    for stride, radix in rounds(tiles):
        whole = held[0] if len(held) == 1 else jnp.concatenate(held, axis=0)
        if stride == 1:
            whole, beside = lax.optimization_barrier((whole, beside))
        covered = tuple(n for place in places for n in place)
        for number in range(1, radix):
            held.append(swap(whole, tiles, number * stride))
            places.append(tuple(n ^ (number * stride) for n in covered))
    return held, tuple(places), beside


def sum_tiles(block, tiles):
    held = [block]
    for stride, radix in rounds(tiles):
        whole = functools.reduce(jnp.add, held)
        held = [whole] + [swap(whole, tiles, number * stride) for number in range(1, radix)]
    return held


def shards(thermal, stirring, depth, adjacent, flags, main_entry, sensitivity, elevation, tiles):
    levels = thermal.shape[1]
    me = lax.axis_index("tile").astype(I32).reshape(1)
    smem = pl.BlockSpec(memory_space=pltpu.SMEM)
    vmem = pl.BlockSpec(memory_space=pltpu.VMEM)

    def shape(*dims):
        return jax.ShapeDtypeStruct(dims, F32)

    hbm = pl.BlockSpec(memory_space=pltpu.HBM)

    def call(kernel, outs, scratch, scalars, arrays, name, flops=1e6, traffic=1e6, far=(), grant=48):
        return pl.pallas_call(
            kernel,
            out_shape=outs,
            in_specs=[smem] * len(scalars) + [vmem] * len(arrays) + [hbm] * len(far),
            out_specs=jax.tree.map(lambda _: vmem, outs),
            scratch_shapes=scratch,
            compiler_params=pltpu.CompilerParams(vmem_limit_bytes=grant * 1024 * 1024),
            cost_estimate=pl.CostEstimate(flops=int(flops), bytes_accessed=int(traffic), transcendentals=0),
            name=name,
        )(*scalars, *arrays, *far)

    exchanges = []
    for stride in (1, ROW_TILES, tiles // 2):
        if (stride, False) not in exchanges and stride < tiles:
            exchanges.append((stride, False))
            if stride < ROW_TILES * 2 and stride * 2 < tiles:
                exchanges.append((stride, True))
    exchanges = tuple(exchanges)

    def to_neighbours(x):
        out = []
        for stride, odd in exchanges:
            if odd:
                pairs = [(t, t + stride if (t // stride) % 2 else t - stride) for t in range(tiles)]
                pairs = [(t, u) for t, u in pairs if 0 <= u < tiles]
            else:
                pairs = [(t, t ^ stride) for t in range(tiles)]
            out.append(lax.ppermute(x, "tile", pairs))
        return out

    def by_level(x):
        return jnp.transpose(x, (1, 0, 2))

    own_depths = call(
        depths_kernel,
        shape(8, LANES),
        [pltpu.VMEM((ROWS, LANES), F32), pltpu.VMEM((2, 8, LANES), F32)],
        (),
        (depth,),
        "depths",
    )
    depths_met = to_neighbours(own_depths)
    far = pltpu.VMEM((levels, 1, CELLS), F32)
    solved, weight, strips, block, dense, reach = call(
        functools.partial(columns_kernel, exchanges, levels),
        (
            shape(levels * ROWS, LANES),
            shape(levels * ROWS, LANES),
            shape(4, 32, LANES),
            shape(BLOCK, LANES),
            shape(4 * ROWS, LANES),
            shape(8, LANES),
        ),
        [
            far,
            far,
            far,
            pltpu.VMEM((1, CELLS), I32),
            pltpu.VMEM((1, CELLS), F32),
            pltpu.VMEM((1, CELLS), F32),
            pltpu.VMEM((levels * ROWS, LANES), F32),
            pltpu.VMEM((8, 32, LANES), F32),
            pltpu.VMEM((4, 32, LANES), F32),
            pltpu.VMEM((24, LANES), F32),
            pltpu.SMEM((1, 4), I32),
            pltpu.SMEM((1, 4), I32),
            pltpu.SemaphoreType.DMA((12,)),
        ],
        (me,),
        (own_depths, *depths_met),
        "columns",
        2e7,
        8e6,
        tuple(
            pltpu.with_memory_space_constraint(x, pltpu.HBM)
            for x in (
                by_level(stirring),
                by_level(sensitivity),
                by_level(thermal),
                depth,
                main_entry,
                elevation,
                adjacent,
                flags,
            )
        ),
        48,
    )
    inside = call(
        functools.partial(interior_kernel, levels),
        shape(levels * ROWS, LANES),
        [],
        (),
        (dense, solved),
        "interior",
        1e7,
        4e6,
    )
    blocks, places, inside = gather_tiles(block, tiles, inside)
    strips_met = to_neighbours(strips)
    lines = 4 * tiles
    frame = pltpu.VMEM((4, lines, LANES), F32)
    basis = shape(ITERS, ROWS, LANES)
    basis_a, basis_b, lines_b, gram = call(
        functools.partial(krylov_kernel, places, lines),
        (basis, basis, shape(ITERS, 8, LANES), shape(32, LANES)),
        [
            pltpu.VMEM((5 * lines, lines), jnp.bfloat16),
            pltpu.VMEM((3 * lines, LANES), I32),
            pltpu.VMEM((3, 5, lines, LANES), F32),
            frame,
            frame,
            pltpu.VMEM((8, lines, LANES), F32),
        ],
        (me,),
        (dense, *blocks),
        "krylov",
    )
    grams = sum_tiles(gram, tiles)
    height, gradient = call(
        functools.partial(gradient_kernel, exchanges, levels, len(grams)),
        (jax.ShapeDtypeStruct(elevation.shape, F32), shape(levels, 1, CELLS)),
        [
            pltpu.VMEM((32, LANES), F32),
            pltpu.VMEM((16, LANES), F32),
            pltpu.VMEM((5, 32, LANES), F32),
            pltpu.VMEM((8 * ROWS, LANES), F32),
            pltpu.SMEM((1, 4), I32),
            pltpu.SMEM((1, 4), I32),
            pltpu.SemaphoreType.DMA((2,)),
        ],
        (me,),
        (
            *grams,
            dense,
            basis_a,
            basis_b,
            lines_b,
            reach,
            inside,
            weight,
            strips,
            *strips_met,
        ),
        "gradient",
        1e7,
        4e6,
        tuple(pltpu.with_memory_space_constraint(x, pltpu.HBM) for x in (adjacent, flags)),
    )
    gradient = by_level(gradient)
    return height, gradient


def solution(mesh):
    placed = (
        P(("ens", "tile"), None, None),
        P("tile", None, None),
        P("tile", None),
        P("tile", None),
        P("tile", None),
        P("tile", None),
        P(("ens", "tile"), None, None),
        P(("ens", "tile"), None),
    )
    return jax.shard_map(
        functools.partial(shards, tiles=mesh.shape["tile"]),
        mesh=mesh,
        in_specs=placed,
        out_specs=(P(("ens", "tile"), None), P(("ens", "tile"), None, None)),
        check_vma=False,
    )
```

```python
import functools
import math

import jax
import jax.numpy as jnp
from jax import lax
from jax.experimental import pallas as pl
from jax.experimental.pallas import tpu as pltpu
from jax.sharding import PartitionSpec as P

SIDE = 90
CELLS = SIDE * SIDE
ROWS = 64
LANES = 128
ITERS = 4
ROW_TILES = 8
SPREAD = 0.2
CENTRE = 4.1
BLOCK = 48
F32 = jnp.float32
I32 = jnp.int32


def grid_iotas():
    row = lax.broadcasted_iota(I32, (ROWS, LANES), 0)
    lane = lax.broadcasted_iota(I32, (ROWS, LANES), 1)
    cell = row * LANES + lane
    i = (cell * 46604) >> 22
    j = cell - SIDE * i
    return row, lane, cell, i, j


def ahead(x, n):
    lane = lax.broadcasted_iota(I32, x.shape, 1)
    y = pltpu.roll(x, LANES - n, 1)
    return jnp.where(lane < LANES - n, y, pltpu.roll(y, ROWS - 1, 0))


def behind(x, n):
    lane = lax.broadcasted_iota(I32, x.shape, 1)
    y = pltpu.roll(x, n, 1)
    return jnp.where(lane >= n, y, pltpu.roll(y, 1, 0))


def take(x, index):
    pieces = []
    for first in range(0, x.shape[0], 8):
        part = index if index.shape[0] == 8 else index[first : first + 8]
        pieces.append(jnp.take_along_axis(x[first : first + 8], part, axis=1, mode="promise_in_bounds"))
    return pieces[0] if len(pieces) == 1 else jnp.concatenate(pieces, axis=0)


def lanes8():
    return lax.broadcasted_iota(I32, (8, LANES), 1)


def column_owner(lane):
    odd = lane & 1
    half = (lane - 89 * odd) >> 1
    return (37 * half) & 63


def lines_23(za, zb, depth_row):
    lane = lanes8()
    near = (SIDE * lane + depth_row) & 127
    far = (SIDE * lane + SIDE - 1 - depth_row) & 127
    wide = lax.broadcasted_iota(I32, za.shape, 1)
    first = wide < 64
    return (
        jnp.where(first, take(za, near), take(zb, near)),
        jnp.where(first, take(za, far), take(zb, far)),
    )


def spread_lines(side2, side3, side1):
    lane = lanes8()
    owner = column_owner(lane)
    later = (owner + 64) & 127
    even = (lax.broadcasted_iota(I32, side2.shape, 1) & 1) == 0
    wa = jnp.where(even, take(side2, owner), take(side3, owner))
    wb = jnp.where(even, take(side2, later), take(side3, later))
    return wa, wb, pltpu.roll(side1, 74, 1)


def scatter_masks():
    row, lane, cell, i, j = grid_iotas()
    column = (j == 0) | (j == SIDE - 1)
    return (
        column & (i < 64),
        column & (i >= 64) & (i < SIDE),
        cell < SIDE,
        i == SIDE - 1,
    )


def scatter_rows(masks, wa, wb, side0, w1):
    zero = jnp.zeros((ROWS, LANES), F32)
    out = jnp.where(masks[0], wa, zero) + jnp.where(masks[1], wb, zero)
    return out + jnp.where(masks[2], side0, zero) + jnp.where(masks[3], w1, zero)


def scatter_lines(masks, lines):
    wa, wb, w1 = spread_lines(
        jnp.broadcast_to(lines[2:3], (8, LANES)),
        jnp.broadcast_to(lines[3:4], (8, LANES)),
        jnp.broadcast_to(lines[1:2], (8, LANES)),
    )
    return scatter_rows(masks, wa[0:1], wb[0:1], lines[0:1], w1[0:1])


def row_line(ref, base, first_cell):
    row, off = divmod(first_cell, LANES)
    top = ref[pl.ds(base + row, 1), :]
    if off == 0:
        return top
    lane = lax.broadcasted_iota(I32, (1, LANES), 1)
    top = pltpu.roll(top, LANES - off, 1)
    if off + SIDE <= LANES:
        return top
    low = pltpu.roll(ref[pl.ds(base + row + 1, 1), :], LANES - off, 1)
    return jnp.where(lane < LANES - off, top, low)


def write_frames(field_ref, base, out_ref, first_row, za_ref, zb_ref, depths):
    field = field_ref[base : base + ROWS, :]
    row, lane, cell, i, j = grid_iotas()
    za_ref[0:8, :] = jnp.zeros((8, LANES), F32)
    zb_ref[0:8, :] = jnp.zeros((8, LANES), F32)
    for depth in range(depths):
        column = ((j == depth) | (j == SIDE - 1 - depth)) & (i < SIDE)
        za_ref[depth : depth + 1, :] = jnp.sum(
            jnp.where(column & (i < 64), field, 0.0)[0:48], axis=0, keepdims=True
        )
        zb_ref[depth : depth + 1, :] = jnp.sum(
            jnp.where(column & (i >= 64), field, 0.0)[40:ROWS], axis=0, keepdims=True
        )
        at = first_row + depth * 4
        out_ref[at : at + 1, :] = row_line(field_ref, base, depth * SIDE)
        out_ref[at + 1 : at + 2, :] = row_line(field_ref, base, (SIDE - 1 - depth) * SIDE)
    depth_row = lax.broadcasted_iota(I32, (8, LANES), 0) & 3
    side2, side3 = lines_23(za_ref[0:8, :], zb_ref[0:8, :], depth_row)
    for depth in range(depths):
        at = first_row + depth * 4
        out_ref[at + 2 : at + 3, :] = side2[depth : depth + 1]
        out_ref[at + 3 : at + 4, :] = side3[depth : depth + 1]


def pack_line(rows, spare, depth):
    lane = lax.broadcasted_iota(I32, rows.shape, 1)
    return jnp.where(lane < SIDE, rows, pltpu.roll(spare, (SIDE - 38 * depth) % LANES, 1))


def unpack_line(first, second, third):
    lane = lax.broadcasted_iota(I32, first.shape, 1)
    out = jnp.where(lane < 38, pltpu.roll(first, 38, 1), pltpu.roll(second, 76, 1))
    return jnp.where(lane < 76, out, pltpu.roll(third, 114, 1))


def level_rows(ref, level):
    whole = (CELLS // LANES // 8) * 8
    rows = CELLS // LANES
    window = ref[level, :, CELLS - LANES : CELLS]
    return jnp.concatenate(
        [
            ref[level, :, 0 : whole * LANES].reshape(whole, LANES),
            ref[level, :, whole * LANES : rows * LANES].reshape(rows - whole, LANES),
            pltpu.roll(window, CELLS - rows * LANES, 1),
        ],
        axis=0,
    )


def surface_rows(ref):
    whole = (CELLS // LANES // 8) * 8
    rows = CELLS // LANES
    window = ref[:, CELLS - LANES : CELLS]
    return jnp.concatenate(
        [
            ref[:, 0 : whole * LANES].reshape(whole, LANES),
            ref[:, whole * LANES : rows * LANES].reshape(rows - whole, LANES),
            pltpu.roll(window, CELLS - rows * LANES, 1),
        ],
        axis=0,
    )


def interior_reach(depth):
    row, lane, cell, i, j = grid_iotas()
    zero = jnp.zeros_like(depth)
    along = jnp.where(j < SIDE - 1, jnp.minimum(depth, ahead(depth, 1)), zero)
    across = jnp.where(cell < CELLS - SIDE, jnp.minimum(depth, ahead(depth, SIDE)), zero)
    return along, across


def interior_spread(x, along, across, level):
    zero = jnp.zeros_like(x)
    flux1 = jnp.where(along > level, ahead(x, 1) - x, zero)
    flux2 = jnp.where(across > level, ahead(x, SIDE) - x, zero)
    return (flux1 - behind(flux1, 1)) + (flux2 - behind(flux2, SIDE))


def depths_kernel(depth_ref, out_ref, dense_ref, z_ref):
    row, lane, cell, i, j = grid_iotas()
    dense_ref[...] = jnp.where(cell < CELLS, surface_rows(depth_ref).astype(F32), 0.0)
    write_frames(dense_ref, 0, out_ref, 0, z_ref.at[0], z_ref.at[1], 1)
    out_ref[4:8, :] = jnp.zeros((4, LANES), F32)


def columns_kernel(exchanges, levels, me_ref, own_ref, *rest):
    met_refs = rest[: len(exchanges)]
    k_hbm, s_hbm, t_hbm, depth_hbm, d_hbm, b_hbm, adj_hbm, flag_hbm = rest[len(exchanges) : len(exchanges) + 8]
    a_ref, q_ref, as_ref, blk_ref, dense_ref, reach_ref = rest[len(exchanges) + 8 : len(exchanges) + 14]
    k_ref, s_ref, t_ref, depth_ref, d_ref, b_ref, g_ref, z_ref, ts_ref, frame_ref, adj_ref, flag_ref, sems = rest[len(exchanges) + 14 :]
    parts = 3
    third = levels // parts
    surface = [
        pltpu.make_async_copy(source, target, sems.at[number])
        for number, (source, target) in enumerate(((depth_hbm, depth_ref), (b_hbm, b_ref), (d_hbm, d_ref)))
    ]
    for copy in surface:
        copy.start()
    columns = []
    for part in range(parts):
        at = pl.ds(part * third, third if part < parts - 1 else levels - part * third)
        for number, (source, target) in enumerate(((k_hbm, k_ref), (s_hbm, s_ref))):
            columns.append(pltpu.make_async_copy(source.at[at], target.at[at], sems.at[3 + 2 * part + number]))
            columns[-1].start()
    tracer = pltpu.make_async_copy(t_hbm, t_ref, sems.at[3 + 2 * parts])
    tracer.start()
    tables = [
        pltpu.make_async_copy(source, target, sems.at[4 + 2 * parts + number])
        for number, (source, target) in enumerate(((adj_hbm, adj_ref), (flag_hbm, flag_ref)))
    ]
    for copy in tables:
        copy.start()
    me = me_ref[0]
    row, lane, cell, i, j = grid_iotas()
    inside = cell < CELLS
    for number, ref in enumerate((depth_ref, b_ref, d_ref)):
        surface[number].wait()
        place = (2, 0, 1)[number]
        rows = slice(place * ROWS, (place + 1) * ROWS)
        dense_ref[rows, :] = jnp.where(inside, surface_rows(ref).astype(F32), 0.0)
    depth = dense_ref[2 * ROWS : 3 * ROWS, :]
    along, across = interior_reach(depth)
    zero = jnp.zeros((ROWS, LANES), F32)

    def down(level, carry):
        link, below, va, vq = carry
        at = pl.ds(pl.multiple_of(level * ROWS, ROWS), ROWS)
        here = level.astype(F32)
        r = jnp.where(depth > here + 1.0, level_rows(k_ref, level), zero)
        wet = jnp.where(depth > here, 1.0, zero)
        upper = 1.0 + below
        centre = upper + r
        inverse = pl.reciprocal(centre, approx=True)
        inverse = inverse * (2.0 - centre * inverse)
        ratio = r * inverse
        va = (level_rows(s_ref, level) + link * va) * inverse
        vq = (wet + link * vq) * inverse
        g_ref[at, :] = ratio
        a_ref[at, :] = va
        q_ref[at, :] = vq
        return r, upper * ratio, va, vq

    carry = (zero, zero, zero, zero)
    for part in range(parts):
        columns[2 * part].wait()
        columns[2 * part + 1].wait()
        last = (part + 1) * third if part < parts - 1 else levels
        carry = lax.fori_loop(part * third, last, down, carry, unroll=10)
    tracer.wait()
    for copy in tables:
        copy.wait()
    column = ((j == 0) | (j == SIDE - 1)) & (i < SIDE)
    first = (column & (i < 64))[0:48]
    second = (column & (i >= 64))[40:ROWS]

    def up(step, carry):
        xa, xq, total, flux1, flux2 = carry
        level = levels - 1 - step
        here = level.astype(F32)
        at = pl.ds(pl.multiple_of(level * ROWS, ROWS), ROWS)
        ratio = g_ref[at, :]
        xa = a_ref[at, :] + ratio * xa
        xq = q_ref[at, :] + ratio * xq
        a_ref[at, :] = xa
        q_ref[at, :] = xq
        t = level_rows(t_ref, level)
        line = pl.ds(level, 1)
        for number, (x, out) in enumerate(((t, ts_ref), (xa, as_ref))):
            base = number * 4
            z_ref[base, line, :] = jnp.sum(jnp.where(first, x[0:48], 0.0), axis=0, keepdims=True)
            z_ref[base + 1, line, :] = jnp.sum(jnp.where(second, x[40:ROWS], 0.0), axis=0, keepdims=True)
            out[0, line, :] = x[0:1]
            z_ref[base + 2, line, :] = x[ROWS - 2 : ROWS - 1]
            z_ref[base + 3, line, :] = x[ROWS - 1 : ROWS]
        flux1 = flux1 + jnp.where(along > here, xq * (ahead(t, 1) - t), zero)
        flux2 = flux2 + jnp.where(across > here, xq * (ahead(t, SIDE) - t), zero)
        return xa, xq, total + xq * t, flux1, flux2

    xa, xq, total, flux1, flux2 = lax.fori_loop(0, levels, up, (zero,) * 5, unroll=6)
    level_scale = 1.0 / math.sqrt(levels)
    spread = (flux1 - behind(flux1, 1)) + (flux2 - behind(flux2, SIDE))
    dense_ref[3 * ROWS : 4 * ROWS, :] = jnp.where(inside, (total + SPREAD * spread) * level_scale, zero)
    spare = z_ref.shape[1] - levels
    for number, out in enumerate((ts_ref, as_ref)):
        base = number * 4
        for part in range(4):
            z_ref[base + part, levels:, :] = jnp.zeros((spare, LANES), F32)
        out[0, levels:, :] = jnp.zeros((spare, LANES), F32)
        side2, side3 = lines_23(z_ref[base], z_ref[base + 1], 0)
        out[2] = side2
        out[3] = side3
        low, high = z_ref[base + 2], z_ref[base + 3]
        wide = lax.broadcasted_iota(I32, low.shape, 1)
        out[1] = jnp.where(wide < 54, pltpu.roll(low, 54, 1), pltpu.roll(high, 54, 1))
    level = lax.broadcasted_iota(I32, (32, LANES), 0).astype(F32)
    reach_ref[4:8, :] = jnp.zeros((4, LANES), F32)
    for side in range(4):
        neighbour = adj_ref[0, side]
        flag = flag_ref[0, side]
        met = pick(exchanges, me, neighbour, lambda n: met_refs[n][pl.ds(flag >> 1, 1), :])
        met = take(jnp.broadcast_to(met, (8, LANES)), seam_index(flag))[0:1]
        reach = jnp.where(neighbour >= 0, jnp.minimum(met, own_ref[side : side + 1, :]), 0.0)
        reach_ref[side : side + 1, :] = reach
        shared = jnp.sum(jnp.where(reach > level, ts_ref[side], 0.0), axis=0, keepdims=True)
        frame_ref[12 + side : 13 + side, :] = (SPREAD * level_scale) * shared
        table = jnp.zeros((1, LANES), F32)
        where = lax.broadcasted_iota(I32, (1, LANES), 1)
        for number, of in enumerate((side, 2 if side < 2 else 0, 3 if side < 2 else 1)):
            table = jnp.where(where == 104 + 2 * number, adj_ref[0, of].astype(F32), table)
            table = jnp.where(where == 105 + 2 * number, flag_ref[0, of].astype(F32), table)
        frame_ref[16 + side : 17 + side, :] = table
    g_ref[0:ROWS, :] = jnp.minimum(depth, 1.0)
    za_ref, zb_ref = z_ref.at[0], z_ref.at[1]
    sums = frame_ref[12:16, :]
    seams = frame_ref[16:20, :]
    for number, (source, base) in enumerate(((dense_ref, 0), (dense_ref, 3 * ROWS), (g_ref, 0), (dense_ref, ROWS))):
        depths = 4 if number < 3 else 3
        write_frames(source, base, frame_ref, 0, za_ref, zb_ref, depths)
        spare = frame_ref[12:16, :] if number < 3 else sums
        for depth in range(3):
            rows = pack_line(frame_ref[4 * depth : 4 * depth + 4, :], spare, depth)
            if number == 3 and depth == 2:
                rows = jnp.where(lax.broadcasted_iota(I32, (4, LANES), 1) >= 104, seams, rows)
            at = 12 * number + 4 * depth
            blk_ref[at : at + 4, :] = rows


def partner(exchange, me):
    stride, odd = exchange
    if not odd:
        return me ^ stride
    return jnp.where(((me // stride) & 1) == 1, me + stride, me - stride)


def pick(exchanges, me, neighbour, lines_of):
    value = lines_of(0)
    for number in range(1, len(exchanges)):
        value = jnp.where(neighbour == partner(exchanges[number], me), lines_of(number), value)
    return value


def seam_index(flag):
    lane = lanes8()
    return jnp.where((flag & 1) == 1, SIDE - 1 - lane, lane) & 127


def block_rows(refs, places, first, size):
    for ref, held in zip(refs, places):
        for number, position in enumerate(held):
            at = number * BLOCK + first
            yield position, ref[at : at + size, :]


def gather_lines(p, lines):
    high = lines.astype(jnp.bfloat16)
    rest = lines - high.astype(F32)
    middle = rest.astype(jnp.bfloat16)
    low = (rest - middle.astype(F32)).astype(jnp.bfloat16)
    out = jnp.dot(p, high, preferred_element_type=F32)
    out = out + jnp.dot(p, middle, preferred_element_type=F32)
    return out + jnp.dot(p, low, preferred_element_type=F32)


def ends(x, low, high, low_parity, high_parity, depth):
    lane = lax.broadcasted_iota(I32, x.shape, 1)
    low_end = take(low, jnp.where(low_parity == 1, SIDE - 1 - depth, depth))
    high_end = take(high, jnp.where(high_parity == 1, SIDE - 1 - depth, depth))
    return (
        jnp.where(lane == 0, low_end, pltpu.roll(x, 1, 1)),
        jnp.where(lane == SIDE - 1, high_end, pltpu.roll(x, LANES - 1, 1)),
    )


def krylov_kernel(places, lines, me_ref, dense_ref, *rest):
    refs = rest[: len(places)]
    va_ref, vb_ref, line_ref, gram_ref = rest[len(places) : len(places) + 4]
    p_ref, index_ref, frame_ref, wet_ref, d_ref, x_ref = rest[len(places) + 4 :]
    me = me_ref[0]

    def collect(out, first):
        for position, rows in block_rows(refs, places, first, 4):
            out[position * 4 : position * 4 + 4, :] = rows

    for depth in range(3):
        collect(x_ref.at[depth], 4 * depth)
        collect(x_ref.at[4 + depth], 12 + 4 * depth)
        collect(wet_ref.at[depth], 24 + 4 * depth)
        collect(d_ref.at[depth], 36 + 4 * depth)
    x_ref[3] = unpack_line(x_ref[0], x_ref[1], x_ref[2])
    x_ref[7] = unpack_line(x_ref[4], x_ref[5], x_ref[6])
    wet_ref[3] = unpack_line(wet_ref[0], wet_ref[1], wet_ref[2])
    shared = unpack_line(d_ref[0], d_ref[1], d_ref[2])
    lane = lax.broadcasted_iota(I32, (lines, LANES), 1)
    line = lax.broadcasted_iota(I32, (lines, LANES), 0)
    odd = line & 1
    column = lax.broadcasted_iota(I32, (lines, lines), 1)
    line_of = lax.broadcasted_iota(I32, (lines, lines), 0)
    for number in range(3):
        tile = d_ref[2, :, 104 + 2 * number : 105 + 2 * number].astype(I32)
        flag = d_ref[2, :, 105 + 2 * number : 106 + 2 * number].astype(I32)
        at = jnp.where(tile >= 0, 4 * (tile ^ me) + (flag >> 1), -1)
        p = jnp.where(jnp.broadcast_to(at, (lines, lines)) == column, 1.0, 0.0)
        p_ref[number * lines : (number + 1) * lines, :] = p.astype(jnp.bfloat16)
        parity = jnp.broadcast_to(flag & 1, (lines, LANES))
        if number == 0:
            index_ref[0:lines, :] = jnp.where(parity == 1, SIDE - 1 - lane, lane) & 127
        else:
            index_ref[number * lines : (number + 1) * lines, :] = parity ^ odd
    first_half = (line_of & 2) == 0
    for number in range(2):
        at = (line_of & -4) + jnp.where(first_half, 2, 0) + number
        p = jnp.where(at == column, 1.0, 0.0)
        p_ref[(3 + number) * lines : (4 + number) * lines, :] = p.astype(jnp.bfloat16)
    p = p_ref[0 : 3 * lines, :]
    facing_at = index_ref[0:lines, :]
    low_parity = index_ref[lines : 2 * lines, :]
    high_parity = index_ref[2 * lines : 3 * lines, :]
    wet = [wet_ref[depth] for depth in range(4)]
    met = gather_lines(p, wet[0])
    facing = take(met[0:lines], facing_at)
    for depth in range(3):
        low, high = ends(
            wet[depth], met[lines : 2 * lines], met[2 * lines : 3 * lines], low_parity, high_parity, depth
        )
        masks = [
            wet[depth] * (facing if depth == 0 else wet[depth - 1]),
            wet[depth] * wet[depth + 1],
            wet[depth] * low,
            wet[depth] * high,
        ]
        frame_ref[depth, 0] = d_ref[depth] + ((masks[0] + masks[1]) + (masks[2] + masks[3]))
        for number in range(4):
            frame_ref[depth, 1 + number] = masks[number]
        if depth == 0:
            seam = masks[0][0:8]
    gain = take(gather_lines(p_ref[0:lines, :], shared), facing_at) - shared
    moved = gather_lines(p_ref[3 * lines : 5 * lines, :], gain)
    zero_line = jnp.zeros((lines, LANES), F32)
    for depth in range(4):
        end = jnp.where(odd == 1, SIDE - 1 - depth, depth)
        extra = jnp.where(lane == 0, take(moved[0:lines], end), zero_line)
        extra = extra + jnp.where(lane == SIDE - 1, take(moved[lines : 2 * lines], end), zero_line)
        if depth == 0:
            extra = extra + gain
        x_ref[4 + depth] = x_ref[4 + depth] + extra
    surface = jnp.minimum(dense_ref[2 * ROWS : 3 * ROWS, :], 1.0)
    along, across = interior_reach(surface)
    degree = (along + behind(along, 1)) + (across + behind(across, SIDE))
    masks = scatter_masks()
    diagonal = dense_ref[ROWS : 2 * ROWS, :] + (degree + scatter_lines(masks, seam))
    scale = 2.0 / CENTRE
    row, lane, cell, i, j = grid_iotas()
    inside = cell < CELLS
    forcing = dense_ref[3 * ROWS : 4 * ROWS, :] + scatter_lines(masks, gain[0:8])
    va_ref[0] = forcing
    vb_ref[0] = dense_ref[0:ROWS, :]
    frames = [[[x_ref[4 * solve + depth] for depth in range(4)]] for solve in range(2)]
    own = [[dense_ref[0:ROWS, :]], [forcing]]
    for step in range(ITERS):
        for solve in range(2):
            x = frames[solve][-1]
            met = gather_lines(p, x[0])
            facing = take(met[0:lines], facing_at)
            if solve == 0:
                line_ref[step] = facing[0:8]
            mine = own[solve][-1]
            flow = (along * ahead(mine, 1) + behind(along * mine, 1)) + (
                across * ahead(mine, SIDE) + behind(across * mine, SIDE)
            )
            image = diagonal * mine - flow - scatter_lines(masks, seam * facing[0:8])
            image = jnp.where(inside, scale * image - 2.0 * mine, 0.0)
            own[solve].append(0.5 * image if step == 0 else image - own[solve][-2])
            following = []
            for depth in range(ITERS - 1 - step):
                low, high = ends(
                    x[depth],
                    met[lines : 2 * lines],
                    met[2 * lines : 3 * lines],
                    low_parity,
                    high_parity,
                    depth,
                )
                before = facing if depth == 0 else x[depth - 1]
                flow = (frame_ref[depth, 1] * before + frame_ref[depth, 2] * x[depth + 1]) + (
                    frame_ref[depth, 3] * low + frame_ref[depth, 4] * high
                )
                image = scale * (frame_ref[depth, 0] * x[depth] - flow) - 2.0 * x[depth]
                following.append(0.5 * image if step == 0 else image - frames[solve][-2][depth])
            frames[solve].append(following)
            if step < ITERS - 1:
                (vb_ref if solve == 0 else va_ref)[step + 1] = own[solve][-1]
    gram_ref[30:32, :] = jnp.zeros((2, LANES), F32)
    for solve in range(2):
        at = solve
        for first in range(ITERS + 1):
            for second in range(first + 1):
                gram_ref[at : at + 1, :] = jnp.sum(own[solve][first] * own[solve][second], axis=0, keepdims=True)
                at += 2


def image_of(p):
    out = [None] * (len(p) + 1)

    def add(at, value):
        out[at] = value if out[at] is None else out[at] + value

    for at, value in enumerate(p):
        add(at, CENTRE * value)
        if at == 0:
            add(1, CENTRE * value)
        else:
            add(at + 1, 0.5 * CENTRE * value)
            add(at - 1, 0.5 * CENTRE * value)
    return out


def form(left, gram, right):
    total = None
    for first, x in enumerate(left):
        inner = None
        for second, y in enumerate(right):
            term = gram[max(first, second)][min(first, second)] * y
            inner = term if inner is None else inner + term
        total = x * inner if total is None else total + x * inner
    return total


def total_gram(refs, sum_ref):
    total = refs[0][...]
    for ref in refs[1:]:
        total = total + ref[...]
    sum_ref[...] = jnp.broadcast_to(jnp.sum(total, axis=1, keepdims=True), sum_ref.shape)


def coefficients(sum_ref):
    gram = []
    at = 0
    for first in range(ITERS + 1):
        gram.append([sum_ref[at + 2 * second : at + 2 * second + 2, :] for second in range(first + 1)])
        at += 2 * (first + 1)
    one = jnp.ones((2, LANES), F32)
    x = []
    r = [one]
    p = [one]
    rr = gram[0][0]
    for step in range(ITERS):
        image = image_of(p)
        curve = form(p, gram, image)
        alpha = jnp.where(curve > 0.0, rr / curve, 0.0)
        x = [x[n] + alpha * p[n] if n < len(x) else alpha * p[n] for n in range(len(p))]
        r = [r[n] - alpha * image[n] if n < len(r) else -alpha * image[n] for n in range(len(image))]
        if step < ITERS - 1:
            new = jnp.maximum(form(r, gram, r), 0.0)
            beta = jnp.where(rr > 0.0, new / rr, 0.0)
            p = [r[n] + beta * p[n] if n < len(p) else r[n] for n in range(len(r))]
            rr = new
    return x


def store_rows(ref, rows):
    last = CELLS // LANES
    ref[:, 0 : last * LANES] = rows[0:last].reshape(1, last * LANES)
    ref[:, last * LANES : CELLS] = rows[last : last + 1, 0 : CELLS - last * LANES]


def combine(x, v_ref):
    out = x[0] * v_ref[0]
    for number in range(1, ITERS):
        out = out + x[number] * v_ref[number]
    return out


def gradient_kernel(exchanges, levels, grams, me_ref, *rest):
    gram_refs = rest[:grams]
    rest = rest[grams:]
    dense_ref, va_ref, v_ref, line_ref, reach_ref, a_ref, q_ref, as_ref = rest[:8]
    refs = rest[8 : 8 + len(exchanges)]
    adj_hbm, flag_hbm, height_ref, out_ref = rest[8 + len(exchanges) : 12 + len(exchanges)]
    gram_ref, sum_ref, w_ref, h_ref, adj_ref, flag_ref, sems = rest[12 + len(exchanges) :]
    tables = [
        pltpu.make_async_copy(source, target, sems.at[number])
        for number, (source, target) in enumerate(((adj_hbm, adj_ref), (flag_hbm, flag_ref)))
    ]
    for copy in tables:
        copy.start()
    me = me_ref[0]
    total_gram(gram_refs, gram_ref)
    both = coefficients(gram_ref)
    store_rows(height_ref, combine([x[1:2] for x in both], va_ref))
    x = [x[0:1] for x in both]
    level_scale = 1.0 / math.sqrt(levels)
    adjoint = combine(x, v_ref) * level_scale
    met_line = x[0] * line_ref[0]
    depth = dense_ref[2 * ROWS : 3 * ROWS, :]
    along, across = interior_reach(depth)
    sum_ref[0:8, :] = met_line + x[1] * line_ref[1] + x[2] * line_ref[2] + x[3] * line_ref[3]
    h_ref[0:ROWS, :] = adjoint
    w_ref[4, 8:9, :] = h_ref[0:1, :]
    w_ref[4, 9:10, :] = row_line(h_ref, 0, (SIDE - 1) * SIDE)
    row, lane, cell, i, j = grid_iotas()
    column = (j == 0) | (j == SIDE - 1)
    zero = jnp.zeros((ROWS, LANES), F32)
    za = jnp.sum(jnp.where(column & (i < 64), adjoint, zero), axis=0, keepdims=True)
    zb = jnp.sum(jnp.where(column & (i >= 64), adjoint, zero), axis=0, keepdims=True)
    side2, side3 = lines_23(jnp.broadcast_to(za, (8, LANES)), jnp.broadcast_to(zb, (8, LANES)), 0)
    w_ref[4, 10:11, :] = side2[0:1]
    w_ref[4, 11:12, :] = side3[0:1]
    level = lax.broadcasted_iota(I32, (32, LANES), 0).astype(F32)
    fluxes = []
    for copy in tables:
        copy.wait()
    for side in range(4):
        neighbour = adj_ref[0, side]
        flag = flag_ref[0, side]
        index = seam_index(flag)
        other = take(pick(exchanges, me, neighbour, lambda n: refs[n][flag >> 1]), index)
        other = other + sum_ref[side : side + 1, :] * level_scale
        own = as_ref[side] + w_ref[4, 8 + side : 9 + side, :]
        fluxes.append(jnp.where(reach_ref[side : side + 1, :] > level, other - own, 0.0))
    wa, wb, w1 = spread_lines(fluxes[2], fluxes[3], fluxes[1])
    w_ref[0] = wa
    w_ref[1] = wb
    w_ref[2] = fluxes[0]
    w_ref[3] = w1
    masks = scatter_masks()

    along_back, across_back = behind(along, 1), behind(across, SIDE)
    h_ref[0:ROWS, :] = along
    h_ref[ROWS : 2 * ROWS, :] = across
    h_ref[2 * ROWS : 3 * ROWS, :] = along_back
    h_ref[3 * ROWS : 4 * ROWS, :] = across_back
    for number, step in enumerate((ahead(adjoint, 1), ahead(adjoint, SIDE), behind(adjoint, 1), behind(adjoint, SIDE))):
        h_ref[(4 + number) * ROWS : (5 + number) * ROWS, :] = step - adjoint

    def per_level(number, carry):
        at = pl.ds(pl.multiple_of(number * ROWS, ROWS), ROWS)
        here = pl.ds(number, 1)
        floor = number.astype(F32)
        spread = scatter_rows(
            masks, w_ref[0, here, :], w_ref[1, here, :], w_ref[2, here, :], w_ref[3, here, :]
        )
        for way in range(4):
            reach = h_ref[way * ROWS : (way + 1) * ROWS, :]
            gain = h_ref[(4 + way) * ROWS : (5 + way) * ROWS, :]
            spread = spread + jnp.where(reach > floor, gain, 0.0)
        store_rows(out_ref.at[number], a_ref[at, :] + adjoint * q_ref[at, :] + SPREAD * spread)
        return carry

    lax.fori_loop(0, levels, per_level, 0, unroll=5)


def interior_kernel(levels, dense_ref, a_ref, out_ref):
    along, across = interior_reach(dense_ref[2 * ROWS : 3 * ROWS, :])

    def per_level(number, carry):
        at = pl.ds(pl.multiple_of(number * ROWS, ROWS), ROWS)
        a = a_ref[at, :]
        out_ref[at, :] = a + SPREAD * interior_spread(a, along, across, number.astype(F32))
        return carry

    lax.fori_loop(0, levels, per_level, 0, unroll=5)


def rounds(tiles):
    out = []
    stride = tiles
    while stride > 1:
        radix = 4 if stride >= 16 else 2
        stride //= radix
        out.append((stride, radix))
    return out


def swap(x, tiles, offset):
    return lax.ppermute(x, "tile", [(t, t ^ offset) for t in range(tiles)])


def gather_tiles(block, tiles, beside):
    held = [block]
    places = [(0,)]
    for stride, radix in rounds(tiles):
        whole = held[0] if len(held) == 1 else jnp.concatenate(held, axis=0)
        if stride == 1:
            whole, beside = lax.optimization_barrier((whole, beside))
        covered = tuple(n for place in places for n in place)
        for number in range(1, radix):
            held.append(swap(whole, tiles, number * stride))
            places.append(tuple(n ^ (number * stride) for n in covered))
    return held, tuple(places), beside


def sum_tiles(block, tiles):
    held = [block]
    for stride, radix in rounds(tiles):
        whole = functools.reduce(jnp.add, held)
        held = [whole] + [swap(whole, tiles, number * stride) for number in range(1, radix)]
    return held


def shards(thermal, stirring, depth, adjacent, flags, main_entry, sensitivity, elevation, tiles):
    levels = thermal.shape[1]
    me = lax.axis_index("tile").astype(I32).reshape(1)
    smem = pl.BlockSpec(memory_space=pltpu.SMEM)
    vmem = pl.BlockSpec(memory_space=pltpu.VMEM)

    def shape(*dims):
        return jax.ShapeDtypeStruct(dims, F32)

    hbm = pl.BlockSpec(memory_space=pltpu.HBM)

    def call(kernel, outs, scratch, scalars, arrays, name, flops=1e6, traffic=1e6, far=(), grant=48):
        return pl.pallas_call(
            kernel,
            out_shape=outs,
            in_specs=[smem] * len(scalars) + [vmem] * len(arrays) + [hbm] * len(far),
            out_specs=jax.tree.map(lambda _: vmem, outs),
            scratch_shapes=scratch,
            compiler_params=pltpu.CompilerParams(vmem_limit_bytes=grant * 1024 * 1024),
            cost_estimate=pl.CostEstimate(flops=int(flops), bytes_accessed=int(traffic), transcendentals=0),
            name=name,
        )(*scalars, *arrays, *far)

    exchanges = []
    for stride in (1, ROW_TILES, tiles // 2):
        if (stride, False) not in exchanges and stride < tiles:
            exchanges.append((stride, False))
            if stride < ROW_TILES * 2 and stride * 2 < tiles:
                exchanges.append((stride, True))
    exchanges = tuple(exchanges)

    def to_neighbours(x):
        out = []
        for stride, odd in exchanges:
            if odd:
                pairs = [(t, t + stride if (t // stride) % 2 else t - stride) for t in range(tiles)]
                pairs = [(t, u) for t, u in pairs if 0 <= u < tiles]
            else:
                pairs = [(t, t ^ stride) for t in range(tiles)]
            out.append(lax.ppermute(x, "tile", pairs))
        return out

    def by_level(x):
        return jnp.transpose(x, (1, 0, 2))

    own_depths = call(
        depths_kernel,
        shape(8, LANES),
        [pltpu.VMEM((ROWS, LANES), F32), pltpu.VMEM((2, 8, LANES), F32)],
        (),
        (depth,),
        "depths",
    )
    depths_met = to_neighbours(own_depths)
    far = pltpu.VMEM((levels, 1, CELLS), F32)
    solved, weight, strips, block, dense, reach = call(
        functools.partial(columns_kernel, exchanges, levels),
        (
            shape(levels * ROWS, LANES),
            shape(levels * ROWS, LANES),
            shape(4, 32, LANES),
            shape(BLOCK, LANES),
            shape(4 * ROWS, LANES),
            shape(8, LANES),
        ),
        [
            far,
            far,
            far,
            pltpu.VMEM((1, CELLS), I32),
            pltpu.VMEM((1, CELLS), F32),
            pltpu.VMEM((1, CELLS), F32),
            pltpu.VMEM((levels * ROWS, LANES), F32),
            pltpu.VMEM((8, 32, LANES), F32),
            pltpu.VMEM((4, 32, LANES), F32),
            pltpu.VMEM((24, LANES), F32),
            pltpu.SMEM((1, 4), I32),
            pltpu.SMEM((1, 4), I32),
            pltpu.SemaphoreType.DMA((12,)),
        ],
        (me,),
        (own_depths, *depths_met),
        "columns",
        2e7,
        8e6,
        tuple(
            pltpu.with_memory_space_constraint(x, pltpu.HBM)
            for x in (
                by_level(stirring),
                by_level(sensitivity),
                by_level(thermal),
                depth,
                main_entry,
                elevation,
                adjacent,
                flags,
            )
        ),
        48,
    )
    inside = call(
        functools.partial(interior_kernel, levels),
        shape(levels * ROWS, LANES),
        [],
        (),
        (dense, solved),
        "interior",
        1e7,
        4e6,
    )
    blocks, places, inside = gather_tiles(block, tiles, inside)
    strips_met = to_neighbours(strips)
    lines = 4 * tiles
    frame = pltpu.VMEM((4, lines, LANES), F32)
    basis = shape(ITERS, ROWS, LANES)
    basis_a, basis_b, lines_b, gram = call(
        functools.partial(krylov_kernel, places, lines),
        (basis, basis, shape(ITERS, 8, LANES), shape(32, LANES)),
        [
            pltpu.VMEM((5 * lines, lines), jnp.bfloat16),
            pltpu.VMEM((3 * lines, LANES), I32),
            pltpu.VMEM((3, 5, lines, LANES), F32),
            frame,
            frame,
            pltpu.VMEM((8, lines, LANES), F32),
        ],
        (me,),
        (dense, *blocks),
        "krylov",
    )
    grams = sum_tiles(gram, tiles)
    height, gradient = call(
        functools.partial(gradient_kernel, exchanges, levels, len(grams)),
        (jax.ShapeDtypeStruct(elevation.shape, F32), shape(levels, 1, CELLS)),
        [
            pltpu.VMEM((32, LANES), F32),
            pltpu.VMEM((16, LANES), F32),
            pltpu.VMEM((5, 32, LANES), F32),
            pltpu.VMEM((8 * ROWS, LANES), F32),
            pltpu.SMEM((1, 4), I32),
            pltpu.SMEM((1, 4), I32),
            pltpu.SemaphoreType.DMA((2,)),
        ],
        (me,),
        (
            *grams,
            dense,
            basis_a,
            basis_b,
            lines_b,
            reach,
            inside,
            weight,
            strips,
            *strips_met,
        ),
        "gradient",
        1e7,
        4e6,
        tuple(pltpu.with_memory_space_constraint(x, pltpu.HBM) for x in (adjacent, flags)),
    )
    gradient = by_level(gradient)
    return height, gradient


def solution(mesh):
    placed = (
        P(("ens", "tile"), None, None),
        P("tile", None, None),
        P("tile", None),
        P("tile", None),
        P("tile", None),
        P("tile", None),
        P(("ens", "tile"), None, None),
        P(("ens", "tile"), None),
    )
    return jax.shard_map(
        functools.partial(shards, tiles=mesh.shape["tile"]),
        mesh=mesh,
        in_specs=placed,
        out_specs=(P(("ens", "tile"), None), P(("ens", "tile"), None, None)),
        check_vma=False,
    )
```

```python
import functools
import math

import jax
import jax.numpy as jnp
from jax import lax
from jax.experimental import pallas as pl
from jax.experimental.pallas import tpu as pltpu
from jax.sharding import PartitionSpec as P

SIDE = 90
CELLS = SIDE * SIDE
ROWS = 64
LANES = 128
ITERS = 4
ROW_TILES = 8
SPREAD = 0.2
CENTRE = 4.1
BLOCK = 48
F32 = jnp.float32
I32 = jnp.int32


def grid_iotas():
    row = lax.broadcasted_iota(I32, (ROWS, LANES), 0)
    lane = lax.broadcasted_iota(I32, (ROWS, LANES), 1)
    cell = row * LANES + lane
    i = (cell * 46604) >> 22
    j = cell - SIDE * i
    return row, lane, cell, i, j


def ahead(x, n):
    lane = lax.broadcasted_iota(I32, x.shape, 1)
    y = pltpu.roll(x, LANES - n, 1)
    return jnp.where(lane < LANES - n, y, pltpu.roll(y, ROWS - 1, 0))


def behind(x, n):
    lane = lax.broadcasted_iota(I32, x.shape, 1)
    y = pltpu.roll(x, n, 1)
    return jnp.where(lane >= n, y, pltpu.roll(y, 1, 0))


def take(x, index):
    pieces = []
    for first in range(0, x.shape[0], 8):
        part = index if index.shape[0] == 8 else index[first : first + 8]
        pieces.append(jnp.take_along_axis(x[first : first + 8], part, axis=1, mode="promise_in_bounds"))
    return pieces[0] if len(pieces) == 1 else jnp.concatenate(pieces, axis=0)


def lanes8():
    return lax.broadcasted_iota(I32, (8, LANES), 1)


def column_owner(lane):
    odd = lane & 1
    half = (lane - 89 * odd) >> 1
    return (37 * half) & 63


def lines_23(za, zb, depth_row):
    lane = lanes8()
    near = (SIDE * lane + depth_row) & 127
    far = (SIDE * lane + SIDE - 1 - depth_row) & 127
    wide = lax.broadcasted_iota(I32, za.shape, 1)
    first = wide < 64
    return (
        jnp.where(first, take(za, near), take(zb, near)),
        jnp.where(first, take(za, far), take(zb, far)),
    )


def spread_lines(side2, side3, side1):
    lane = lanes8()
    owner = column_owner(lane)
    later = (owner + 64) & 127
    even = (lax.broadcasted_iota(I32, side2.shape, 1) & 1) == 0
    wa = jnp.where(even, take(side2, owner), take(side3, owner))
    wb = jnp.where(even, take(side2, later), take(side3, later))
    return wa, wb, pltpu.roll(side1, 74, 1)


def scatter_masks():
    row, lane, cell, i, j = grid_iotas()
    column = (j == 0) | (j == SIDE - 1)
    return (
        column & (i < 64),
        column & (i >= 64) & (i < SIDE),
        cell < SIDE,
        i == SIDE - 1,
    )


def scatter_rows(masks, wa, wb, side0, w1):
    zero = jnp.zeros((ROWS, LANES), F32)
    out = jnp.where(masks[0], wa, zero) + jnp.where(masks[1], wb, zero)
    return out + jnp.where(masks[2], side0, zero) + jnp.where(masks[3], w1, zero)


def scatter_lines(masks, lines):
    wa, wb, w1 = spread_lines(
        jnp.broadcast_to(lines[2:3], (8, LANES)),
        jnp.broadcast_to(lines[3:4], (8, LANES)),
        jnp.broadcast_to(lines[1:2], (8, LANES)),
    )
    return scatter_rows(masks, wa[0:1], wb[0:1], lines[0:1], w1[0:1])


def row_line(ref, base, first_cell):
    row, off = divmod(first_cell, LANES)
    top = ref[pl.ds(base + row, 1), :]
    if off == 0:
        return top
    lane = lax.broadcasted_iota(I32, (1, LANES), 1)
    top = pltpu.roll(top, LANES - off, 1)
    if off + SIDE <= LANES:
        return top
    low = pltpu.roll(ref[pl.ds(base + row + 1, 1), :], LANES - off, 1)
    return jnp.where(lane < LANES - off, top, low)


def write_frames(field_ref, base, out_ref, first_row, za_ref, zb_ref, depths):
    field = field_ref[base : base + ROWS, :]
    row, lane, cell, i, j = grid_iotas()
    za_ref[0:8, :] = jnp.zeros((8, LANES), F32)
    zb_ref[0:8, :] = jnp.zeros((8, LANES), F32)
    for depth in range(depths):
        column = ((j == depth) | (j == SIDE - 1 - depth)) & (i < SIDE)
        za_ref[depth : depth + 1, :] = jnp.sum(
            jnp.where(column & (i < 64), field, 0.0)[0:48], axis=0, keepdims=True
        )
        zb_ref[depth : depth + 1, :] = jnp.sum(
            jnp.where(column & (i >= 64), field, 0.0)[40:ROWS], axis=0, keepdims=True
        )
        at = first_row + depth * 4
        out_ref[at : at + 1, :] = row_line(field_ref, base, depth * SIDE)
        out_ref[at + 1 : at + 2, :] = row_line(field_ref, base, (SIDE - 1 - depth) * SIDE)
    depth_row = lax.broadcasted_iota(I32, (8, LANES), 0) & 3
    side2, side3 = lines_23(za_ref[0:8, :], zb_ref[0:8, :], depth_row)
    for depth in range(depths):
        at = first_row + depth * 4
        out_ref[at + 2 : at + 3, :] = side2[depth : depth + 1]
        out_ref[at + 3 : at + 4, :] = side3[depth : depth + 1]


def pack_line(rows, spare, depth):
    lane = lax.broadcasted_iota(I32, rows.shape, 1)
    return jnp.where(lane < SIDE, rows, pltpu.roll(spare, (SIDE - 38 * depth) % LANES, 1))


def unpack_line(first, second, third):
    lane = lax.broadcasted_iota(I32, first.shape, 1)
    out = jnp.where(lane < 38, pltpu.roll(first, 38, 1), pltpu.roll(second, 76, 1))
    return jnp.where(lane < 76, out, pltpu.roll(third, 114, 1))


def level_rows(ref, level):
    whole = (CELLS // LANES // 8) * 8
    rows = CELLS // LANES
    window = ref[level, :, CELLS - LANES : CELLS]
    return jnp.concatenate(
        [
            ref[level, :, 0 : whole * LANES].reshape(whole, LANES),
            ref[level, :, whole * LANES : rows * LANES].reshape(rows - whole, LANES),
            pltpu.roll(window, CELLS - rows * LANES, 1),
        ],
        axis=0,
    )


def surface_rows(ref):
    whole = (CELLS // LANES // 8) * 8
    rows = CELLS // LANES
    window = ref[:, CELLS - LANES : CELLS]
    return jnp.concatenate(
        [
            ref[:, 0 : whole * LANES].reshape(whole, LANES),
            ref[:, whole * LANES : rows * LANES].reshape(rows - whole, LANES),
            pltpu.roll(window, CELLS - rows * LANES, 1),
        ],
        axis=0,
    )


def interior_reach(depth):
    row, lane, cell, i, j = grid_iotas()
    zero = jnp.zeros_like(depth)
    along = jnp.where(j < SIDE - 1, jnp.minimum(depth, ahead(depth, 1)), zero)
    across = jnp.where(cell < CELLS - SIDE, jnp.minimum(depth, ahead(depth, SIDE)), zero)
    return along, across


def interior_spread(x, along, across, level):
    zero = jnp.zeros_like(x)
    flux1 = jnp.where(along > level, ahead(x, 1) - x, zero)
    flux2 = jnp.where(across > level, ahead(x, SIDE) - x, zero)
    return (flux1 - behind(flux1, 1)) + (flux2 - behind(flux2, SIDE))


def depths_kernel(depth_ref, out_ref, dense_ref, z_ref):
    row, lane, cell, i, j = grid_iotas()
    dense_ref[...] = jnp.where(cell < CELLS, surface_rows(depth_ref).astype(F32), 0.0)
    write_frames(dense_ref, 0, out_ref, 0, z_ref.at[0], z_ref.at[1], 1)
    out_ref[4:8, :] = jnp.zeros((4, LANES), F32)


def columns_kernel(exchanges, levels, me_ref, own_ref, *rest):
    met_refs = rest[: len(exchanges)]
    k_hbm, s_hbm, t_hbm, depth_hbm, d_hbm, b_hbm, adj_hbm, flag_hbm = rest[len(exchanges) : len(exchanges) + 8]
    a_ref, q_ref, as_ref, blk_ref, dense_ref, reach_ref = rest[len(exchanges) + 8 : len(exchanges) + 14]
    k_ref, s_ref, t_ref, depth_ref, d_ref, b_ref, g_ref, z_ref, ts_ref, frame_ref, adj_ref, flag_ref, sems = rest[len(exchanges) + 14 :]
    parts = 3
    third = levels // parts
    surface = [
        pltpu.make_async_copy(source, target, sems.at[number])
        for number, (source, target) in enumerate(((depth_hbm, depth_ref), (b_hbm, b_ref), (d_hbm, d_ref)))
    ]
    for copy in surface:
        copy.start()
    columns = []
    for part in range(parts):
        at = pl.ds(part * third, third if part < parts - 1 else levels - part * third)
        for number, (source, target) in enumerate(((k_hbm, k_ref), (s_hbm, s_ref))):
            columns.append(pltpu.make_async_copy(source.at[at], target.at[at], sems.at[3 + 2 * part + number]))
            columns[-1].start()
    tracer = pltpu.make_async_copy(t_hbm, t_ref, sems.at[3 + 2 * parts])
    tracer.start()
    tables = [
        pltpu.make_async_copy(source, target, sems.at[4 + 2 * parts + number])
        for number, (source, target) in enumerate(((adj_hbm, adj_ref), (flag_hbm, flag_ref)))
    ]
    for copy in tables:
        copy.start()
    me = me_ref[0]
    row, lane, cell, i, j = grid_iotas()
    inside = cell < CELLS
    for number, ref in enumerate((depth_ref, b_ref, d_ref)):
        surface[number].wait()
        place = (2, 0, 1)[number]
        rows = slice(place * ROWS, (place + 1) * ROWS)
        dense_ref[rows, :] = jnp.where(inside, surface_rows(ref).astype(F32), 0.0)
    depth = dense_ref[2 * ROWS : 3 * ROWS, :]
    along, across = interior_reach(depth)
    zero = jnp.zeros((ROWS, LANES), F32)

    def down(level, carry):
        link, below, va, vq = carry
        at = pl.ds(pl.multiple_of(level * ROWS, ROWS), ROWS)
        here = level.astype(F32)
        r = jnp.where(depth > here + 1.0, level_rows(k_ref, level), zero)
        wet = jnp.where(depth > here, 1.0, zero)
        upper = 1.0 + below
        centre = upper + r
        inverse = pl.reciprocal(centre, approx=True)
        inverse = inverse * (2.0 - centre * inverse)
        ratio = r * inverse
        va = (level_rows(s_ref, level) + link * va) * inverse
        vq = (wet + link * vq) * inverse
        g_ref[at, :] = ratio
        a_ref[at, :] = va
        q_ref[at, :] = vq
        return r, upper * ratio, va, vq

    carry = (zero, zero, zero, zero)
    for part in range(parts):
        columns[2 * part].wait()
        columns[2 * part + 1].wait()
        last = (part + 1) * third if part < parts - 1 else levels
        carry = lax.fori_loop(part * third, last, down, carry, unroll=10)
    tracer.wait()
    for copy in tables:
        copy.wait()
    column = ((j == 0) | (j == SIDE - 1)) & (i < SIDE)
    first = (column & (i < 64))[0:48]
    second = (column & (i >= 64))[40:ROWS]

    def up(step, carry):
        xa, xq, total, flux1, flux2 = carry
        level = levels - 1 - step
        here = level.astype(F32)
        at = pl.ds(pl.multiple_of(level * ROWS, ROWS), ROWS)
        ratio = g_ref[at, :]
        xa = a_ref[at, :] + ratio * xa
        xq = q_ref[at, :] + ratio * xq
        a_ref[at, :] = xa
        q_ref[at, :] = xq
        t = level_rows(t_ref, level)
        line = pl.ds(level, 1)
        for number, (x, out) in enumerate(((t, ts_ref), (xa, as_ref))):
            base = number * 4
            z_ref[base, line, :] = jnp.sum(jnp.where(first, x[0:48], 0.0), axis=0, keepdims=True)
            z_ref[base + 1, line, :] = jnp.sum(jnp.where(second, x[40:ROWS], 0.0), axis=0, keepdims=True)
            out[0, line, :] = x[0:1]
            z_ref[base + 2, line, :] = x[ROWS - 2 : ROWS - 1]
            z_ref[base + 3, line, :] = x[ROWS - 1 : ROWS]
        flux1 = flux1 + jnp.where(along > here, xq * (ahead(t, 1) - t), zero)
        flux2 = flux2 + jnp.where(across > here, xq * (ahead(t, SIDE) - t), zero)
        return xa, xq, total + xq * t, flux1, flux2

    xa, xq, total, flux1, flux2 = lax.fori_loop(0, levels, up, (zero,) * 5, unroll=10)
    level_scale = 1.0 / math.sqrt(levels)
    spread = (flux1 - behind(flux1, 1)) + (flux2 - behind(flux2, SIDE))
    dense_ref[3 * ROWS : 4 * ROWS, :] = jnp.where(inside, (total + SPREAD * spread) * level_scale, zero)
    spare = z_ref.shape[1] - levels
    for number, out in enumerate((ts_ref, as_ref)):
        base = number * 4
        for part in range(4):
            z_ref[base + part, levels:, :] = jnp.zeros((spare, LANES), F32)
        out[0, levels:, :] = jnp.zeros((spare, LANES), F32)
        side2, side3 = lines_23(z_ref[base], z_ref[base + 1], 0)
        out[2] = side2
        out[3] = side3
        low, high = z_ref[base + 2], z_ref[base + 3]
        wide = lax.broadcasted_iota(I32, low.shape, 1)
        out[1] = jnp.where(wide < 54, pltpu.roll(low, 54, 1), pltpu.roll(high, 54, 1))
    level = lax.broadcasted_iota(I32, (32, LANES), 0).astype(F32)
    reach_ref[4:8, :] = jnp.zeros((4, LANES), F32)
    for side in range(4):
        neighbour = adj_ref[0, side]
        flag = flag_ref[0, side]
        met = pick(exchanges, me, neighbour, lambda n: met_refs[n][pl.ds(flag >> 1, 1), :])
        met = take(jnp.broadcast_to(met, (8, LANES)), seam_index(flag))[0:1]
        reach = jnp.where(neighbour >= 0, jnp.minimum(met, own_ref[side : side + 1, :]), 0.0)
        reach_ref[side : side + 1, :] = reach
        shared = jnp.sum(jnp.where(reach > level, ts_ref[side], 0.0), axis=0, keepdims=True)
        frame_ref[12 + side : 13 + side, :] = (SPREAD * level_scale) * shared
        table = jnp.zeros((1, LANES), F32)
        where = lax.broadcasted_iota(I32, (1, LANES), 1)
        for number, of in enumerate((side, 2 if side < 2 else 0, 3 if side < 2 else 1)):
            table = jnp.where(where == 104 + 2 * number, adj_ref[0, of].astype(F32), table)
            table = jnp.where(where == 105 + 2 * number, flag_ref[0, of].astype(F32), table)
        frame_ref[16 + side : 17 + side, :] = table
    g_ref[0:ROWS, :] = jnp.minimum(depth, 1.0)
    za_ref, zb_ref = z_ref.at[0], z_ref.at[1]
    sums = frame_ref[12:16, :]
    seams = frame_ref[16:20, :]
    for number, (source, base) in enumerate(((dense_ref, 0), (dense_ref, 3 * ROWS), (g_ref, 0), (dense_ref, ROWS))):
        depths = 4 if number < 3 else 3
        write_frames(source, base, frame_ref, 0, za_ref, zb_ref, depths)
        spare = frame_ref[12:16, :] if number < 3 else sums
        for depth in range(3):
            rows = pack_line(frame_ref[4 * depth : 4 * depth + 4, :], spare, depth)
            if number == 3 and depth == 2:
                rows = jnp.where(lax.broadcasted_iota(I32, (4, LANES), 1) >= 104, seams, rows)
            at = 12 * number + 4 * depth
            blk_ref[at : at + 4, :] = rows


def partner(exchange, me):
    stride, odd = exchange
    if not odd:
        return me ^ stride
    return jnp.where(((me // stride) & 1) == 1, me + stride, me - stride)


def pick(exchanges, me, neighbour, lines_of):
    value = lines_of(0)
    for number in range(1, len(exchanges)):
        value = jnp.where(neighbour == partner(exchanges[number], me), lines_of(number), value)
    return value


def seam_index(flag):
    lane = lanes8()
    return jnp.where((flag & 1) == 1, SIDE - 1 - lane, lane) & 127


def block_rows(refs, places, first, size):
    for ref, held in zip(refs, places):
        for number, position in enumerate(held):
            at = number * BLOCK + first
            yield position, ref[at : at + size, :]


def gather_lines(p, lines):
    high = lines.astype(jnp.bfloat16)
    rest = lines - high.astype(F32)
    middle = rest.astype(jnp.bfloat16)
    low = (rest - middle.astype(F32)).astype(jnp.bfloat16)
    out = jnp.dot(p, high, preferred_element_type=F32)
    out = out + jnp.dot(p, middle, preferred_element_type=F32)
    return out + jnp.dot(p, low, preferred_element_type=F32)


def ends(x, low, high, low_parity, high_parity, depth):
    lane = lax.broadcasted_iota(I32, x.shape, 1)
    low_end = take(low, jnp.where(low_parity == 1, SIDE - 1 - depth, depth))
    high_end = take(high, jnp.where(high_parity == 1, SIDE - 1 - depth, depth))
    return (
        jnp.where(lane == 0, low_end, pltpu.roll(x, 1, 1)),
        jnp.where(lane == SIDE - 1, high_end, pltpu.roll(x, LANES - 1, 1)),
    )


def krylov_kernel(places, lines, me_ref, dense_ref, *rest):
    refs = rest[: len(places)]
    va_ref, vb_ref, line_ref, gram_ref = rest[len(places) : len(places) + 4]
    p_ref, index_ref, frame_ref, wet_ref, d_ref, x_ref = rest[len(places) + 4 :]
    me = me_ref[0]

    def collect(out, first):
        for position, rows in block_rows(refs, places, first, 4):
            out[position * 4 : position * 4 + 4, :] = rows

    for depth in range(3):
        collect(x_ref.at[depth], 4 * depth)
        collect(x_ref.at[4 + depth], 12 + 4 * depth)
        collect(wet_ref.at[depth], 24 + 4 * depth)
        collect(d_ref.at[depth], 36 + 4 * depth)
    x_ref[3] = unpack_line(x_ref[0], x_ref[1], x_ref[2])
    x_ref[7] = unpack_line(x_ref[4], x_ref[5], x_ref[6])
    wet_ref[3] = unpack_line(wet_ref[0], wet_ref[1], wet_ref[2])
    shared = unpack_line(d_ref[0], d_ref[1], d_ref[2])
    lane = lax.broadcasted_iota(I32, (lines, LANES), 1)
    line = lax.broadcasted_iota(I32, (lines, LANES), 0)
    odd = line & 1
    column = lax.broadcasted_iota(I32, (lines, lines), 1)
    line_of = lax.broadcasted_iota(I32, (lines, lines), 0)
    for number in range(3):
        tile = d_ref[2, :, 104 + 2 * number : 105 + 2 * number].astype(I32)
        flag = d_ref[2, :, 105 + 2 * number : 106 + 2 * number].astype(I32)
        at = jnp.where(tile >= 0, 4 * (tile ^ me) + (flag >> 1), -1)
        p = jnp.where(jnp.broadcast_to(at, (lines, lines)) == column, 1.0, 0.0)
        p_ref[number * lines : (number + 1) * lines, :] = p.astype(jnp.bfloat16)
        parity = jnp.broadcast_to(flag & 1, (lines, LANES))
        if number == 0:
            index_ref[0:lines, :] = jnp.where(parity == 1, SIDE - 1 - lane, lane) & 127
        else:
            index_ref[number * lines : (number + 1) * lines, :] = parity ^ odd
    first_half = (line_of & 2) == 0
    for number in range(2):
        at = (line_of & -4) + jnp.where(first_half, 2, 0) + number
        p = jnp.where(at == column, 1.0, 0.0)
        p_ref[(3 + number) * lines : (4 + number) * lines, :] = p.astype(jnp.bfloat16)
    p = p_ref[0 : 3 * lines, :]
    facing_at = index_ref[0:lines, :]
    low_parity = index_ref[lines : 2 * lines, :]
    high_parity = index_ref[2 * lines : 3 * lines, :]
    wet = [wet_ref[depth] for depth in range(4)]
    met = gather_lines(p, wet[0])
    facing = take(met[0:lines], facing_at)
    for depth in range(3):
        low, high = ends(
            wet[depth], met[lines : 2 * lines], met[2 * lines : 3 * lines], low_parity, high_parity, depth
        )
        masks = [
            wet[depth] * (facing if depth == 0 else wet[depth - 1]),
            wet[depth] * wet[depth + 1],
            wet[depth] * low,
            wet[depth] * high,
        ]
        frame_ref[depth, 0] = d_ref[depth] + ((masks[0] + masks[1]) + (masks[2] + masks[3]))
        for number in range(4):
            frame_ref[depth, 1 + number] = masks[number]
        if depth == 0:
            seam = masks[0][0:8]
    gain = take(gather_lines(p_ref[0:lines, :], shared), facing_at) - shared
    moved = gather_lines(p_ref[3 * lines : 5 * lines, :], gain)
    zero_line = jnp.zeros((lines, LANES), F32)
    for depth in range(4):
        end = jnp.where(odd == 1, SIDE - 1 - depth, depth)
        extra = jnp.where(lane == 0, take(moved[0:lines], end), zero_line)
        extra = extra + jnp.where(lane == SIDE - 1, take(moved[lines : 2 * lines], end), zero_line)
        if depth == 0:
            extra = extra + gain
        x_ref[4 + depth] = x_ref[4 + depth] + extra
    surface = jnp.minimum(dense_ref[2 * ROWS : 3 * ROWS, :], 1.0)
    along, across = interior_reach(surface)
    degree = (along + behind(along, 1)) + (across + behind(across, SIDE))
    masks = scatter_masks()
    diagonal = dense_ref[ROWS : 2 * ROWS, :] + (degree + scatter_lines(masks, seam))
    scale = 2.0 / CENTRE
    row, lane, cell, i, j = grid_iotas()
    inside = cell < CELLS
    forcing = dense_ref[3 * ROWS : 4 * ROWS, :] + scatter_lines(masks, gain[0:8])
    va_ref[0] = forcing
    vb_ref[0] = dense_ref[0:ROWS, :]
    frames = [[[x_ref[4 * solve + depth] for depth in range(4)]] for solve in range(2)]
    own = [[dense_ref[0:ROWS, :]], [forcing]]
    for step in range(ITERS):
        for solve in range(2):
            x = frames[solve][-1]
            met = gather_lines(p, x[0])
            facing = take(met[0:lines], facing_at)
            if solve == 0:
                line_ref[step] = facing[0:8]
            mine = own[solve][-1]
            flow = (along * ahead(mine, 1) + behind(along * mine, 1)) + (
                across * ahead(mine, SIDE) + behind(across * mine, SIDE)
            )
            image = diagonal * mine - flow - scatter_lines(masks, seam * facing[0:8])
            image = jnp.where(inside, scale * image - 2.0 * mine, 0.0)
            own[solve].append(0.5 * image if step == 0 else image - own[solve][-2])
            following = []
            for depth in range(ITERS - 1 - step):
                low, high = ends(
                    x[depth],
                    met[lines : 2 * lines],
                    met[2 * lines : 3 * lines],
                    low_parity,
                    high_parity,
                    depth,
                )
                before = facing if depth == 0 else x[depth - 1]
                flow = (frame_ref[depth, 1] * before + frame_ref[depth, 2] * x[depth + 1]) + (
                    frame_ref[depth, 3] * low + frame_ref[depth, 4] * high
                )
                image = scale * (frame_ref[depth, 0] * x[depth] - flow) - 2.0 * x[depth]
                following.append(0.5 * image if step == 0 else image - frames[solve][-2][depth])
            frames[solve].append(following)
            if step < ITERS - 1:
                (vb_ref if solve == 0 else va_ref)[step + 1] = own[solve][-1]
    gram_ref[30:32, :] = jnp.zeros((2, LANES), F32)
    for solve in range(2):
        at = solve
        for first in range(ITERS + 1):
            for second in range(first + 1):
                gram_ref[at : at + 1, :] = jnp.sum(own[solve][first] * own[solve][second], axis=0, keepdims=True)
                at += 2


def image_of(p):
    out = [None] * (len(p) + 1)

    def add(at, value):
        out[at] = value if out[at] is None else out[at] + value

    for at, value in enumerate(p):
        add(at, CENTRE * value)
        if at == 0:
            add(1, CENTRE * value)
        else:
            add(at + 1, 0.5 * CENTRE * value)
            add(at - 1, 0.5 * CENTRE * value)
    return out


def form(left, gram, right):
    total = None
    for first, x in enumerate(left):
        inner = None
        for second, y in enumerate(right):
            term = gram[max(first, second)][min(first, second)] * y
            inner = term if inner is None else inner + term
        total = x * inner if total is None else total + x * inner
    return total


def total_gram(refs, sum_ref):
    total = refs[0][...]
    for ref in refs[1:]:
        total = total + ref[...]
    sum_ref[...] = jnp.broadcast_to(jnp.sum(total, axis=1, keepdims=True), sum_ref.shape)


def coefficients(sum_ref):
    gram = []
    at = 0
    for first in range(ITERS + 1):
        gram.append([sum_ref[at + 2 * second : at + 2 * second + 2, :] for second in range(first + 1)])
        at += 2 * (first + 1)
    one = jnp.ones((2, LANES), F32)
    x = []
    r = [one]
    p = [one]
    rr = gram[0][0]
    for step in range(ITERS):
        image = image_of(p)
        curve = form(p, gram, image)
        alpha = jnp.where(curve > 0.0, rr / curve, 0.0)
        x = [x[n] + alpha * p[n] if n < len(x) else alpha * p[n] for n in range(len(p))]
        r = [r[n] - alpha * image[n] if n < len(r) else -alpha * image[n] for n in range(len(image))]
        if step < ITERS - 1:
            new = jnp.maximum(form(r, gram, r), 0.0)
            beta = jnp.where(rr > 0.0, new / rr, 0.0)
            p = [r[n] + beta * p[n] if n < len(p) else r[n] for n in range(len(r))]
            rr = new
    return x


def store_rows(ref, rows):
    last = CELLS // LANES
    ref[:, 0 : last * LANES] = rows[0:last].reshape(1, last * LANES)
    ref[:, last * LANES : CELLS] = rows[last : last + 1, 0 : CELLS - last * LANES]


def combine(x, v_ref):
    out = x[0] * v_ref[0]
    for number in range(1, ITERS):
        out = out + x[number] * v_ref[number]
    return out


def gradient_kernel(exchanges, levels, grams, me_ref, *rest):
    gram_refs = rest[:grams]
    rest = rest[grams:]
    dense_ref, va_ref, v_ref, line_ref, reach_ref, a_ref, q_ref, as_ref = rest[:8]
    refs = rest[8 : 8 + len(exchanges)]
    adj_hbm, flag_hbm, height_ref, out_ref = rest[8 + len(exchanges) : 12 + len(exchanges)]
    gram_ref, sum_ref, w_ref, h_ref, adj_ref, flag_ref, sems = rest[12 + len(exchanges) :]
    tables = [
        pltpu.make_async_copy(source, target, sems.at[number])
        for number, (source, target) in enumerate(((adj_hbm, adj_ref), (flag_hbm, flag_ref)))
    ]
    for copy in tables:
        copy.start()
    me = me_ref[0]
    total_gram(gram_refs, gram_ref)
    both = coefficients(gram_ref)
    store_rows(height_ref, combine([x[1:2] for x in both], va_ref))
    x = [x[0:1] for x in both]
    level_scale = 1.0 / math.sqrt(levels)
    adjoint = combine(x, v_ref) * level_scale
    met_line = x[0] * line_ref[0]
    depth = dense_ref[2 * ROWS : 3 * ROWS, :]
    along, across = interior_reach(depth)
    sum_ref[0:8, :] = met_line + x[1] * line_ref[1] + x[2] * line_ref[2] + x[3] * line_ref[3]
    h_ref[0:ROWS, :] = adjoint
    w_ref[4, 8:9, :] = h_ref[0:1, :]
    w_ref[4, 9:10, :] = row_line(h_ref, 0, (SIDE - 1) * SIDE)
    row, lane, cell, i, j = grid_iotas()
    column = (j == 0) | (j == SIDE - 1)
    zero = jnp.zeros((ROWS, LANES), F32)
    za = jnp.sum(jnp.where(column & (i < 64), adjoint, zero), axis=0, keepdims=True)
    zb = jnp.sum(jnp.where(column & (i >= 64), adjoint, zero), axis=0, keepdims=True)
    side2, side3 = lines_23(jnp.broadcast_to(za, (8, LANES)), jnp.broadcast_to(zb, (8, LANES)), 0)
    w_ref[4, 10:11, :] = side2[0:1]
    w_ref[4, 11:12, :] = side3[0:1]
    level = lax.broadcasted_iota(I32, (32, LANES), 0).astype(F32)
    fluxes = []
    for copy in tables:
        copy.wait()
    for side in range(4):
        neighbour = adj_ref[0, side]
        flag = flag_ref[0, side]
        index = seam_index(flag)
        other = take(pick(exchanges, me, neighbour, lambda n: refs[n][flag >> 1]), index)
        other = other + sum_ref[side : side + 1, :] * level_scale
        own = as_ref[side] + w_ref[4, 8 + side : 9 + side, :]
        fluxes.append(jnp.where(reach_ref[side : side + 1, :] > level, other - own, 0.0))
    wa, wb, w1 = spread_lines(fluxes[2], fluxes[3], fluxes[1])
    w_ref[0] = wa
    w_ref[1] = wb
    w_ref[2] = fluxes[0]
    w_ref[3] = w1
    masks = scatter_masks()

    along_back, across_back = behind(along, 1), behind(across, SIDE)
    h_ref[0:ROWS, :] = along
    h_ref[ROWS : 2 * ROWS, :] = across
    h_ref[2 * ROWS : 3 * ROWS, :] = along_back
    h_ref[3 * ROWS : 4 * ROWS, :] = across_back
    for number, step in enumerate((ahead(adjoint, 1), ahead(adjoint, SIDE), behind(adjoint, 1), behind(adjoint, SIDE))):
        h_ref[(4 + number) * ROWS : (5 + number) * ROWS, :] = step - adjoint

    def per_level(number, carry):
        at = pl.ds(pl.multiple_of(number * ROWS, ROWS), ROWS)
        here = pl.ds(number, 1)
        floor = number.astype(F32)
        spread = scatter_rows(
            masks, w_ref[0, here, :], w_ref[1, here, :], w_ref[2, here, :], w_ref[3, here, :]
        )
        for way in range(4):
            reach = h_ref[way * ROWS : (way + 1) * ROWS, :]
            gain = h_ref[(4 + way) * ROWS : (5 + way) * ROWS, :]
            spread = spread + jnp.where(reach > floor, gain, 0.0)
        store_rows(out_ref.at[number], a_ref[at, :] + adjoint * q_ref[at, :] + SPREAD * spread)
        return carry

    lax.fori_loop(0, levels, per_level, 0, unroll=5)


def interior_kernel(levels, dense_ref, a_ref, out_ref):
    along, across = interior_reach(dense_ref[2 * ROWS : 3 * ROWS, :])

    def per_level(number, carry):
        at = pl.ds(pl.multiple_of(number * ROWS, ROWS), ROWS)
        a = a_ref[at, :]
        out_ref[at, :] = a + SPREAD * interior_spread(a, along, across, number.astype(F32))
        return carry

    lax.fori_loop(0, levels, per_level, 0, unroll=5)


def rounds(tiles):
    out = []
    stride = tiles
    while stride > 1:
        radix = 4 if stride >= 16 else 2
        stride //= radix
        out.append((stride, radix))
    return out


def swap(x, tiles, offset):
    return lax.ppermute(x, "tile", [(t, t ^ offset) for t in range(tiles)])


def gather_tiles(block, tiles, beside, strips, to_neighbours):
    held = [block]
    places = [(0,)]
    for stride, radix in rounds(tiles):
        whole = held[0] if len(held) == 1 else jnp.concatenate(held, axis=0)
        if stride == 2:
            whole, strips = lax.optimization_barrier((whole, strips))
            strips_met = to_neighbours(strips)
        if stride == 1:
            whole, beside, strips_met = lax.optimization_barrier((whole, beside, strips_met))
        covered = tuple(n for place in places for n in place)
        for number in range(1, radix):
            held.append(swap(whole, tiles, number * stride))
            places.append(tuple(n ^ (number * stride) for n in covered))
    return held, tuple(places), beside, strips_met


def sum_tiles(block, tiles):
    held = [block]
    for stride, radix in rounds(tiles):
        whole = functools.reduce(jnp.add, held)
        held = [whole] + [swap(whole, tiles, number * stride) for number in range(1, radix)]
    return held


def shards(thermal, stirring, depth, adjacent, flags, main_entry, sensitivity, elevation, tiles):
    levels = thermal.shape[1]
    me = lax.axis_index("tile").astype(I32).reshape(1)
    smem = pl.BlockSpec(memory_space=pltpu.SMEM)
    vmem = pl.BlockSpec(memory_space=pltpu.VMEM)

    def shape(*dims):
        return jax.ShapeDtypeStruct(dims, F32)

    hbm = pl.BlockSpec(memory_space=pltpu.HBM)

    def call(kernel, outs, scratch, scalars, arrays, name, flops=1e6, traffic=1e6, far=(), grant=48):
        return pl.pallas_call(
            kernel,
            out_shape=outs,
            in_specs=[smem] * len(scalars) + [vmem] * len(arrays) + [hbm] * len(far),
            out_specs=jax.tree.map(lambda _: vmem, outs),
            scratch_shapes=scratch,
            compiler_params=pltpu.CompilerParams(vmem_limit_bytes=grant * 1024 * 1024),
            cost_estimate=pl.CostEstimate(flops=int(flops), bytes_accessed=int(traffic), transcendentals=0),
            name=name,
        )(*scalars, *arrays, *far)

    exchanges = []
    for stride in (1, ROW_TILES, tiles // 2):
        if (stride, False) not in exchanges and stride < tiles:
            exchanges.append((stride, False))
            if stride < ROW_TILES * 2 and stride * 2 < tiles:
                exchanges.append((stride, True))
    exchanges = tuple(exchanges)

    def to_neighbours(x):
        out = []
        for stride, odd in exchanges:
            if odd:
                pairs = [(t, t + stride if (t // stride) % 2 else t - stride) for t in range(tiles)]
                pairs = [(t, u) for t, u in pairs if 0 <= u < tiles]
            else:
                pairs = [(t, t ^ stride) for t in range(tiles)]
            out.append(lax.ppermute(x, "tile", pairs))
        return out

    def by_level(x):
        return jnp.transpose(x, (1, 0, 2))

    own_depths = call(
        depths_kernel,
        shape(8, LANES),
        [pltpu.VMEM((ROWS, LANES), F32), pltpu.VMEM((2, 8, LANES), F32)],
        (),
        (depth,),
        "depths",
    )
    depths_met = to_neighbours(own_depths)
    far = pltpu.VMEM((levels, 1, CELLS), F32)
    solved, weight, strips, block, dense, reach = call(
        functools.partial(columns_kernel, exchanges, levels),
        (
            shape(levels * ROWS, LANES),
            shape(levels * ROWS, LANES),
            shape(4, 32, LANES),
            shape(BLOCK, LANES),
            shape(4 * ROWS, LANES),
            shape(8, LANES),
        ),
        [
            far,
            far,
            far,
            pltpu.VMEM((1, CELLS), I32),
            pltpu.VMEM((1, CELLS), F32),
            pltpu.VMEM((1, CELLS), F32),
            pltpu.VMEM((levels * ROWS, LANES), F32),
            pltpu.VMEM((8, 32, LANES), F32),
            pltpu.VMEM((4, 32, LANES), F32),
            pltpu.VMEM((24, LANES), F32),
            pltpu.SMEM((1, 4), I32),
            pltpu.SMEM((1, 4), I32),
            pltpu.SemaphoreType.DMA((12,)),
        ],
        (me,),
        (own_depths, *depths_met),
        "columns",
        2e7,
        8e6,
        tuple(
            pltpu.with_memory_space_constraint(x, pltpu.HBM)
            for x in (
                by_level(stirring),
                by_level(sensitivity),
                by_level(thermal),
                depth,
                main_entry,
                elevation,
                adjacent,
                flags,
            )
        ),
        48,
    )
    inside = call(
        functools.partial(interior_kernel, levels),
        shape(levels * ROWS, LANES),
        [],
        (),
        (dense, solved),
        "interior",
        1e7,
        4e6,
    )
    blocks, places, inside, strips_met = gather_tiles(block, tiles, inside, strips, to_neighbours)
    lines = 4 * tiles
    frame = pltpu.VMEM((4, lines, LANES), F32)
    basis = shape(ITERS, ROWS, LANES)
    basis_a, basis_b, lines_b, gram = call(
        functools.partial(krylov_kernel, places, lines),
        (basis, basis, shape(ITERS, 8, LANES), shape(32, LANES)),
        [
            pltpu.VMEM((5 * lines, lines), jnp.bfloat16),
            pltpu.VMEM((3 * lines, LANES), I32),
            pltpu.VMEM((3, 5, lines, LANES), F32),
            frame,
            frame,
            pltpu.VMEM((8, lines, LANES), F32),
        ],
        (me,),
        (dense, *blocks),
        "krylov",
    )
    grams = sum_tiles(gram, tiles)
    height, gradient = call(
        functools.partial(gradient_kernel, exchanges, levels, len(grams)),
        (jax.ShapeDtypeStruct(elevation.shape, F32), shape(levels, 1, CELLS)),
        [
            pltpu.VMEM((32, LANES), F32),
            pltpu.VMEM((16, LANES), F32),
            pltpu.VMEM((5, 32, LANES), F32),
            pltpu.VMEM((8 * ROWS, LANES), F32),
            pltpu.SMEM((1, 4), I32),
            pltpu.SMEM((1, 4), I32),
            pltpu.SemaphoreType.DMA((2,)),
        ],
        (me,),
        (
            *grams,
            dense,
            basis_a,
            basis_b,
            lines_b,
            reach,
            inside,
            weight,
            strips,
            *strips_met,
        ),
        "gradient",
        1e7,
        4e6,
        tuple(pltpu.with_memory_space_constraint(x, pltpu.HBM) for x in (adjacent, flags)),
    )
    gradient = by_level(gradient)
    return height, gradient


def solution(mesh):
    placed = (
        P(("ens", "tile"), None, None),
        P("tile", None, None),
        P("tile", None),
        P("tile", None),
        P("tile", None),
        P("tile", None),
        P(("ens", "tile"), None, None),
        P(("ens", "tile"), None),
    )
    return jax.shard_map(
        functools.partial(shards, tiles=mesh.shape["tile"]),
        mesh=mesh,
        in_specs=placed,
        out_specs=(P(("ens", "tile"), None), P(("ens", "tile"), None, None)),
        check_vma=False,
    )
```

```python
import functools
import math

import jax
import jax.numpy as jnp
from jax import lax
from jax.experimental import pallas as pl
from jax.experimental.pallas import tpu as pltpu
from jax.sharding import PartitionSpec as P

SIDE = 90
CELLS = SIDE * SIDE
ROWS = 64
LANES = 128
ITERS = 4
ROW_TILES = 8
SPREAD = 0.2
CENTRE = 4.1
BLOCK = 48
F32 = jnp.float32
I32 = jnp.int32


def grid_iotas():
    row = lax.broadcasted_iota(I32, (ROWS, LANES), 0)
    lane = lax.broadcasted_iota(I32, (ROWS, LANES), 1)
    cell = row * LANES + lane
    i = (cell * 46604) >> 22
    j = cell - SIDE * i
    return row, lane, cell, i, j


def ahead(x, n):
    lane = lax.broadcasted_iota(I32, x.shape, 1)
    y = pltpu.roll(x, LANES - n, 1)
    return jnp.where(lane < LANES - n, y, pltpu.roll(y, ROWS - 1, 0))


def behind(x, n):
    lane = lax.broadcasted_iota(I32, x.shape, 1)
    y = pltpu.roll(x, n, 1)
    return jnp.where(lane >= n, y, pltpu.roll(y, 1, 0))


def take(x, index):
    pieces = []
    for first in range(0, x.shape[0], 8):
        part = index if index.shape[0] == 8 else index[first : first + 8]
        pieces.append(jnp.take_along_axis(x[first : first + 8], part, axis=1, mode="promise_in_bounds"))
    return pieces[0] if len(pieces) == 1 else jnp.concatenate(pieces, axis=0)


def lanes8():
    return lax.broadcasted_iota(I32, (8, LANES), 1)


def column_owner(lane):
    odd = lane & 1
    half = (lane - 89 * odd) >> 1
    return (37 * half) & 63


def lines_23(za, zb, depth_row):
    lane = lanes8()
    near = (SIDE * lane + depth_row) & 127
    far = (SIDE * lane + SIDE - 1 - depth_row) & 127
    wide = lax.broadcasted_iota(I32, za.shape, 1)
    first = wide < 64
    return (
        jnp.where(first, take(za, near), take(zb, near)),
        jnp.where(first, take(za, far), take(zb, far)),
    )


def spread_lines(side2, side3, side1):
    lane = lanes8()
    owner = column_owner(lane)
    later = (owner + 64) & 127
    even = (lax.broadcasted_iota(I32, side2.shape, 1) & 1) == 0
    wa = jnp.where(even, take(side2, owner), take(side3, owner))
    wb = jnp.where(even, take(side2, later), take(side3, later))
    return wa, wb, pltpu.roll(side1, 74, 1)


def scatter_masks():
    row, lane, cell, i, j = grid_iotas()
    column = (j == 0) | (j == SIDE - 1)
    return (
        column & (i < 64),
        column & (i >= 64) & (i < SIDE),
        cell < SIDE,
        i == SIDE - 1,
    )


def scatter_rows(masks, wa, wb, side0, w1):
    zero = jnp.zeros((ROWS, LANES), F32)
    out = jnp.where(masks[0], wa, zero) + jnp.where(masks[1], wb, zero)
    return out + jnp.where(masks[2], side0, zero) + jnp.where(masks[3], w1, zero)


def scatter_lines(masks, lines):
    wa, wb, w1 = spread_lines(
        jnp.broadcast_to(lines[2:3], (8, LANES)),
        jnp.broadcast_to(lines[3:4], (8, LANES)),
        jnp.broadcast_to(lines[1:2], (8, LANES)),
    )
    return scatter_rows(masks, wa[0:1], wb[0:1], lines[0:1], w1[0:1])


def row_line(ref, base, first_cell):
    row, off = divmod(first_cell, LANES)
    top = ref[pl.ds(base + row, 1), :]
    if off == 0:
        return top
    lane = lax.broadcasted_iota(I32, (1, LANES), 1)
    top = pltpu.roll(top, LANES - off, 1)
    if off + SIDE <= LANES:
        return top
    low = pltpu.roll(ref[pl.ds(base + row + 1, 1), :], LANES - off, 1)
    return jnp.where(lane < LANES - off, top, low)


def write_frames(field_ref, base, out_ref, first_row, za_ref, zb_ref, depths):
    field = field_ref[base : base + ROWS, :]
    row, lane, cell, i, j = grid_iotas()
    za_ref[0:8, :] = jnp.zeros((8, LANES), F32)
    zb_ref[0:8, :] = jnp.zeros((8, LANES), F32)
    for depth in range(depths):
        column = ((j == depth) | (j == SIDE - 1 - depth)) & (i < SIDE)
        za_ref[depth : depth + 1, :] = jnp.sum(
            jnp.where(column & (i < 64), field, 0.0)[0:48], axis=0, keepdims=True
        )
        zb_ref[depth : depth + 1, :] = jnp.sum(
            jnp.where(column & (i >= 64), field, 0.0)[40:ROWS], axis=0, keepdims=True
        )
        at = first_row + depth * 4
        out_ref[at : at + 1, :] = row_line(field_ref, base, depth * SIDE)
        out_ref[at + 1 : at + 2, :] = row_line(field_ref, base, (SIDE - 1 - depth) * SIDE)
    depth_row = lax.broadcasted_iota(I32, (8, LANES), 0) & 3
    side2, side3 = lines_23(za_ref[0:8, :], zb_ref[0:8, :], depth_row)
    for depth in range(depths):
        at = first_row + depth * 4
        out_ref[at + 2 : at + 3, :] = side2[depth : depth + 1]
        out_ref[at + 3 : at + 4, :] = side3[depth : depth + 1]


def pack_line(rows, spare, depth):
    lane = lax.broadcasted_iota(I32, rows.shape, 1)
    return jnp.where(lane < SIDE, rows, pltpu.roll(spare, (SIDE - 38 * depth) % LANES, 1))


def unpack_line(first, second, third):
    lane = lax.broadcasted_iota(I32, first.shape, 1)
    out = jnp.where(lane < 38, pltpu.roll(first, 38, 1), pltpu.roll(second, 76, 1))
    return jnp.where(lane < 76, out, pltpu.roll(third, 114, 1))


def level_rows(ref, level):
    whole = (CELLS // LANES // 8) * 8
    rows = CELLS // LANES
    window = ref[level, :, CELLS - LANES : CELLS]
    return jnp.concatenate(
        [
            ref[level, :, 0 : whole * LANES].reshape(whole, LANES),
            ref[level, :, whole * LANES : rows * LANES].reshape(rows - whole, LANES),
            pltpu.roll(window, CELLS - rows * LANES, 1),
        ],
        axis=0,
    )


def surface_rows(ref):
    whole = (CELLS // LANES // 8) * 8
    rows = CELLS // LANES
    window = ref[:, CELLS - LANES : CELLS]
    return jnp.concatenate(
        [
            ref[:, 0 : whole * LANES].reshape(whole, LANES),
            ref[:, whole * LANES : rows * LANES].reshape(rows - whole, LANES),
            pltpu.roll(window, CELLS - rows * LANES, 1),
        ],
        axis=0,
    )


def interior_reach(depth):
    row, lane, cell, i, j = grid_iotas()
    zero = jnp.zeros_like(depth)
    along = jnp.where(j < SIDE - 1, jnp.minimum(depth, ahead(depth, 1)), zero)
    across = jnp.where(cell < CELLS - SIDE, jnp.minimum(depth, ahead(depth, SIDE)), zero)
    return along, across


def interior_spread(x, along, across, level):
    zero = jnp.zeros_like(x)
    flux1 = jnp.where(along > level, ahead(x, 1) - x, zero)
    flux2 = jnp.where(across > level, ahead(x, SIDE) - x, zero)
    return (flux1 - behind(flux1, 1)) + (flux2 - behind(flux2, SIDE))


def depths_kernel(depth_ref, out_ref, dense_ref, z_ref):
    row, lane, cell, i, j = grid_iotas()
    dense_ref[...] = jnp.where(cell < CELLS, surface_rows(depth_ref).astype(F32), 0.0)
    write_frames(dense_ref, 0, out_ref, 0, z_ref.at[0], z_ref.at[1], 1)
    out_ref[4:8, :] = jnp.zeros((4, LANES), F32)


def columns_kernel(exchanges, levels, me_ref, own_ref, *rest):
    met_refs = rest[: len(exchanges)]
    k_hbm, s_hbm, t_hbm, depth_hbm, d_hbm, b_hbm, adj_hbm, flag_hbm = rest[len(exchanges) : len(exchanges) + 8]
    a_ref, q_ref, as_ref, blk_ref, dense_ref, reach_ref = rest[len(exchanges) + 8 : len(exchanges) + 14]
    k_ref, s_ref, t_ref, depth_ref, d_ref, b_ref, g_ref, z_ref, ts_ref, frame_ref, adj_ref, flag_ref, sems = rest[len(exchanges) + 14 :]
    parts = 3
    third = levels // parts
    surface = [
        pltpu.make_async_copy(source, target, sems.at[number])
        for number, (source, target) in enumerate(((depth_hbm, depth_ref), (b_hbm, b_ref), (d_hbm, d_ref)))
    ]
    for copy in surface:
        copy.start()
    columns = []
    for part in range(parts):
        at = pl.ds(part * third, third if part < parts - 1 else levels - part * third)
        for number, (source, target) in enumerate(((k_hbm, k_ref), (s_hbm, s_ref))):
            columns.append(pltpu.make_async_copy(source.at[at], target.at[at], sems.at[3 + 2 * part + number]))
            columns[-1].start()
    tracer = pltpu.make_async_copy(t_hbm, t_ref, sems.at[3 + 2 * parts])
    tracer.start()
    tables = [
        pltpu.make_async_copy(source, target, sems.at[4 + 2 * parts + number])
        for number, (source, target) in enumerate(((adj_hbm, adj_ref), (flag_hbm, flag_ref)))
    ]
    for copy in tables:
        copy.start()
    me = me_ref[0]
    row, lane, cell, i, j = grid_iotas()
    inside = cell < CELLS
    for number, ref in enumerate((depth_ref, b_ref, d_ref)):
        surface[number].wait()
        place = (2, 0, 1)[number]
        rows = slice(place * ROWS, (place + 1) * ROWS)
        dense_ref[rows, :] = jnp.where(inside, surface_rows(ref).astype(F32), 0.0)
    depth = dense_ref[2 * ROWS : 3 * ROWS, :]
    along, across = interior_reach(depth)
    zero = jnp.zeros((ROWS, LANES), F32)

    def down(level, carry):
        link, below, va, vq = carry
        at = pl.ds(pl.multiple_of(level * ROWS, ROWS), ROWS)
        here = level.astype(F32)
        r = jnp.where(depth > here + 1.0, level_rows(k_ref, level), zero)
        wet = jnp.where(depth > here, 1.0, zero)
        upper = 1.0 + below
        centre = upper + r
        inverse = pl.reciprocal(centre, approx=True)
        inverse = inverse * (2.0 - centre * inverse)
        ratio = r * inverse
        va = (level_rows(s_ref, level) + link * va) * inverse
        vq = (wet + link * vq) * inverse
        g_ref[at, :] = ratio
        a_ref[at, :] = va
        q_ref[at, :] = vq
        return r, upper * ratio, va, vq

    carry = (zero, zero, zero, zero)
    for part in range(parts):
        columns[2 * part].wait()
        columns[2 * part + 1].wait()
        last = (part + 1) * third if part < parts - 1 else levels
        carry = lax.fori_loop(part * third, last, down, carry, unroll=10)
    tracer.wait()
    for copy in tables:
        copy.wait()
    column = ((j == 0) | (j == SIDE - 1)) & (i < SIDE)
    first = (column & (i < 64))[0:48]
    second = (column & (i >= 64))[40:ROWS]

    def up(step, carry):
        xa, xq, total, flux1, flux2 = carry
        level = levels - 1 - step
        here = level.astype(F32)
        at = pl.ds(pl.multiple_of(level * ROWS, ROWS), ROWS)
        ratio = g_ref[at, :]
        xa = a_ref[at, :] + ratio * xa
        xq = q_ref[at, :] + ratio * xq
        a_ref[at, :] = xa
        q_ref[at, :] = xq
        t = level_rows(t_ref, level)
        line = pl.ds(level, 1)
        for number, (x, out) in enumerate(((t, ts_ref), (xa, as_ref))):
            base = number * 4
            z_ref[base, line, :] = jnp.sum(jnp.where(first, x[0:48], 0.0), axis=0, keepdims=True)
            z_ref[base + 1, line, :] = jnp.sum(jnp.where(second, x[40:ROWS], 0.0), axis=0, keepdims=True)
            out[0, line, :] = x[0:1]
            z_ref[base + 2, line, :] = x[ROWS - 2 : ROWS - 1]
            z_ref[base + 3, line, :] = x[ROWS - 1 : ROWS]
        flux1 = flux1 + jnp.where(along > here, xq * (ahead(t, 1) - t), zero)
        flux2 = flux2 + jnp.where(across > here, xq * (ahead(t, SIDE) - t), zero)
        return xa, xq, total + xq * t, flux1, flux2

    xa, xq, total, flux1, flux2 = lax.fori_loop(0, levels, up, (zero,) * 5, unroll=6)
    level_scale = 1.0 / math.sqrt(levels)
    spread = (flux1 - behind(flux1, 1)) + (flux2 - behind(flux2, SIDE))
    dense_ref[3 * ROWS : 4 * ROWS, :] = jnp.where(inside, (total + SPREAD * spread) * level_scale, zero)
    spare = z_ref.shape[1] - levels
    for number, out in enumerate((ts_ref, as_ref)):
        base = number * 4
        for part in range(4):
            z_ref[base + part, levels:, :] = jnp.zeros((spare, LANES), F32)
        out[0, levels:, :] = jnp.zeros((spare, LANES), F32)
        side2, side3 = lines_23(z_ref[base], z_ref[base + 1], 0)
        out[2] = side2
        out[3] = side3
        low, high = z_ref[base + 2], z_ref[base + 3]
        wide = lax.broadcasted_iota(I32, low.shape, 1)
        out[1] = jnp.where(wide < 54, pltpu.roll(low, 54, 1), pltpu.roll(high, 54, 1))
    level = lax.broadcasted_iota(I32, (32, LANES), 0).astype(F32)
    reach_ref[4:8, :] = jnp.zeros((4, LANES), F32)
    for side in range(4):
        neighbour = adj_ref[0, side]
        flag = flag_ref[0, side]
        met = pick(exchanges, me, neighbour, lambda n: met_refs[n][pl.ds(flag >> 1, 1), :])
        met = take(jnp.broadcast_to(met, (8, LANES)), seam_index(flag))[0:1]
        reach = jnp.where(neighbour >= 0, jnp.minimum(met, own_ref[side : side + 1, :]), 0.0)
        reach_ref[side : side + 1, :] = reach
        shared = jnp.sum(jnp.where(reach > level, ts_ref[side], 0.0), axis=0, keepdims=True)
        frame_ref[12 + side : 13 + side, :] = (SPREAD * level_scale) * shared
        table = jnp.zeros((1, LANES), F32)
        where = lax.broadcasted_iota(I32, (1, LANES), 1)
        for number, of in enumerate((side, 2 if side < 2 else 0, 3 if side < 2 else 1)):
            table = jnp.where(where == 104 + 2 * number, adj_ref[0, of].astype(F32), table)
            table = jnp.where(where == 105 + 2 * number, flag_ref[0, of].astype(F32), table)
        frame_ref[16 + side : 17 + side, :] = table
    g_ref[0:ROWS, :] = jnp.minimum(depth, 1.0)
    za_ref, zb_ref = z_ref.at[0], z_ref.at[1]
    sums = frame_ref[12:16, :]
    seams = frame_ref[16:20, :]
    for number, (source, base) in enumerate(((dense_ref, 0), (dense_ref, 3 * ROWS), (g_ref, 0), (dense_ref, ROWS))):
        depths = 4 if number < 3 else 3
        write_frames(source, base, frame_ref, 0, za_ref, zb_ref, depths)
        spare = frame_ref[12:16, :] if number < 3 else sums
        for depth in range(3):
            rows = pack_line(frame_ref[4 * depth : 4 * depth + 4, :], spare, depth)
            if number == 3 and depth == 2:
                rows = jnp.where(lax.broadcasted_iota(I32, (4, LANES), 1) >= 104, seams, rows)
            at = 12 * number + 4 * depth
            blk_ref[at : at + 4, :] = rows


def partner(exchange, me):
    stride, odd = exchange
    if not odd:
        return me ^ stride
    return jnp.where(((me // stride) & 1) == 1, me + stride, me - stride)


def pick(exchanges, me, neighbour, lines_of):
    value = lines_of(0)
    for number in range(1, len(exchanges)):
        value = jnp.where(neighbour == partner(exchanges[number], me), lines_of(number), value)
    return value


def seam_index(flag):
    lane = lanes8()
    return jnp.where((flag & 1) == 1, SIDE - 1 - lane, lane) & 127


def block_rows(refs, places, first, size):
    for ref, held in zip(refs, places):
        for number, position in enumerate(held):
            at = number * BLOCK + first
            yield position, ref[at : at + size, :]


def gather_lines(p, lines):
    high = lines.astype(jnp.bfloat16)
    rest = lines - high.astype(F32)
    middle = rest.astype(jnp.bfloat16)
    low = (rest - middle.astype(F32)).astype(jnp.bfloat16)
    out = jnp.dot(p, high, preferred_element_type=F32)
    out = out + jnp.dot(p, middle, preferred_element_type=F32)
    return out + jnp.dot(p, low, preferred_element_type=F32)


def ends(x, low, high, low_parity, high_parity, depth):
    lane = lax.broadcasted_iota(I32, x.shape, 1)
    low_end = take(low, jnp.where(low_parity == 1, SIDE - 1 - depth, depth))
    high_end = take(high, jnp.where(high_parity == 1, SIDE - 1 - depth, depth))
    return (
        jnp.where(lane == 0, low_end, pltpu.roll(x, 1, 1)),
        jnp.where(lane == SIDE - 1, high_end, pltpu.roll(x, LANES - 1, 1)),
    )


def krylov_kernel(places, lines, me_ref, dense_ref, *rest):
    refs = rest[: len(places)]
    va_ref, vb_ref, line_ref, gram_ref = rest[len(places) : len(places) + 4]
    p_ref, index_ref, frame_ref, wet_ref, d_ref, x_ref = rest[len(places) + 4 :]
    me = me_ref[0]

    def collect(out, first):
        for position, rows in block_rows(refs, places, first, 4):
            out[position * 4 : position * 4 + 4, :] = rows

    for depth in range(3):
        collect(x_ref.at[depth], 4 * depth)
        collect(x_ref.at[4 + depth], 12 + 4 * depth)
        collect(wet_ref.at[depth], 24 + 4 * depth)
        collect(d_ref.at[depth], 36 + 4 * depth)
    x_ref[3] = unpack_line(x_ref[0], x_ref[1], x_ref[2])
    x_ref[7] = unpack_line(x_ref[4], x_ref[5], x_ref[6])
    wet_ref[3] = unpack_line(wet_ref[0], wet_ref[1], wet_ref[2])
    shared = unpack_line(d_ref[0], d_ref[1], d_ref[2])
    lane = lax.broadcasted_iota(I32, (lines, LANES), 1)
    line = lax.broadcasted_iota(I32, (lines, LANES), 0)
    odd = line & 1
    column = lax.broadcasted_iota(I32, (lines, lines), 1)
    line_of = lax.broadcasted_iota(I32, (lines, lines), 0)
    for number in range(3):
        tile = d_ref[2, :, 104 + 2 * number : 105 + 2 * number].astype(I32)
        flag = d_ref[2, :, 105 + 2 * number : 106 + 2 * number].astype(I32)
        at = jnp.where(tile >= 0, 4 * (tile ^ me) + (flag >> 1), -1)
        p = jnp.where(jnp.broadcast_to(at, (lines, lines)) == column, 1.0, 0.0)
        p_ref[number * lines : (number + 1) * lines, :] = p.astype(jnp.bfloat16)
        parity = jnp.broadcast_to(flag & 1, (lines, LANES))
        if number == 0:
            index_ref[0:lines, :] = jnp.where(parity == 1, SIDE - 1 - lane, lane) & 127
        else:
            index_ref[number * lines : (number + 1) * lines, :] = parity ^ odd
    first_half = (line_of & 2) == 0
    for number in range(2):
        at = (line_of & -4) + jnp.where(first_half, 2, 0) + number
        p = jnp.where(at == column, 1.0, 0.0)
        p_ref[(3 + number) * lines : (4 + number) * lines, :] = p.astype(jnp.bfloat16)
    p = p_ref[0 : 3 * lines, :]
    facing_at = index_ref[0:lines, :]
    low_parity = index_ref[lines : 2 * lines, :]
    high_parity = index_ref[2 * lines : 3 * lines, :]
    wet = [wet_ref[depth] for depth in range(4)]
    met = gather_lines(p, wet[0])
    facing = take(met[0:lines], facing_at)
    for depth in range(3):
        low, high = ends(
            wet[depth], met[lines : 2 * lines], met[2 * lines : 3 * lines], low_parity, high_parity, depth
        )
        masks = [
            wet[depth] * (facing if depth == 0 else wet[depth - 1]),
            wet[depth] * wet[depth + 1],
            wet[depth] * low,
            wet[depth] * high,
        ]
        frame_ref[depth, 0] = d_ref[depth] + ((masks[0] + masks[1]) + (masks[2] + masks[3]))
        for number in range(4):
            frame_ref[depth, 1 + number] = masks[number]
        if depth == 0:
            seam = masks[0][0:8]
    gain = take(gather_lines(p_ref[0:lines, :], shared), facing_at) - shared
    moved = gather_lines(p_ref[3 * lines : 5 * lines, :], gain)
    zero_line = jnp.zeros((lines, LANES), F32)
    for depth in range(4):
        end = jnp.where(odd == 1, SIDE - 1 - depth, depth)
        extra = jnp.where(lane == 0, take(moved[0:lines], end), zero_line)
        extra = extra + jnp.where(lane == SIDE - 1, take(moved[lines : 2 * lines], end), zero_line)
        if depth == 0:
            extra = extra + gain
        x_ref[4 + depth] = x_ref[4 + depth] + extra
    surface = jnp.minimum(dense_ref[2 * ROWS : 3 * ROWS, :], 1.0)
    along, across = interior_reach(surface)
    degree = (along + behind(along, 1)) + (across + behind(across, SIDE))
    masks = scatter_masks()
    diagonal = dense_ref[ROWS : 2 * ROWS, :] + (degree + scatter_lines(masks, seam))
    scale = 2.0 / CENTRE
    row, lane, cell, i, j = grid_iotas()
    inside = cell < CELLS
    forcing = dense_ref[3 * ROWS : 4 * ROWS, :] + scatter_lines(masks, gain[0:8])
    va_ref[0] = forcing
    vb_ref[0] = dense_ref[0:ROWS, :]
    frames = [[[x_ref[4 * solve + depth] for depth in range(4)]] for solve in range(2)]
    own = [[dense_ref[0:ROWS, :]], [forcing]]
    for step in range(ITERS):
        for solve in range(2):
            x = frames[solve][-1]
            met = gather_lines(p, x[0])
            facing = take(met[0:lines], facing_at)
            if solve == 0:
                line_ref[step] = facing[0:8]
            mine = own[solve][-1]
            flow = (along * ahead(mine, 1) + behind(along * mine, 1)) + (
                across * ahead(mine, SIDE) + behind(across * mine, SIDE)
            )
            image = diagonal * mine - flow - scatter_lines(masks, seam * facing[0:8])
            image = jnp.where(inside, scale * image - 2.0 * mine, 0.0)
            own[solve].append(0.5 * image if step == 0 else image - own[solve][-2])
            following = []
            for depth in range(ITERS - 1 - step):
                low, high = ends(
                    x[depth],
                    met[lines : 2 * lines],
                    met[2 * lines : 3 * lines],
                    low_parity,
                    high_parity,
                    depth,
                )
                before = facing if depth == 0 else x[depth - 1]
                flow = (frame_ref[depth, 1] * before + frame_ref[depth, 2] * x[depth + 1]) + (
                    frame_ref[depth, 3] * low + frame_ref[depth, 4] * high
                )
                image = scale * (frame_ref[depth, 0] * x[depth] - flow) - 2.0 * x[depth]
                following.append(0.5 * image if step == 0 else image - frames[solve][-2][depth])
            frames[solve].append(following)
            if step < ITERS - 1:
                (vb_ref if solve == 0 else va_ref)[step + 1] = own[solve][-1]
    gram_ref[30:32, :] = jnp.zeros((2, LANES), F32)
    for solve in range(2):
        at = solve
        for first in range(ITERS + 1):
            for second in range(first + 1):
                gram_ref[at : at + 1, :] = jnp.sum(own[solve][first] * own[solve][second], axis=0, keepdims=True)
                at += 2


def image_of(p):
    out = [None] * (len(p) + 1)

    def add(at, value):
        out[at] = value if out[at] is None else out[at] + value

    for at, value in enumerate(p):
        add(at, CENTRE * value)
        if at == 0:
            add(1, CENTRE * value)
        else:
            add(at + 1, 0.5 * CENTRE * value)
            add(at - 1, 0.5 * CENTRE * value)
    return out


def form(left, gram, right):
    total = None
    for first, x in enumerate(left):
        inner = None
        for second, y in enumerate(right):
            term = gram[max(first, second)][min(first, second)] * y
            inner = term if inner is None else inner + term
        total = x * inner if total is None else total + x * inner
    return total


def total_gram(refs, sum_ref):
    total = refs[0][...]
    for ref in refs[1:]:
        total = total + ref[...]
    sum_ref[...] = jnp.broadcast_to(jnp.sum(total, axis=1, keepdims=True), sum_ref.shape)


def coefficients(sum_ref):
    gram = []
    at = 0
    for first in range(ITERS + 1):
        gram.append([sum_ref[at + 2 * second : at + 2 * second + 2, :] for second in range(first + 1)])
        at += 2 * (first + 1)
    one = jnp.ones((2, LANES), F32)
    x = []
    r = [one]
    p = [one]
    rr = gram[0][0]
    for step in range(ITERS):
        image = image_of(p)
        curve = form(p, gram, image)
        alpha = jnp.where(curve > 0.0, rr / curve, 0.0)
        x = [x[n] + alpha * p[n] if n < len(x) else alpha * p[n] for n in range(len(p))]
        r = [r[n] - alpha * image[n] if n < len(r) else -alpha * image[n] for n in range(len(image))]
        if step < ITERS - 1:
            new = jnp.maximum(form(r, gram, r), 0.0)
            beta = jnp.where(rr > 0.0, new / rr, 0.0)
            p = [r[n] + beta * p[n] if n < len(p) else r[n] for n in range(len(r))]
            rr = new
    return x


def store_rows(ref, rows):
    last = CELLS // LANES
    ref[:, 0 : last * LANES] = rows[0:last].reshape(1, last * LANES)
    ref[:, last * LANES : CELLS] = rows[last : last + 1, 0 : CELLS - last * LANES]


def combine(x, v_ref):
    out = x[0] * v_ref[0]
    for number in range(1, ITERS):
        out = out + x[number] * v_ref[number]
    return out


def gradient_kernel(exchanges, levels, grams, me_ref, *rest):
    gram_refs = rest[:grams]
    rest = rest[grams:]
    dense_ref, va_ref, v_ref, line_ref, reach_ref, a_ref, q_ref, as_ref = rest[:8]
    refs = rest[8 : 8 + len(exchanges)]
    adj_hbm, flag_hbm, height_ref, out_hbm = rest[8 + len(exchanges) : 12 + len(exchanges)]
    gram_ref, sum_ref, w_ref, h_ref, adj_ref, flag_ref, out_ref, sems = rest[12 + len(exchanges) :]
    tables = [
        pltpu.make_async_copy(source, target, sems.at[number])
        for number, (source, target) in enumerate(((adj_hbm, adj_ref), (flag_hbm, flag_ref)))
    ]
    for copy in tables:
        copy.start()
    me = me_ref[0]
    total_gram(gram_refs, gram_ref)
    both = coefficients(gram_ref)
    store_rows(height_ref, combine([x[1:2] for x in both], va_ref))
    x = [x[0:1] for x in both]
    level_scale = 1.0 / math.sqrt(levels)
    adjoint = combine(x, v_ref) * level_scale
    met_line = x[0] * line_ref[0]
    depth = dense_ref[2 * ROWS : 3 * ROWS, :]
    along, across = interior_reach(depth)
    sum_ref[0:8, :] = met_line + x[1] * line_ref[1] + x[2] * line_ref[2] + x[3] * line_ref[3]
    h_ref[0:ROWS, :] = adjoint
    w_ref[4, 8:9, :] = h_ref[0:1, :]
    w_ref[4, 9:10, :] = row_line(h_ref, 0, (SIDE - 1) * SIDE)
    row, lane, cell, i, j = grid_iotas()
    column = (j == 0) | (j == SIDE - 1)
    zero = jnp.zeros((ROWS, LANES), F32)
    za = jnp.sum(jnp.where(column & (i < 64), adjoint, zero), axis=0, keepdims=True)
    zb = jnp.sum(jnp.where(column & (i >= 64), adjoint, zero), axis=0, keepdims=True)
    side2, side3 = lines_23(jnp.broadcast_to(za, (8, LANES)), jnp.broadcast_to(zb, (8, LANES)), 0)
    w_ref[4, 10:11, :] = side2[0:1]
    w_ref[4, 11:12, :] = side3[0:1]
    level = lax.broadcasted_iota(I32, (32, LANES), 0).astype(F32)
    fluxes = []
    for copy in tables:
        copy.wait()
    for side in range(4):
        neighbour = adj_ref[0, side]
        flag = flag_ref[0, side]
        index = seam_index(flag)
        other = take(pick(exchanges, me, neighbour, lambda n: refs[n][flag >> 1]), index)
        other = other + sum_ref[side : side + 1, :] * level_scale
        own = as_ref[side] + w_ref[4, 8 + side : 9 + side, :]
        fluxes.append(jnp.where(reach_ref[side : side + 1, :] > level, other - own, 0.0))
    wa, wb, w1 = spread_lines(fluxes[2], fluxes[3], fluxes[1])
    w_ref[0] = wa
    w_ref[1] = wb
    w_ref[2] = fluxes[0]
    w_ref[3] = w1
    masks = scatter_masks()

    along_back, across_back = behind(along, 1), behind(across, SIDE)
    h_ref[0:ROWS, :] = along
    h_ref[ROWS : 2 * ROWS, :] = across
    h_ref[2 * ROWS : 3 * ROWS, :] = along_back
    h_ref[3 * ROWS : 4 * ROWS, :] = across_back
    for number, step in enumerate((ahead(adjoint, 1), ahead(adjoint, SIDE), behind(adjoint, 1), behind(adjoint, SIDE))):
        h_ref[(4 + number) * ROWS : (5 + number) * ROWS, :] = step - adjoint

    def per_level(number, carry):
        at = pl.ds(pl.multiple_of(number * ROWS, ROWS), ROWS)
        here = pl.ds(number, 1)
        floor = number.astype(F32)
        spread = scatter_rows(
            masks, w_ref[0, here, :], w_ref[1, here, :], w_ref[2, here, :], w_ref[3, here, :]
        )
        for way in range(4):
            reach = h_ref[way * ROWS : (way + 1) * ROWS, :]
            gain = h_ref[(4 + way) * ROWS : (5 + way) * ROWS, :]
            spread = spread + jnp.where(reach > floor, gain, 0.0)
        store_rows(out_ref.at[number], a_ref[at, :] + adjoint * q_ref[at, :] + SPREAD * spread)
        return carry

    parts = 3
    third = levels // parts
    copies = []
    for part in range(parts):
        first = part * third
        last = first + third if part < parts - 1 else levels
        lax.fori_loop(first, last, per_level, 0, unroll=5)
        at = pl.ds(first, last - first)
        copies.append(pltpu.make_async_copy(out_ref.at[at], out_hbm.at[at], sems.at[2 + part]))
        copies[-1].start()
    for copy in copies:
        copy.wait()


def interior_kernel(levels, dense_ref, a_ref, out_ref):
    along, across = interior_reach(dense_ref[2 * ROWS : 3 * ROWS, :])

    def per_level(number, carry):
        at = pl.ds(pl.multiple_of(number * ROWS, ROWS), ROWS)
        a = a_ref[at, :]
        out_ref[at, :] = a + SPREAD * interior_spread(a, along, across, number.astype(F32))
        return carry

    lax.fori_loop(0, levels, per_level, 0, unroll=5)


def rounds(tiles):
    out = []
    stride = tiles
    while stride > 1:
        radix = 4 if stride >= 16 else 2
        stride //= radix
        out.append((stride, radix))
    return out


def swap(x, tiles, offset):
    return lax.ppermute(x, "tile", [(t, t ^ offset) for t in range(tiles)])


def gather_tiles(block, tiles, beside):
    held = [block]
    places = [(0,)]
    for stride, radix in rounds(tiles):
        whole = held[0] if len(held) == 1 else jnp.concatenate(held, axis=0)
        if stride == 1:
            whole, beside = lax.optimization_barrier((whole, beside))
        covered = tuple(n for place in places for n in place)
        for number in range(1, radix):
            held.append(swap(whole, tiles, number * stride))
            places.append(tuple(n ^ (number * stride) for n in covered))
    return held, tuple(places), beside


def sum_tiles(block, tiles):
    held = [block]
    for stride, radix in rounds(tiles):
        whole = functools.reduce(jnp.add, held)
        held = [whole] + [swap(whole, tiles, number * stride) for number in range(1, radix)]
    return held


def shards(thermal, stirring, depth, adjacent, flags, main_entry, sensitivity, elevation, tiles):
    levels = thermal.shape[1]
    me = lax.axis_index("tile").astype(I32).reshape(1)
    smem = pl.BlockSpec(memory_space=pltpu.SMEM)
    vmem = pl.BlockSpec(memory_space=pltpu.VMEM)

    def shape(*dims):
        return jax.ShapeDtypeStruct(dims, F32)

    hbm = pl.BlockSpec(memory_space=pltpu.HBM)

    def call(kernel, outs, scratch, scalars, arrays, name, flops=1e6, traffic=1e6, far=(), grant=48, places=None):
        return pl.pallas_call(
            kernel,
            out_shape=outs,
            in_specs=[smem] * len(scalars) + [vmem] * len(arrays) + [hbm] * len(far),
            out_specs=places or jax.tree.map(lambda _: vmem, outs),
            scratch_shapes=scratch,
            compiler_params=pltpu.CompilerParams(vmem_limit_bytes=grant * 1024 * 1024),
            cost_estimate=pl.CostEstimate(flops=int(flops), bytes_accessed=int(traffic), transcendentals=0),
            name=name,
        )(*scalars, *arrays, *far)

    exchanges = []
    for stride in (1, ROW_TILES, tiles // 2):
        if (stride, False) not in exchanges and stride < tiles:
            exchanges.append((stride, False))
            if stride < ROW_TILES * 2 and stride * 2 < tiles:
                exchanges.append((stride, True))
    exchanges = tuple(exchanges)

    def to_neighbours(x):
        out = []
        for stride, odd in exchanges:
            if odd:
                pairs = [(t, t + stride if (t // stride) % 2 else t - stride) for t in range(tiles)]
                pairs = [(t, u) for t, u in pairs if 0 <= u < tiles]
            else:
                pairs = [(t, t ^ stride) for t in range(tiles)]
            out.append(lax.ppermute(x, "tile", pairs))
        return out

    def by_level(x):
        return jnp.transpose(x, (1, 0, 2))

    own_depths = call(
        depths_kernel,
        shape(8, LANES),
        [pltpu.VMEM((ROWS, LANES), F32), pltpu.VMEM((2, 8, LANES), F32)],
        (),
        (depth,),
        "depths",
    )
    depths_met = to_neighbours(own_depths)
    far = pltpu.VMEM((levels, 1, CELLS), F32)
    solved, weight, strips, block, dense, reach = call(
        functools.partial(columns_kernel, exchanges, levels),
        (
            shape(levels * ROWS, LANES),
            shape(levels * ROWS, LANES),
            shape(4, 32, LANES),
            shape(BLOCK, LANES),
            shape(4 * ROWS, LANES),
            shape(8, LANES),
        ),
        [
            far,
            far,
            far,
            pltpu.VMEM((1, CELLS), I32),
            pltpu.VMEM((1, CELLS), F32),
            pltpu.VMEM((1, CELLS), F32),
            pltpu.VMEM((levels * ROWS, LANES), F32),
            pltpu.VMEM((8, 32, LANES), F32),
            pltpu.VMEM((4, 32, LANES), F32),
            pltpu.VMEM((24, LANES), F32),
            pltpu.SMEM((1, 4), I32),
            pltpu.SMEM((1, 4), I32),
            pltpu.SemaphoreType.DMA((12,)),
        ],
        (me,),
        (own_depths, *depths_met),
        "columns",
        2e7,
        8e6,
        tuple(
            pltpu.with_memory_space_constraint(x, pltpu.HBM)
            for x in (
                by_level(stirring),
                by_level(sensitivity),
                by_level(thermal),
                depth,
                main_entry,
                elevation,
                adjacent,
                flags,
            )
        ),
        48,
    )
    inside = call(
        functools.partial(interior_kernel, levels),
        shape(levels * ROWS, LANES),
        [],
        (),
        (dense, solved),
        "interior",
        1e7,
        4e6,
    )
    blocks, places, inside = gather_tiles(block, tiles, inside)
    strips_met = to_neighbours(strips)
    lines = 4 * tiles
    frame = pltpu.VMEM((4, lines, LANES), F32)
    basis = shape(ITERS, ROWS, LANES)
    basis_a, basis_b, lines_b, gram = call(
        functools.partial(krylov_kernel, places, lines),
        (basis, basis, shape(ITERS, 8, LANES), shape(32, LANES)),
        [
            pltpu.VMEM((5 * lines, lines), jnp.bfloat16),
            pltpu.VMEM((3 * lines, LANES), I32),
            pltpu.VMEM((3, 5, lines, LANES), F32),
            frame,
            frame,
            pltpu.VMEM((8, lines, LANES), F32),
        ],
        (me,),
        (dense, *blocks),
        "krylov",
    )
    grams = sum_tiles(gram, tiles)
    height, gradient = call(
        functools.partial(gradient_kernel, exchanges, levels, len(grams)),
        (jax.ShapeDtypeStruct(elevation.shape, F32), shape(levels, 1, CELLS)),
        [
            pltpu.VMEM((32, LANES), F32),
            pltpu.VMEM((16, LANES), F32),
            pltpu.VMEM((5, 32, LANES), F32),
            pltpu.VMEM((8 * ROWS, LANES), F32),
            pltpu.SMEM((1, 4), I32),
            pltpu.SMEM((1, 4), I32),
            pltpu.VMEM((levels, 1, CELLS), F32),
            pltpu.SemaphoreType.DMA((5,)),
        ],
        (me,),
        (
            *grams,
            dense,
            basis_a,
            basis_b,
            lines_b,
            reach,
            inside,
            weight,
            strips,
            *strips_met,
        ),
        "gradient",
        1e7,
        4e6,
        tuple(pltpu.with_memory_space_constraint(x, pltpu.HBM) for x in (adjacent, flags)),
        places=(vmem, hbm),
    )
    gradient = by_level(gradient)
    return height, gradient


def solution(mesh):
    placed = (
        P(("ens", "tile"), None, None),
        P("tile", None, None),
        P("tile", None),
        P("tile", None),
        P("tile", None),
        P("tile", None),
        P(("ens", "tile"), None, None),
        P(("ens", "tile"), None),
    )
    return jax.shard_map(
        functools.partial(shards, tiles=mesh.shape["tile"]),
        mesh=mesh,
        in_specs=placed,
        out_specs=(P(("ens", "tile"), None), P(("ens", "tile"), None, None)),
        check_vma=False,
    )
```
